32 devices in a mesh: groups: 2 (over x), ep: 16 (over z, y, core).
Axes of the slice: x: 2, y: 2, z: 4, core: 2. Of those that a mesh axis runs over, the one named last changes fastest.
Arguments:
- residual: bfloat16 [2048, 7168], P('groups', 'ep'), parts along dimension 0, may hold values from -6 to 6
- attn_out: bfloat16 [2048, 7168], P('groups', 'ep'), parts along dimension 0, may hold values from -6 to 6
- norm_gain: float32 [7168], replicated, may hold values from 0.5 to 1.5
- expert_routes: int32 [2048, 2], P(('groups', 'ep')), parts along dimension 0, may hold values from 0 to 2, as said below
- route_gain: float32 [2048, 2], P(('groups', 'ep')), parts along dimension 0, may hold values from 0.1 to 1
- w_gate: bfloat16 [7168, 4096], P(None, 'ep'), may hold values from -0.0625 to 0.0625
- w_up: bfloat16 [7168, 4096], P(None, 'ep'), may hold values from -0.0625 to 0.0625
- w_down: bfloat16 [4096, 7168], P('ep'), may hold values from -0.125 to 0.125
Outputs:
- mixed: bfloat16 [2048, 7168], P(('groups', 'ep')), parts along dimension 0
The draws below stay inside these ranges and needn't reach their ends.
There are 2 independent parts, one for each index of `groups`. The reference program is written for one: setup_inputs(seed, part) draws one part's arguments, and reference() takes and returns one part's arrays. A program takes and returns all parts, laid end to end along the dimension named above; an argument that names none is the same for every part. Nothing has to cross between parts.
Inputs may be any that keep to these rules, and one draw needn't show every extreme that they name: `expert_routes`: value 2 marks a route to an expert outside this wave; a token names each expert of the wave at most once. Among the tokens of one block of 64, at most 64 routes name one expert, and in every draw some expert is named exactly 64 times by every block.
All inputs are finite; a program needn't handle non-finite values.
Results may differ from the reference program's by a relative error of at most 0.0055.
Values may be sent and summed in bfloat16 or wider, within the bound.
No kernel may reach another device: no remote copies, remote signals or barrier semaphores. Data moves between devices by JAX's collectives and lax.ppermute only.
A program may use at most 192 MiB of HBM per device.

```python
import math
import jax
import jax.numpy as jnp
from jax import lax

D = 7168
FF = 2048
FSPLIT = 8
TOK_DEV = 64
EW = 2
WSLOT = 2
CAP = 64
FF_DEV = 256
TOKENS = 1024


def draw_expert_routes(key, part):
    base = jax.random.fold_in(key, 7)
    key_perm, key_hot, key_coin = jax.random.split(base, 3)
    blocks = TOKENS // TOK_DEV
    perm_keys = jax.random.split(key_perm, blocks)
    orders = jax.vmap(lambda single: jax.random.permutation(single, EW))(perm_keys)
    position = (jnp.arange(TOK_DEV)[:, None] + jnp.arange(WSLOT)[None, :]) % EW
    named = orders[:, position]
    hottest = jax.random.randint(key_hot, (), 0, EW)
    coin_flip = jax.random.randint(key_coin, (blocks, TOK_DEV, WSLOT), 0, 2)
    live_mask = (coin_flip == 1) | (named == hottest)
    return jnp.where(live_mask, named, EW).reshape(TOKENS, WSLOT).astype(jnp.int32)


def level_of(key, shape, shards, smallest, largest):
    level = 1.0
    for dim, blocks in shards:
        steps = jax.random.uniform(jax.random.fold_in(jax.random.fold_in(key, 6), dim), (blocks,), jnp.float32, smallest / len(shards), largest / len(shards))
        level = level * jnp.repeat(jnp.exp(steps), shape[dim] // blocks).reshape((-1,) + (1,) * (len(shape) - 1 - dim))
    return level


def bell_draw(key, dims, scale, most, shards=(), kind=jnp.bfloat16):
    result = scale * jax.random.normal(key, dims, jnp.float32)
    if shards:
        result = result * level_of(key, dims, shards, -0.22, 0.18)
    return jnp.clip(result, -most, most).astype(kind)


def setup_inputs(seed: int = 0, part: int = 0) -> dict:
    splits = jax.random.split(jax.random.key(seed), 9)
    own_keys = jax.random.split(jax.random.fold_in(splits[8], part), 9)
    return {
        "residual": bell_draw(own_keys[0], (TOKENS, D), 1.0, 6.0, ((1, 16),)),
        "attn_out": bell_draw(own_keys[1], (TOKENS, D), 1.0, 6.0, ((1, 16),)),
        "norm_gain": jnp.clip(1.0 + 0.1 * jax.random.normal(splits[2], (D,), jnp.float32), 0.5, 1.5),
        "expert_routes": draw_expert_routes(jax.random.fold_in(jax.random.fold_in(splits[8], part), 71), part),
        "route_gain": jnp.clip(jnp.exp(math.log(1.0) - 2.3025851 * jax.random.uniform(own_keys[4], (TOKENS, WSLOT), jnp.float32) ** level_of(own_keys[4], (TOKENS, WSLOT), ((0, 16),), -0.2, 0.2)), 0.1, 1.0),
        "w_gate": bell_draw(splits[5], (D, EW * FF), D ** -0.5, 0.0625, ((1, 16),)),
        "w_up": bell_draw(splits[6], (D, EW * FF), D ** -0.5, 0.0625, ((1, 16),)),
        "w_down": bell_draw(splits[7], (EW * FF, D), FF ** -0.5, 0.125, ((0, 16),)),
    }


epsilon = 1e-06

def reference(residual, attn_out, norm_gain, expert_routes, route_gain, w_gate, w_up, w_down):
    stream = (residual.astype(jnp.float32) + attn_out.astype(jnp.float32)).astype(jnp.bfloat16)
    values = stream.astype(jnp.float32)
    inv_rms = lax.rsqrt(lax.optimization_barrier(jnp.mean(values * values, axis=-1, keepdims=True)) + epsilon)
    normed = (values * inv_rms * norm_gain).astype(jnp.bfloat16)
    blocks = TOKENS // TOK_DEV
    route_width = TOK_DEV * WSLOT
    route_ids = expert_routes.reshape(blocks, route_width)
    onehot = (route_ids[:, :, None] == jnp.arange(EW, dtype=jnp.int32)[None, None, :]).astype(jnp.int32)
    earlier = jnp.cumsum(onehot, axis=1) - onehot
    slot_pos = lax.optimization_barrier(jnp.sum(earlier * onehot, axis=2)).astype(jnp.int32)
    live_mask = route_ids < EW
    source = jnp.broadcast_to(jnp.arange(blocks, dtype=jnp.int32)[:, None], (blocks, route_width))
    token_index = (source * TOK_DEV + jnp.arange(route_width, dtype=jnp.int32)[None, :] // WSLOT).astype(jnp.int32)
    buffers = jnp.zeros((EW, blocks, CAP, D), jnp.bfloat16)
    buffers = buffers.at[route_ids, source, slot_pos].set(normed[token_index], mode='drop')

    def one_expert(expert_index):
        slot_rows = buffers[expert_index].reshape(blocks * CAP, D)
        column = (expert_index * FF).astype(jnp.int32)
        gate_cols = lax.dynamic_slice_in_dim(w_gate, column, FF, 1)
        up_cols = lax.dynamic_slice_in_dim(w_up, column, FF, 1)
        down_rows = lax.dynamic_slice_in_dim(w_down, column, FF, 0)
        gate_act = jnp.dot(slot_rows, gate_cols, preferred_element_type=jnp.float32)
        up_act = jnp.dot(slot_rows, up_cols, preferred_element_type=jnp.float32)
        hidden = (jax.nn.silu(gate_act) * up_act).astype(jnp.bfloat16)
        partials = jnp.einsum('rjh,jhd->jrd', hidden.reshape(blocks * CAP, FSPLIT, FF_DEV).astype(jnp.float32), down_rows.reshape(FSPLIT, FF_DEV, D).astype(jnp.float32), precision=lax.Precision.HIGHEST)
        rounded = lax.optimization_barrier(partials.astype(jnp.bfloat16))
        return lax.optimization_barrier(jnp.sum(rounded.astype(jnp.float32), axis=0))
    combined = lax.map(one_expert, jnp.arange(EW, dtype=jnp.int32))
    flat_rows = combined.reshape(EW * blocks * CAP, D)
    row_index = jnp.where(live_mask, route_ids * (blocks * CAP) + source * CAP + slot_pos, 0).astype(jnp.int32)
    live_gains = jnp.where(live_mask, route_gain.reshape(blocks, route_width), 0.0)
    picked = flat_rows[row_index] * live_gains[:, :, None]
    routed_sum = lax.optimization_barrier(jnp.sum(picked.reshape(TOKENS, WSLOT, D), axis=1))
    return (values + routed_sum).astype(jnp.bfloat16)
```

```python
import jax
import jax.numpy as jnp
from jax import lax
from jax.sharding import PartitionSpec as P

FSPLIT = 8


epsilon = 1e-06


def normalize(stream_rows, norm_gain):
    values = stream_rows.astype(jnp.float32)
    inv_rms = lax.rsqrt(jnp.mean(values * values, axis=-1, keepdims=True) + epsilon)
    return (values * inv_rms * norm_gain).astype(jnp.bfloat16)


def route_match(routes, experts, capacity):
    flat_ids = routes.reshape(-1)
    onehot = (flat_ids[:, None] == jnp.arange(experts, dtype=jnp.int32)[None, :]).astype(jnp.int32)
    earlier = jnp.cumsum(onehot, axis=0) - onehot
    slot_pos = jnp.sum(earlier * onehot, axis=1)
    slot_code = jnp.where(flat_ids < experts, flat_ids * capacity + slot_pos, -1)
    target = jnp.arange(experts * capacity, dtype=jnp.int32)
    return slot_code[None, :] == target[:, None]


def selection(routes, experts, capacity):
    matched = route_match(routes, experts, capacity).astype(jnp.int32)
    return matched.reshape(experts * capacity, routes.shape[0], routes.shape[1]).sum(axis=2)


def gain_table(routes, route_gain, experts, capacity):
    matched = route_match(routes, experts, capacity)
    weighted = jnp.where(matched, route_gain.reshape(-1)[None, :], 0.0)
    return weighted.reshape(experts * capacity, routes.shape[0], routes.shape[1]).sum(axis=2).T


def expert_rows(normed, w_gate, w_up, w_down):
    gate_act = jnp.dot(normed, w_gate, preferred_element_type=jnp.float32)
    up_act = jnp.dot(normed, w_up, preferred_element_type=jnp.float32)
    hidden = (jax.nn.silu(gate_act) * up_act).astype(jnp.bfloat16)
    return jnp.dot(hidden, w_down, preferred_element_type=jnp.float32).astype(jnp.bfloat16)


def routed_body(residual, attn_out, norm_gain, expert_routes, route_gain, w_gate, w_up, w_down):
    devices = lax.axis_size("ep")
    tok_here = expert_routes.shape[0]
    route_slots = expert_routes.shape[1]
    experts = devices // FSPLIT
    capacity = route_slots * tok_here // experts
    model_width = w_gate.shape[0]
    stream_feat = (residual.astype(jnp.float32) + attn_out.astype(jnp.float32)).astype(jnp.bfloat16)
    stream_rows = lax.all_to_all(stream_feat, "ep", split_axis=0, concat_axis=1, tiled=True)
    combine_weights = gain_table(expert_routes, route_gain, experts, capacity)
    normed_rows = normalize(stream_rows, norm_gain)
    select = selection(expert_routes, experts, capacity).astype(jnp.bfloat16)
    per_expert = jnp.dot(select, normed_rows, preferred_element_type=jnp.float32).astype(
        jnp.bfloat16
    )
    per_expert = per_expert.reshape(experts, 1, capacity, model_width)
    outgoing = jnp.broadcast_to(per_expert, (experts, FSPLIT, capacity, model_width))
    outgoing = outgoing.reshape(devices, capacity, model_width)
    received = lax.all_to_all(outgoing, "ep", split_axis=0, concat_axis=0, tiled=True)
    slot_count = received.shape[1]
    partial_value = expert_rows(received.reshape(-1, model_width), w_gate, w_up, w_down)
    partial_value = partial_value.reshape(devices, slot_count, model_width)
    returned = lax.all_to_all(partial_value, "ep", split_axis=0, concat_axis=0, tiled=True)
    summed = (
        returned.reshape(experts, FSPLIT, capacity, model_width).astype(jnp.float32).sum(axis=1)
    )
    summed = summed.reshape(experts * capacity, model_width)
    routed_sum = jnp.dot(combine_weights, summed, precision=lax.Precision.HIGHEST)
    return (stream_rows.astype(jnp.float32) + routed_sum).astype(jnp.bfloat16)


def token_gains(routes, route_gain, experts):
    named = routes[:, :, None] == jnp.arange(experts, dtype=jnp.int32)
    return jnp.where(named, route_gain[:, :, None], 0.0).sum(axis=1)


def dense_body(residual, attn_out, norm_gain, expert_routes, route_gain, w_gate, w_up, w_down):
    experts = lax.axis_size("ep") // FSPLIT
    tok_here = expert_routes.shape[0]
    me = lax.axis_index("ep")
    stream_feat = (residual.astype(jnp.float32) + attn_out.astype(jnp.float32)).astype(jnp.bfloat16)
    stream = lax.all_gather(stream_feat.T, "ep", axis=0, tiled=True)
    gains = lax.all_gather(token_gains(expert_routes, route_gain, experts), "ep", axis=0, tiled=True)
    gain_here = lax.dynamic_slice_in_dim(gains, me // FSPLIT, 1, axis=1)
    scaled_gate = (w_gate.astype(jnp.float32) * norm_gain[:, None]).astype(jnp.bfloat16)
    scaled_up = (w_up.astype(jnp.float32) * norm_gain[:, None]).astype(jnp.bfloat16)
    values = stream.astype(jnp.float32)
    inv_rms = lax.rsqrt(jnp.mean(values * values, axis=0) + epsilon)[:, None]
    over_features = (((0,), (0,)), ((), ()))
    gate_act = lax.dot_general(stream, scaled_gate, over_features, preferred_element_type=jnp.float32)
    up_act = lax.dot_general(stream, scaled_up, over_features, preferred_element_type=jnp.float32)
    hidden = (jax.nn.silu(gate_act * inv_rms) * (up_act * inv_rms)).astype(jnp.bfloat16)
    partial_value = jnp.dot(hidden, w_down, preferred_element_type=jnp.float32)
    partial_value = (partial_value * gain_here).astype(jnp.bfloat16)
    routed_sum = lax.psum_scatter(partial_value, "ep", scatter_dimension=0, tiled=True)
    stream_rows = lax.dynamic_slice_in_dim(stream, me * tok_here, tok_here, axis=1).T
    return (stream_rows.astype(jnp.float32) + routed_sum.astype(jnp.float32)).astype(jnp.bfloat16)


def body(residual, attn_out, norm_gain, expert_routes, route_gain, w_gate, w_up, w_down):
    tok_here, route_slots = expert_routes.shape
    capacity = route_slots * tok_here // (lax.axis_size("ep") // FSPLIT)
    chosen = dense_body if capacity >= tok_here else routed_body
    return chosen(residual, attn_out, norm_gain, expert_routes, route_gain, w_gate, w_up, w_down)


def solution(mesh):
    in_specs = (
        P("groups", "ep"),
        P("groups", "ep"),
        P(),
        P(("groups", "ep"), None),
        P(("groups", "ep"), None),
        P(None, "ep"),
        P(None, "ep"),
        P("ep", None),
    )
    out_specs = P(("groups", "ep"), None)
    return jax.shard_map(body, mesh=mesh, in_specs=in_specs, out_specs=out_specs, check_vma=False)
```

```python
import jax
import jax.numpy as jnp
from jax import lax
from jax.sharding import PartitionSpec as P

FSPLIT = 8


epsilon = 1e-06


def normalize(stream_rows, norm_gain):
    values = stream_rows.astype(jnp.float32)
    inv_rms = lax.rsqrt(jnp.mean(values * values, axis=-1, keepdims=True) + epsilon)
    return (values * inv_rms * norm_gain).astype(jnp.bfloat16)


def route_match(routes, experts, capacity):
    flat_ids = routes.reshape(-1)
    onehot = (flat_ids[:, None] == jnp.arange(experts, dtype=jnp.int32)[None, :]).astype(jnp.int32)
    earlier = jnp.cumsum(onehot, axis=0) - onehot
    slot_pos = jnp.sum(earlier * onehot, axis=1)
    slot_code = jnp.where(flat_ids < experts, flat_ids * capacity + slot_pos, -1)
    target = jnp.arange(experts * capacity, dtype=jnp.int32)
    return slot_code[None, :] == target[:, None]


def selection(routes, experts, capacity):
    matched = route_match(routes, experts, capacity).astype(jnp.int32)
    return matched.reshape(experts * capacity, routes.shape[0], routes.shape[1]).sum(axis=2)


def gain_table(routes, route_gain, experts, capacity):
    matched = route_match(routes, experts, capacity)
    weighted = jnp.where(matched, route_gain.reshape(-1)[None, :], 0.0)
    return weighted.reshape(experts * capacity, routes.shape[0], routes.shape[1]).sum(axis=2).T


def expert_rows(normed, w_gate, w_up, w_down):
    gate_act = jnp.dot(normed, w_gate, preferred_element_type=jnp.float32)
    up_act = jnp.dot(normed, w_up, preferred_element_type=jnp.float32)
    hidden = (jax.nn.silu(gate_act) * up_act).astype(jnp.bfloat16)
    return jnp.dot(hidden, w_down, preferred_element_type=jnp.float32).astype(jnp.bfloat16)


def routed_body(residual, attn_out, norm_gain, expert_routes, route_gain, w_gate, w_up, w_down):
    devices = lax.axis_size("ep")
    tok_here = expert_routes.shape[0]
    route_slots = expert_routes.shape[1]
    experts = devices // FSPLIT
    capacity = route_slots * tok_here // experts
    model_width = w_gate.shape[0]
    stream_feat = (residual.astype(jnp.float32) + attn_out.astype(jnp.float32)).astype(jnp.bfloat16)
    stream_rows = lax.all_to_all(stream_feat, "ep", split_axis=0, concat_axis=1, tiled=True)
    combine_weights = gain_table(expert_routes, route_gain, experts, capacity)
    normed_rows = normalize(stream_rows, norm_gain)
    select = selection(expert_routes, experts, capacity).astype(jnp.bfloat16)
    per_expert = jnp.dot(select, normed_rows, preferred_element_type=jnp.float32).astype(
        jnp.bfloat16
    )
    per_expert = per_expert.reshape(experts, 1, capacity, model_width)
    outgoing = jnp.broadcast_to(per_expert, (experts, FSPLIT, capacity, model_width))
    outgoing = outgoing.reshape(devices, capacity, model_width)
    received = lax.all_to_all(outgoing, "ep", split_axis=0, concat_axis=0, tiled=True)
    slot_count = received.shape[1]
    partial_value = expert_rows(received.reshape(-1, model_width), w_gate, w_up, w_down)
    partial_value = partial_value.reshape(devices, slot_count, model_width)
    returned = lax.all_to_all(partial_value, "ep", split_axis=0, concat_axis=0, tiled=True)
    summed = (
        returned.reshape(experts, FSPLIT, capacity, model_width).astype(jnp.float32).sum(axis=1)
    )
    summed = summed.reshape(experts * capacity, model_width)
    routed_sum = jnp.dot(combine_weights, summed, precision=lax.Precision.HIGHEST)
    return (stream_rows.astype(jnp.float32) + routed_sum).astype(jnp.bfloat16)


def token_gains(routes, route_gain, experts):
    named = routes[:, :, None] == jnp.arange(experts, dtype=jnp.int32)
    return jnp.where(named, route_gain[:, :, None], 0.0).sum(axis=1)


def ring_order(chips):
    return list(range(0, chips, 2)) + list(reversed(range(1, chips, 2)))


def ring_shift(value, ring, step):
    chips = len(ring)
    pairs = [
        (2 * ring[i] + core, 2 * ring[(i + step) % chips] + core)
        for i in range(chips)
        for core in range(2)
    ]
    return lax.ppermute(value, "ep", pairs)


def swap_cores(value):
    return lax.ppermute(value, "ep", [(i, i ^ 1) for i in range(lax.axis_size("ep"))])


def gather_small(value, chips, chip):
    width = 1
    while width < chips:
        pairs = [
            (2 * i + core, 2 * (i ^ width) + core) for i in range(chips) for core in range(2)
        ]
        other = lax.ppermute(value, "ep", pairs)
        upper = (chip // width) % 2 == 1
        value = jnp.concatenate(
            [jnp.where(upper, other, value), jnp.where(upper, value, other)], axis=0
        )
        width *= 2
    return value


def dense_body(residual, attn_out, norm_gain, expert_routes, route_gain, w_gate, w_up, w_down):
    devices = lax.axis_size("ep")
    experts = devices // FSPLIT
    chips = devices // 2
    far = chips // 2
    tok_here = expert_routes.shape[0]
    feat_here = residual.shape[1]
    model_width = w_gate.shape[0]
    hidden_here = w_gate.shape[1]
    ring = ring_order(chips)
    me = lax.axis_index("ep")
    chip, core = me // 2, me % 2
    spot = jnp.asarray([ring.index(i) for i in range(chips)], jnp.int32)[chip]
    chip_at = jnp.asarray(ring, jnp.int32)

    def chip_by_distance(distance):
        return chip_at[(spot + distance) % chips]

    stream_feat = (residual.astype(jnp.float32) + attn_out.astype(jnp.float32)).astype(jnp.bfloat16)
    by_core = stream_feat.reshape(chips, 2, tok_here, feat_here)
    mine = lax.dynamic_index_in_dim(by_core, core, 1, keepdims=False)
    theirs = lax.dynamic_index_in_dim(by_core, 1 - core, 1, keepdims=False)
    swapped = swap_cores(theirs)
    block = jnp.concatenate(
        [jnp.where(core == 0, mine, swapped), jnp.where(core == 0, swapped, mine)], axis=2
    )
    block = block.reshape(2, far * tok_here, 2 * feat_here)
    blocks = {0: [block[0], block[1]]}

    scaled = jnp.concatenate([w_gate, w_up], axis=1).astype(jnp.float32) * norm_gain[:, None]
    scaled = scaled.astype(jnp.bfloat16)
    weights = [scaled, swap_cores(scaled)]
    down = jnp.concatenate([w_down, swap_cores(w_down)], axis=0)
    gains = gather_small(token_gains(expert_routes, route_gain, experts), chips, chip)
    gain_here = lax.dynamic_slice_in_dim(gains, me // FSPLIT, 1, axis=1)

    for distance in range(1, far):
        for sign, order in ((-1, (0, 1)), (1, (1, 0))):
            came = [None, None]
            for part in order:
                came[part] = ring_shift(blocks[sign * (distance - 1)][part], ring, -sign)
            blocks[sign * distance] = came
    blocks[far] = [
        ring_shift(blocks[1 - far][0], ring, 1),
        ring_shift(blocks[far - 1][1], ring, -1),
    ]

    sums = [[0.0, 0.0], [0.0, 0.0]]
    squares = [0.0, 0.0]
    stream_rows = jnp.zeros((tok_here, model_width), jnp.bfloat16)
    for distance in sorted(blocks, key=abs):
        source = chip_by_distance(distance)
        for part in range(2):
            rows = blocks[distance][part]
            values = rows.astype(jnp.float32)
            squares[part] += jnp.sum(values * values, axis=1, keepdims=True)
            for which in range(2):
                piece = lax.dynamic_slice_in_dim(
                    weights[which], source * 2 * feat_here, 2 * feat_here, axis=0
                )
                sums[part][which] += jnp.dot(rows, piece, preferred_element_type=jnp.float32)
        row = (chip % far) * tok_here
        own = jnp.where(
            chip < far,
            lax.dynamic_slice_in_dim(blocks[distance][0], row, tok_here, axis=0),
            lax.dynamic_slice_in_dim(blocks[distance][1], row, tok_here, axis=0),
        )
        stream_rows = lax.dynamic_update_slice_in_dim(
            stream_rows, own, source * 2 * feat_here, axis=1
        )

    hidden = []
    for part in range(2):
        inv_rms = lax.rsqrt(squares[part] / model_width + epsilon)
        acts = [act * inv_rms for act in sums[part]]
        hidden.append(
            jnp.concatenate(
                [jax.nn.silu(act[:, :hidden_here]) * act[:, hidden_here:] for act in acts], axis=1
            )
        )
    hidden = jnp.concatenate(hidden, axis=0).astype(jnp.bfloat16)

    def contribution(rows, row_gain):
        out = jnp.dot(rows, down, preferred_element_type=jnp.float32)
        return (out * row_gain).astype(jnp.bfloat16)

    half = model_width // 2

    def of_chip(table, distance):
        return lax.dynamic_slice_in_dim(
            table, chip_by_distance(distance) * tok_here, tok_here, axis=0
        )

    first = contribution(of_chip(hidden, far), of_chip(gain_here, far))
    moving = {
        1: [ring_shift(first[:, :half], ring, 1), None],
        -1: [None, ring_shift(first[:, half:], ring, -1)],
    }
    everything = contribution(hidden, gain_here)
    for distance in range(far - 1, 0, -1):
        for sign, order in ((1, (1, 0)), (-1, (0, 1))):
            add = of_chip(everything, sign * distance)
            sent = [None, None]
            for part in order:
                value = add[:, part * half : (part + 1) * half]
                if moving[sign][part] is not None:
                    value = value.astype(jnp.float32) + moving[sign][part].astype(jnp.float32)
                    value = value.astype(jnp.bfloat16)
                sent[part] = ring_shift(value, ring, sign)
            moving[sign] = sent
    out = stream_rows.astype(jnp.float32) + of_chip(everything, 0).astype(jnp.float32)
    outs = []
    for part in range(2):
        total = out[:, part * half : (part + 1) * half]
        for sign in (1, -1):
            if moving[sign][part] is not None:
                total = total + moving[sign][part].astype(jnp.float32)
        outs.append(total)
    return jnp.concatenate(outs, axis=1).astype(jnp.bfloat16)


def body(residual, attn_out, norm_gain, expert_routes, route_gain, w_gate, w_up, w_down):
    tok_here, route_slots = expert_routes.shape
    devices = lax.axis_size("ep")
    capacity = route_slots * tok_here // (devices // FSPLIT)
    dense = capacity >= tok_here and devices % 4 == 0 and devices & (devices - 1) == 0
    chosen = dense_body if dense else routed_body
    return chosen(residual, attn_out, norm_gain, expert_routes, route_gain, w_gate, w_up, w_down)


def solution(mesh):
    in_specs = (
        P("groups", "ep"),
        P("groups", "ep"),
        P(),
        P(("groups", "ep"), None),
        P(("groups", "ep"), None),
        P(None, "ep"),
        P(None, "ep"),
        P("ep", None),
    )
    out_specs = P(("groups", "ep"), None)
    return jax.shard_map(body, mesh=mesh, in_specs=in_specs, out_specs=out_specs, check_vma=False)
```

```python
import jax
import jax.numpy as jnp
from jax import lax
from jax.experimental import pallas as pl
from jax.experimental.pallas import tpu as pltpu
from jax.sharding import PartitionSpec as P

FSPLIT = 8


epsilon = 1e-06


def normalize(stream_rows, norm_gain):
    values = stream_rows.astype(jnp.float32)
    inv_rms = lax.rsqrt(jnp.mean(values * values, axis=-1, keepdims=True) + epsilon)
    return (values * inv_rms * norm_gain).astype(jnp.bfloat16)


def route_match(routes, experts, capacity):
    flat_ids = routes.reshape(-1)
    onehot = (flat_ids[:, None] == jnp.arange(experts, dtype=jnp.int32)[None, :]).astype(jnp.int32)
    earlier = jnp.cumsum(onehot, axis=0) - onehot
    slot_pos = jnp.sum(earlier * onehot, axis=1)
    slot_code = jnp.where(flat_ids < experts, flat_ids * capacity + slot_pos, -1)
    target = jnp.arange(experts * capacity, dtype=jnp.int32)
    return slot_code[None, :] == target[:, None]


def selection(routes, experts, capacity):
    matched = route_match(routes, experts, capacity).astype(jnp.int32)
    return matched.reshape(experts * capacity, routes.shape[0], routes.shape[1]).sum(axis=2)


def gain_table(routes, route_gain, experts, capacity):
    matched = route_match(routes, experts, capacity)
    weighted = jnp.where(matched, route_gain.reshape(-1)[None, :], 0.0)
    return weighted.reshape(experts * capacity, routes.shape[0], routes.shape[1]).sum(axis=2).T


def expert_rows(normed, w_gate, w_up, w_down):
    gate_act = jnp.dot(normed, w_gate, preferred_element_type=jnp.float32)
    up_act = jnp.dot(normed, w_up, preferred_element_type=jnp.float32)
    hidden = (jax.nn.silu(gate_act) * up_act).astype(jnp.bfloat16)
    return jnp.dot(hidden, w_down, preferred_element_type=jnp.float32).astype(jnp.bfloat16)


def routed_body(residual, attn_out, norm_gain, expert_routes, route_gain, w_gate, w_up, w_down):
    devices = lax.axis_size("ep")
    tok_here = expert_routes.shape[0]
    route_slots = expert_routes.shape[1]
    experts = devices // FSPLIT
    capacity = route_slots * tok_here // experts
    model_width = w_gate.shape[0]
    stream_feat = (residual.astype(jnp.float32) + attn_out.astype(jnp.float32)).astype(jnp.bfloat16)
    stream_rows = lax.all_to_all(stream_feat, "ep", split_axis=0, concat_axis=1, tiled=True)
    combine_weights = gain_table(expert_routes, route_gain, experts, capacity)
    normed_rows = normalize(stream_rows, norm_gain)
    select = selection(expert_routes, experts, capacity).astype(jnp.bfloat16)
    per_expert = jnp.dot(select, normed_rows, preferred_element_type=jnp.float32).astype(
        jnp.bfloat16
    )
    per_expert = per_expert.reshape(experts, 1, capacity, model_width)
    outgoing = jnp.broadcast_to(per_expert, (experts, FSPLIT, capacity, model_width))
    outgoing = outgoing.reshape(devices, capacity, model_width)
    received = lax.all_to_all(outgoing, "ep", split_axis=0, concat_axis=0, tiled=True)
    slot_count = received.shape[1]
    partial_value = expert_rows(received.reshape(-1, model_width), w_gate, w_up, w_down)
    partial_value = partial_value.reshape(devices, slot_count, model_width)
    returned = lax.all_to_all(partial_value, "ep", split_axis=0, concat_axis=0, tiled=True)
    summed = (
        returned.reshape(experts, FSPLIT, capacity, model_width).astype(jnp.float32).sum(axis=1)
    )
    summed = summed.reshape(experts * capacity, model_width)
    routed_sum = jnp.dot(combine_weights, summed, precision=lax.Precision.HIGHEST)
    return (stream_rows.astype(jnp.float32) + routed_sum).astype(jnp.bfloat16)


def token_gains(routes, route_gain, experts):
    named = routes[:, :, None] == jnp.arange(experts, dtype=jnp.int32)
    return jnp.where(named, route_gain[:, :, None], 0.0).sum(axis=1)


def ring_order(chips):
    return list(range(0, chips, 2)) + list(reversed(range(1, chips, 2)))


def swap_cores(value):
    return lax.ppermute(value, "ep", [(i, i ^ 1) for i in range(lax.axis_size("ep"))])


def gather_small(value, chips, chip):
    width = 1
    while width < chips:
        pairs = [
            (2 * i + core, 2 * (i ^ width) + core) for i in range(chips) for core in range(2)
        ]
        other = lax.ppermute(value, "ep", pairs)
        upper = (chip // width) % 2 == 1
        value = jnp.concatenate(
            [jnp.where(upper, other, value), jnp.where(upper, value, other)], axis=0
        )
        width *= 2
    return value


def ring_shift(value, ring, step):
    chips = len(ring)
    pairs = [
        (2 * ring[i] + core, 2 * ring[(i + step) % chips] + core)
        for i in range(chips)
        for core in range(2)
    ]
    return lax.ppermute(value, "ep", pairs)


VMEM_BYTES = 32 * 1024 * 1024


def whole(shape):
    return pl.BlockSpec(shape, lambda i, where: (0,) * len(shape))


def accumulate(where, positions, parts, norm_gain, weights, carried, closing):
    count = len(positions)
    rows, width = parts[0][0].shape
    hidden_here = weights[0].shape[1]
    model_width = weights[0].shape[0]
    tok_here = closing["tok_here"]
    far = rows // tok_here
    last = "gain" in closing
    first = carried is None
    side = closing["side"]

    def kernel(where_ref, *refs):
        refs = list(refs)
        xs = [[refs.pop(0) for _ in range(2)] for _ in range(count)]
        scales = [refs.pop(0) for _ in range(count)]
        tables = [[refs.pop(0) for _ in range(len(weights))] for _ in range(count)]
        acc_in, sq_in = (None, None) if first else (refs.pop(0), refs.pop(0))
        gain_ref = refs.pop(0) if last else None
        owns = [refs.pop(0) for _ in range(count)]
        if last:
            hidden_ref = refs.pop(0)
        else:
            acc_out, sq_out = refs.pop(0), refs.pop(0)
        chip = where_ref[0]
        for b in range(count):
            start = pl.multiple_of(lax.rem(chip, far) * tok_here, tok_here)

            @pl.when(chip < far)
            def _():
                owns[b][...] = xs[b][0][pl.ds(start, tok_here), :]

            @pl.when(chip >= far)
            def _():
                owns[b][...] = xs[b][1][pl.ds(start, tok_here), :]

        for part in range(2):
            span = slice(part * rows, (part + 1) * rows)
            scaled, squares = [], None if first else sq_in[span, :]
            for b in range(count):
                values = xs[b][part][...].astype(jnp.float32)
                for lane in range(0, width, side):
                    piece = values[:, lane : lane + side]
                    squares = piece * piece if squares is None else squares + piece * piece
                scaled.append((values * scales[b][0]).astype(jnp.bfloat16))
            totals = []
            for which in range(len(weights)):
                cols = slice(which * hidden_here, (which + 1) * hidden_here)
                total = None if first else acc_in[span, cols]
                for b in range(count):
                    product = jnp.dot(
                        scaled[b], tables[b][which][...], preferred_element_type=jnp.float32
                    )
                    total = product if total is None else total + product
                if last:
                    totals.append(total)
                else:
                    acc_out[span, cols] = total
            if last:
                mean = jnp.sum(squares, axis=1, keepdims=True) / model_width
                inv_rms = lax.rsqrt(mean + epsilon)
                for core in range(len(weights) // 2):
                    gate_act = totals[2 * core] * inv_rms
                    up_act = totals[2 * core + 1] * inv_rms
                    act = gate_act * jax.nn.sigmoid(gate_act) * up_act * gain_ref[span, :]
                    cols = slice(core * hidden_here, (core + 1) * hidden_here)
                    hidden_ref[span, cols] = act.astype(jnp.bfloat16)
            else:
                sq_out[span, :] = squares

    def table_spec(position):
        return pl.BlockSpec((width, hidden_here), lambda i, where: (where[position], 0))

    operands = [half for block in parts for half in block]
    in_specs = [whole((rows, width))] * (2 * count)
    for position in positions:
        operands.append(norm_gain)
        in_specs.append(
            pl.BlockSpec((1, 1, width), lambda i, where, p=position: (where[p], 0, 0))
        )
    for position in positions:
        operands.extend(weights)
        in_specs.extend([table_spec(position)] * len(weights))
    sums = (2 * rows, len(weights) * hidden_here)
    aliases = {}
    if not first:
        if not last:
            aliases = {len(operands) + 1: count, len(operands) + 2: count + 1}
        operands.extend(carried)
        in_specs.extend([whole(sums), whole((2 * rows, side))])
    out_shape = [jax.ShapeDtypeStruct((tok_here, width), jnp.bfloat16)] * count
    out_specs = [whole((tok_here, width))] * count
    if last:
        operands.append(closing["gain"])
        in_specs.append(whole((2 * rows, 1)))
        shape = (2 * rows, len(weights) // 2 * hidden_here)
        out_shape.append(jax.ShapeDtypeStruct(shape, jnp.bfloat16))
        out_specs.append(whole(shape))
    else:
        out_shape.append(jax.ShapeDtypeStruct(sums, jnp.float32))
        out_shape.append(jax.ShapeDtypeStruct((2 * rows, side), jnp.float32))
        out_specs.extend([whole(sums), whole((2 * rows, side))])
    flops = 2 * count * 2 * rows * width * sums[1]
    return pl.pallas_call(
        kernel,
        grid_spec=pltpu.PrefetchScalarGridSpec(
            num_scalar_prefetch=1, grid=(1,), in_specs=in_specs, out_specs=out_specs
        ),
        out_shape=out_shape,
        input_output_aliases=aliases,
        compiler_params=pltpu.CompilerParams(vmem_limit_bytes=VMEM_BYTES),
        cost_estimate=pl.CostEstimate(
            flops=flops,
            bytes_accessed=count * width * (rows * 4 + sums[1] * 2) + sums[0] * sums[1] * 8,
            transcendentals=0,
        ),
    )(where, *operands)


def add_rows(where, position, table, moved):
    rows, width = moved.shape
    steps = 2

    def kernel(where_ref, table_ref, moved_ref, out_ref):
        total = table_ref[...].astype(jnp.float32) + moved_ref[...].astype(jnp.float32)
        out_ref[...] = total.astype(jnp.bfloat16)

    here = pl.BlockSpec((rows, width // steps), lambda i, where: (0, i))
    return pl.pallas_call(
        kernel,
        grid_spec=pltpu.PrefetchScalarGridSpec(
            num_scalar_prefetch=1,
            grid=(steps,),
            in_specs=[
                pl.BlockSpec((rows, width // steps), lambda i, where: (where[position], i)),
                here,
            ],
            out_specs=here,
        ),
        out_shape=jax.ShapeDtypeStruct((rows, width), jnp.bfloat16),
        compiler_params=pltpu.CompilerParams(vmem_limit_bytes=VMEM_BYTES),
        cost_estimate=pl.CostEstimate(
            flops=rows * width, bytes_accessed=rows * width * 6, transcendentals=0
        ),
    )(where, table, moved)


def own_rows(where, positions, pieces, tables):
    rows, width = pieces[0].shape
    chips = len(pieces)
    model_width = chips * width
    half = model_width // 2

    def kernel(where_ref, *refs):
        out_ref = refs[-1]
        for part in range(2):
            out_ref[:, part * half : (part + 1) * half] = refs[chips + part][...].astype(
                jnp.float32
            )
        for k in range(chips):
            start = pl.multiple_of(where_ref[positions[k]] * width, width)
            out_ref[:, pl.ds(start, width)] += refs[k][...].astype(jnp.float32)

    return pl.pallas_call(
        kernel,
        grid_spec=pltpu.PrefetchScalarGridSpec(
            num_scalar_prefetch=1,
            grid=(1,),
            in_specs=[whole((rows, width))] * chips
            + [pl.BlockSpec((rows, half), lambda i, where: (where[0], 0))] * 2,
            out_specs=whole((rows, model_width)),
        ),
        out_shape=jax.ShapeDtypeStruct((rows, model_width), jnp.float32),
        compiler_params=pltpu.CompilerParams(vmem_limit_bytes=VMEM_BYTES),
        cost_estimate=pl.CostEstimate(
            flops=rows * model_width, bytes_accessed=rows * model_width * 8, transcendentals=0
        ),
    )(where, *pieces, *tables)


def final_sum(base, arrived):
    rows, model_width = base.shape
    half = model_width // 2

    def kernel(base_ref, *refs):
        out_ref = refs[-1]
        for part in range(2):
            cols = slice(part * half, (part + 1) * half)
            total = base_ref[:, cols]
            for k in range(len(arrived[part])):
                total = total + refs[k + part * len(arrived[0])][...].astype(jnp.float32)
            out_ref[:, cols] = total.astype(jnp.bfloat16)

    return pl.pallas_call(
        kernel,
        out_shape=jax.ShapeDtypeStruct((rows, model_width), jnp.bfloat16),
        compiler_params=pltpu.CompilerParams(vmem_limit_bytes=VMEM_BYTES),
        cost_estimate=pl.CostEstimate(
            flops=rows * model_width * 3, bytes_accessed=rows * model_width * 10, transcendentals=0
        ),
    )(base, *arrived[0], *arrived[1])


def dense_body(residual, attn_out, norm_gain, expert_routes, route_gain, w_gate, w_up, w_down):
    devices = lax.axis_size("ep")
    experts = devices // FSPLIT
    chips = devices // 2
    far = chips // 2
    tok_here = expert_routes.shape[0]
    feat_here = residual.shape[1]
    model_width = w_gate.shape[0]
    half = model_width // 2
    ring = ring_order(chips)
    me = lax.axis_index("ep")
    chip, core = me // 2, me % 2
    seen = [[ring[(ring.index(i) + d) % chips] for d in range(chips)] for i in range(chips)]
    where = lax.dynamic_index_in_dim(jnp.asarray(seen, jnp.int32), chip, 0, keepdims=False)

    stream_feat = (residual.astype(jnp.float32) + attn_out.astype(jnp.float32)).astype(jnp.bfloat16)
    by_core = stream_feat.reshape(chips, 2, tok_here, feat_here)
    mine = lax.dynamic_index_in_dim(by_core, core, 1, keepdims=False)
    theirs = lax.dynamic_index_in_dim(by_core, 1 - core, 1, keepdims=False)
    swapped = swap_cores(theirs)
    block = jnp.concatenate(
        [jnp.where(core == 0, mine, swapped), jnp.where(core == 0, swapped, mine)], axis=2
    )
    block = block.reshape(2, far * tok_here, 2 * feat_here)
    blocks = {0: [block[0], block[1]]}

    own_gains = token_gains(expert_routes, route_gain, experts)
    swapped, w_gate, w_up, w_down, own_gains = lax.optimization_barrier(
        (swapped, w_gate, w_up, w_down, own_gains)
    )
    weights = [w_gate, w_up, swap_cores(w_gate), swap_cores(w_up)]
    other_down = swap_cores(w_down)
    down = [
        jnp.concatenate([w_down[:, cols], other_down[:, cols]], axis=0)
        for cols in (slice(0, half), slice(half, model_width))
    ]
    gains = gather_small(own_gains, chips, chip)
    gain_here = lax.dynamic_slice_in_dim(gains, me // FSPLIT, 1, axis=1)

    for distance in range(1, far):
        for sign, order in ((-1, (0, 1)), (1, (1, 0))):
            came = [None, None]
            for part in order:
                came[part] = ring_shift(blocks[sign * (distance - 1)][part], ring, -sign)
            blocks[sign * distance] = came
    blocks[far] = [
        ring_shift(blocks[1 - far][0], ring, 1),
        ring_shift(blocks[far - 1][1], ring, -1),
    ]

    gain_rows = norm_gain.reshape(chips, 1, 2 * feat_here)
    closing = {"tok_here": tok_here, "side": 128}
    carried, owns, positions = None, [], []
    for distance in range(far + 1):
        group = [distance] if distance in (0, far) else [distance, -distance]
        at = [d % chips for d in group]
        if distance == far:
            closing["gain"] = gain_here
        made = accumulate(
            where, at, [blocks[d] for d in group], gain_rows, weights, carried, closing
        )
        owns.extend(made[: len(at)])
        positions.extend(at)
        carried = made[len(at) :]
    hidden = carried[0]

    def contribution(rows, part):
        return jnp.dot(rows, down[part], preferred_element_type=jnp.float32).astype(jnp.bfloat16)

    farthest = lax.dynamic_slice_in_dim(hidden, where[far] * tok_here, tok_here, axis=0)
    moving = {
        1: [ring_shift(contribution(farthest, 0), ring, 1), None],
        -1: [None, ring_shift(contribution(farthest, 1), ring, -1)],
    }
    everything = [contribution(hidden, part) for part in range(2)]
    base = own_rows(where, positions, owns, everything)
    for distance in range(far - 1, 0, -1):
        for sign, order in ((1, (1, 0)), (-1, (0, 1))):
            position = (sign * distance) % chips
            sent = [None, None]
            for part in order:
                if moving[sign][part] is None:
                    value = lax.dynamic_slice_in_dim(
                        everything[part], where[position] * tok_here, tok_here, axis=0
                    )
                else:
                    value = add_rows(where, position, everything[part], moving[sign][part])
                sent[part] = ring_shift(value, ring, sign)
            moving[sign] = sent
    arrived = [
        [moving[sign][part] for sign in (1, -1) if moving[sign][part] is not None]
        for part in range(2)
    ]
    return final_sum(base, arrived)


def body(residual, attn_out, norm_gain, expert_routes, route_gain, w_gate, w_up, w_down):
    tok_here, route_slots = expert_routes.shape
    devices = lax.axis_size("ep")
    capacity = route_slots * tok_here // (devices // FSPLIT)
    dense = capacity >= tok_here and devices % 4 == 0 and devices & (devices - 1) == 0
    chosen = dense_body if dense else routed_body
    return chosen(residual, attn_out, norm_gain, expert_routes, route_gain, w_gate, w_up, w_down)


def solution(mesh):
    in_specs = (
        P("groups", "ep"),
        P("groups", "ep"),
        P(),
        P(("groups", "ep"), None),
        P(("groups", "ep"), None),
        P(None, "ep"),
        P(None, "ep"),
        P("ep", None),
    )
    out_specs = P(("groups", "ep"), None)
    return jax.shard_map(body, mesh=mesh, in_specs=in_specs, out_specs=out_specs, check_vma=False)
```

```python
import jax
import jax.numpy as jnp
from jax import lax
from jax.experimental import pallas as pl
from jax.experimental.pallas import tpu as pltpu
from jax.sharding import PartitionSpec as P

FSPLIT = 8


epsilon = 1e-06


def normalize(stream_rows, norm_gain):
    values = stream_rows.astype(jnp.float32)
    inv_rms = lax.rsqrt(jnp.mean(values * values, axis=-1, keepdims=True) + epsilon)
    return (values * inv_rms * norm_gain).astype(jnp.bfloat16)


def route_match(routes, experts, capacity):
    flat_ids = routes.reshape(-1)
    onehot = (flat_ids[:, None] == jnp.arange(experts, dtype=jnp.int32)[None, :]).astype(jnp.int32)
    earlier = jnp.cumsum(onehot, axis=0) - onehot
    slot_pos = jnp.sum(earlier * onehot, axis=1)
    slot_code = jnp.where(flat_ids < experts, flat_ids * capacity + slot_pos, -1)
    target = jnp.arange(experts * capacity, dtype=jnp.int32)
    return slot_code[None, :] == target[:, None]


def selection(routes, experts, capacity):
    matched = route_match(routes, experts, capacity).astype(jnp.int32)
    return matched.reshape(experts * capacity, routes.shape[0], routes.shape[1]).sum(axis=2)


def gain_table(routes, route_gain, experts, capacity):
    matched = route_match(routes, experts, capacity)
    weighted = jnp.where(matched, route_gain.reshape(-1)[None, :], 0.0)
    return weighted.reshape(experts * capacity, routes.shape[0], routes.shape[1]).sum(axis=2).T


def expert_rows(normed, w_gate, w_up, w_down):
    gate_act = jnp.dot(normed, w_gate, preferred_element_type=jnp.float32)
    up_act = jnp.dot(normed, w_up, preferred_element_type=jnp.float32)
    hidden = (jax.nn.silu(gate_act) * up_act).astype(jnp.bfloat16)
    return jnp.dot(hidden, w_down, preferred_element_type=jnp.float32).astype(jnp.bfloat16)


def routed_body(residual, attn_out, norm_gain, expert_routes, route_gain, w_gate, w_up, w_down):
    devices = lax.axis_size("ep")
    tok_here = expert_routes.shape[0]
    route_slots = expert_routes.shape[1]
    experts = devices // FSPLIT
    capacity = route_slots * tok_here // experts
    model_width = w_gate.shape[0]
    stream_feat = (residual.astype(jnp.float32) + attn_out.astype(jnp.float32)).astype(jnp.bfloat16)
    stream_rows = lax.all_to_all(stream_feat, "ep", split_axis=0, concat_axis=1, tiled=True)
    combine_weights = gain_table(expert_routes, route_gain, experts, capacity)
    normed_rows = normalize(stream_rows, norm_gain)
    select = selection(expert_routes, experts, capacity).astype(jnp.bfloat16)
    per_expert = jnp.dot(select, normed_rows, preferred_element_type=jnp.float32).astype(
        jnp.bfloat16
    )
    per_expert = per_expert.reshape(experts, 1, capacity, model_width)
    outgoing = jnp.broadcast_to(per_expert, (experts, FSPLIT, capacity, model_width))
    outgoing = outgoing.reshape(devices, capacity, model_width)
    received = lax.all_to_all(outgoing, "ep", split_axis=0, concat_axis=0, tiled=True)
    slot_count = received.shape[1]
    partial_value = expert_rows(received.reshape(-1, model_width), w_gate, w_up, w_down)
    partial_value = partial_value.reshape(devices, slot_count, model_width)
    returned = lax.all_to_all(partial_value, "ep", split_axis=0, concat_axis=0, tiled=True)
    summed = (
        returned.reshape(experts, FSPLIT, capacity, model_width).astype(jnp.float32).sum(axis=1)
    )
    summed = summed.reshape(experts * capacity, model_width)
    routed_sum = jnp.dot(combine_weights, summed, precision=lax.Precision.HIGHEST)
    return (stream_rows.astype(jnp.float32) + routed_sum).astype(jnp.bfloat16)


def token_gains(routes, route_gain, experts):
    named = routes[:, :, None] == jnp.arange(experts, dtype=jnp.int32)
    return jnp.where(named, route_gain[:, :, None], 0.0).sum(axis=1)


def ring_order(chips):
    return list(range(0, chips, 2)) + list(reversed(range(1, chips, 2)))


def swap_cores(value):
    return lax.ppermute(value, "ep", [(i, i ^ 1) for i in range(lax.axis_size("ep"))])


def pair_gather(value):
    pairs = [[i, i + 1] for i in range(0, lax.axis_size("ep"), 2)]
    return lax.all_gather(value, "ep", axis_index_groups=pairs, axis=0, tiled=True)


def gain_header(gains, width):
    parts, left = [], gains.T
    for _ in range(3):
        part = lax.reduce_precision(left, exponent_bits=8, mantissa_bits=7)
        parts.append(part)
        left = left - part
    rows = jnp.stack(parts, axis=1).reshape(3 * gains.shape[1], gains.shape[0])
    pad = (-rows.shape[0]) % 16
    return jnp.pad(rows, ((0, pad), (0, width - rows.shape[1]))).astype(jnp.bfloat16)


def ring_shift(value, ring, step):
    chips = len(ring)
    pairs = [
        (2 * ring[i] + core, 2 * ring[(i + step) % chips] + core)
        for i in range(chips)
        for core in range(2)
    ]
    return lax.ppermute(value, "ep", pairs)


VMEM_BYTES = 32 * 1024 * 1024
COST_SCALE = 3


def whole(shape):
    return pl.BlockSpec(shape, lambda i, where: (0,) * len(shape))


def accumulate(where, positions, parts, norm_gain, weights, carried, headers):
    count = len(positions)
    width = parts[0][0].shape[1]
    chips = norm_gain.shape[0]
    model_width = chips * width
    hidden_here = weights[0].shape[1]
    both = 2 * hidden_here
    head = parts[0][0].shape[0] - parts[0][1].shape[0]
    sizes = [piece.shape[0] - (head if k == 0 else 0) for k, piece in enumerate(parts[0])]
    starts = [sum(sizes[:k]) for k in range(len(sizes))]
    offsets = [head if k == 0 else 0 for k in range(len(sizes))]
    tokens = sum(sizes)
    tok_here = tokens // chips
    side = 128
    last = headers is not None
    first = carried is None

    def kernel(where_ref, *refs):
        refs = list(refs)
        xs = [[refs.pop(0) for _ in sizes] for _ in range(count)]
        scales = [refs.pop(0) for _ in range(count)]
        stored = [refs.pop(0) for _ in weights]
        acc_in, sq_in = (None, None) if first else (refs.pop(0), refs.pop(0))
        tops = [refs.pop(0) for _ in headers] if last else []
        owns = [refs.pop(0) for _ in range(count)]
        if last:
            hidden_ref = refs.pop(0)
        else:
            acc_out, sq_out, done_ref = refs.pop(0), refs.pop(0), refs.pop(0)
            done_ref[0] = 0
        table_ref, sems = refs.pop(0), refs.pop(0)
        gain_ref = refs.pop(0) if last else None
        copies = {}
        for core in range(2):
            for which in range(2):
                for b in range(count):
                    row = (core * chips + where_ref[positions[b]]) * width
                    slot = (core * 2 + which) * count + b
                    copies[core, which, b] = pltpu.make_async_copy(
                        stored[which].at[pl.ds(pl.multiple_of(row, width), width), :],
                        table_ref.at[slot],
                        sems.at[slot],
                    )
                    copies[core, which, b].start()
        begin = where_ref[0] * tok_here
        for b in range(count):
            for k, size in enumerate(sizes):

                @pl.when((begin >= starts[k]) & (begin < starts[k] + size))
                def _():
                    row = pl.multiple_of(begin - starts[k] + offsets[k], 16)
                    owns[b][...] = xs[b][k][pl.ds(row, tok_here), :]

        if last:
            expert = where_ref[chips]
            row_at = lax.broadcasted_iota(jnp.int32, (head, tok_here), 0)
            diagonal = lax.broadcasted_iota(
                jnp.int32, (tok_here, tok_here), 0
            ) == lax.broadcasted_iota(jnp.int32, (tok_here, tok_here), 1)
            for d in range(chips):
                parts_of = tops[d][:, :tok_here].astype(jnp.float32)
                named = (row_at >= 3 * expert) & (row_at < 3 * expert + 3)
                along = jnp.sum(jnp.where(named, parts_of, 0.0), axis=0, keepdims=True)
                down_rows = jnp.sum(jnp.where(diagonal, along, 0.0), axis=1, keepdims=True)
                at = pl.multiple_of(where_ref[d] * tok_here, tok_here)
                gain_ref[pl.ds(at, tok_here), :] = down_rows

        for k, size in enumerate(sizes):
            span = slice(starts[k], starts[k] + size)
            scaled, squares = [], None if first else sq_in[span, :]
            for b in range(count):
                values = xs[b][k][offsets[k] : offsets[k] + size, :].astype(jnp.float32)
                for lane in range(0, width, side):
                    piece = values[:, lane : lane + side]
                    squares = piece * piece if squares is None else squares + piece * piece
                scaled.append((values * scales[b][0]).astype(jnp.bfloat16))
            if last:
                mean = jnp.sum(squares, axis=1, keepdims=True) / model_width
                inv_rms = lax.rsqrt(mean + epsilon)
            else:
                sq_out[span, :] = squares
            for core in range(2):
                acts = []
                for which in range(2):
                    at = core * both + which * hidden_here
                    cols = slice(at, at + hidden_here)
                    total = None if first else acc_in[span, cols]
                    for b in range(count):
                        if k == 0:
                            copies[core, which, b].wait()
                        product = jnp.dot(
                            scaled[b],
                            table_ref[(core * 2 + which) * count + b],
                            preferred_element_type=jnp.float32,
                        )
                        total = product if total is None else total + product
                    if last:
                        acts.append(total * inv_rms)
                    else:
                        acc_out[span, cols] = total
                if last:
                    act = acts[0] * jax.nn.sigmoid(acts[0]) * acts[1] * gain_ref[span, :]
                    cols = slice(core * hidden_here, (core + 1) * hidden_here)
                    hidden_ref[span, cols] = act.astype(jnp.bfloat16)

    operands = [piece for block in parts for piece in block]
    in_specs = [whole(piece.shape) for piece in operands]
    for position in positions:
        operands.append(norm_gain)
        in_specs.append(
            pl.BlockSpec((1, 1, width), lambda i, where, p=position: (where[p], 0, 0))
        )
    operands.extend(weights)
    in_specs.extend([pl.BlockSpec(memory_space=pltpu.HBM)] * len(weights))
    sums, squared = (tokens, 2 * both), (tokens, side)
    aliases = {}
    if not first:
        if not last:
            aliases = {len(operands) + 1: count, len(operands) + 2: count + 1}
        operands.extend(carried[:2])
        in_specs.extend([whole(sums), whole(squared)])
    out_shape = [jax.ShapeDtypeStruct((tok_here, width), jnp.bfloat16)] * count
    out_specs = [whole((tok_here, width))] * count
    if last:
        operands.extend(headers)
        in_specs.extend([whole((head, width))] * len(headers))
        out_shape.append(jax.ShapeDtypeStruct((tokens, both), jnp.bfloat16))
        out_specs.append(whole((tokens, both)))
    else:
        out_shape.append(jax.ShapeDtypeStruct(sums, jnp.float32))
        out_shape.append(jax.ShapeDtypeStruct(squared, jnp.float32))
        out_shape.append(jax.ShapeDtypeStruct((1,), jnp.int32))
        out_specs.extend([whole(sums), whole(squared), pl.BlockSpec(memory_space=pltpu.SMEM)])
    slots = 4 * count
    scratch = [
        pltpu.VMEM((slots, width, hidden_here), jnp.bfloat16),
        pltpu.SemaphoreType.DMA((slots,)),
    ]
    if last:
        scratch.append(pltpu.VMEM((tokens, 1), jnp.float32))
    made = pl.pallas_call(
        kernel,
        grid_spec=pltpu.PrefetchScalarGridSpec(
            num_scalar_prefetch=1,
            grid=(1,),
            in_specs=in_specs,
            out_specs=out_specs,
            scratch_shapes=scratch,
        ),
        out_shape=out_shape,
        input_output_aliases=aliases,
        compiler_params=pltpu.CompilerParams(vmem_limit_bytes=VMEM_BYTES),
        cost_estimate=pl.CostEstimate(
            flops=COST_SCALE * 2 * count * tokens * width * sums[1],
            bytes_accessed=count * width * (tokens + sums[1]) * 2 + tokens * sums[1] * 8,
            transcendentals=0,
        ),
    )(where, *operands)
    return made[:count], made[count:]


def farthest_rows(where, position, hidden, down):
    tokens, units = hidden.shape
    half = down.shape[1] // 2
    rows = tokens // (where.shape[0] - 1)
    steps = 4

    def kernel(where_ref, hidden_ref, lower_ref, upper_ref, kept_ref, *outs):
        at = pl.multiple_of(where_ref[position] * rows, rows)
        kept_ref[...] = hidden_ref[...]
        for table_ref, out_ref in zip((lower_ref, upper_ref), outs):
            out = jnp.dot(
                hidden_ref[pl.ds(at, rows), :], table_ref[...], preferred_element_type=jnp.float32
            )
            out_ref[...] = out.astype(jnp.bfloat16)

    made = pl.BlockSpec((rows, half // steps), lambda i, where: (0, i))
    return pl.pallas_call(
        kernel,
        grid_spec=pltpu.PrefetchScalarGridSpec(
            num_scalar_prefetch=1,
            grid=(steps,),
            in_specs=[
                whole((tokens, units)),
                pl.BlockSpec((units, half // steps), lambda i, where: (0, i)),
                pl.BlockSpec((units, half // steps), lambda i, where: (0, steps + i)),
            ],
            out_specs=[whole((tokens, units)), made, made],
        ),
        out_shape=[
            jax.ShapeDtypeStruct(hidden.shape, hidden.dtype),
            jax.ShapeDtypeStruct((rows, half), jnp.bfloat16),
            jax.ShapeDtypeStruct((rows, half), jnp.bfloat16),
        ],
        compiler_params=pltpu.CompilerParams(vmem_limit_bytes=VMEM_BYTES),
        cost_estimate=pl.CostEstimate(
            flops=4 * rows * units * half, bytes_accessed=4 * units * half, transcendentals=0
        ),
    )(where, hidden, down, down)


def add_rows(where, position, table, moved):
    rows, width = moved.shape
    steps = 2

    def kernel(where_ref, table_ref, moved_ref, out_ref):
        total = table_ref[...].astype(jnp.float32) + moved_ref[...].astype(jnp.float32)
        out_ref[...] = total.astype(jnp.bfloat16)

    here = pl.BlockSpec((rows, width // steps), lambda i, where: (0, i))
    return pl.pallas_call(
        kernel,
        grid_spec=pltpu.PrefetchScalarGridSpec(
            num_scalar_prefetch=1,
            grid=(steps,),
            in_specs=[
                pl.BlockSpec((rows, width // steps), lambda i, where: (where[position], i)),
                here,
            ],
            out_specs=here,
        ),
        out_shape=jax.ShapeDtypeStruct((rows, width), jnp.bfloat16),
        compiler_params=pltpu.CompilerParams(vmem_limit_bytes=VMEM_BYTES),
        cost_estimate=pl.CostEstimate(
            flops=rows * width, bytes_accessed=rows * width * 6, transcendentals=0
        ),
    )(where, table, moved)


def own_rows(where, positions, pieces, tables):
    rows, width = pieces[0].shape
    chips = len(pieces)
    model_width = chips * width
    half = model_width // 2

    def kernel(where_ref, *refs):
        out_ref = refs[-1]
        for part in range(2):
            out_ref[:, part * half : (part + 1) * half] = refs[chips + part][...].astype(
                jnp.float32
            )
        for k in range(chips):
            start = pl.multiple_of(where_ref[positions[k]] * width, width)
            out_ref[:, pl.ds(start, width)] += refs[k][...].astype(jnp.float32)

    return pl.pallas_call(
        kernel,
        grid_spec=pltpu.PrefetchScalarGridSpec(
            num_scalar_prefetch=1,
            grid=(1,),
            in_specs=[whole((rows, width))] * chips
            + [pl.BlockSpec((rows, half), lambda i, where: (where[0], 0))] * 2,
            out_specs=whole((rows, model_width)),
        ),
        out_shape=jax.ShapeDtypeStruct((rows, model_width), jnp.float32),
        compiler_params=pltpu.CompilerParams(vmem_limit_bytes=VMEM_BYTES),
        cost_estimate=pl.CostEstimate(
            flops=rows * model_width, bytes_accessed=rows * model_width * 8, transcendentals=0
        ),
    )(where, *pieces, *tables)


def final_sum(base, arrived):
    rows, model_width = base.shape
    half = model_width // 2

    def kernel(base_ref, *refs):
        out_ref = refs[-1]
        for part in range(2):
            cols = slice(part * half, (part + 1) * half)
            total = base_ref[:, cols]
            for k in range(len(arrived[part])):
                total = total + refs[k + part * len(arrived[0])][...].astype(jnp.float32)
            out_ref[:, cols] = total.astype(jnp.bfloat16)

    return pl.pallas_call(
        kernel,
        out_shape=jax.ShapeDtypeStruct((rows, model_width), jnp.bfloat16),
        compiler_params=pltpu.CompilerParams(vmem_limit_bytes=VMEM_BYTES),
        cost_estimate=pl.CostEstimate(
            flops=rows * model_width * 3, bytes_accessed=rows * model_width * 10, transcendentals=0
        ),
    )(base, *arrived[0], *arrived[1])


def dense_body(residual, attn_out, norm_gain, expert_routes, route_gain, w_gate, w_up, w_down):
    devices = lax.axis_size("ep")
    experts = devices // FSPLIT
    chips = devices // 2
    far = chips // 2
    tok_here = expert_routes.shape[0]
    feat_here = residual.shape[1]
    model_width = w_gate.shape[0]
    half = model_width // 2
    ring = ring_order(chips)
    me = lax.axis_index("ep")
    chip, core = me // 2, me % 2
    seen = [[ring[(ring.index(i) + d) % chips] for d in range(chips)] for i in range(chips)]
    seen = [row + [2 * i // FSPLIT] for i, row in enumerate(seen)]
    where = lax.dynamic_index_in_dim(jnp.asarray(seen, jnp.int32), chip, 0, keepdims=False)

    stream_feat = (residual.astype(jnp.float32) + attn_out.astype(jnp.float32)).astype(jnp.bfloat16)
    by_core = stream_feat.reshape(chips, 2, tok_here, feat_here)
    mine = lax.dynamic_index_in_dim(by_core, core, 1, keepdims=False)
    theirs = lax.dynamic_index_in_dim(by_core, 1 - core, 1, keepdims=False)
    swapped = swap_cores(theirs)
    block = jnp.concatenate(
        [jnp.where(core == 0, mine, swapped), jnp.where(core == 0, swapped, mine)], axis=2
    )
    block = block.reshape(2, far * tok_here, 2 * feat_here)
    header = gain_header(token_gains(expert_routes, route_gain, experts), 2 * feat_here)
    blocks = {0: [jnp.concatenate([header, block[0]], axis=0), block[1]]}

    swapped, w_gate, w_up, w_down = lax.optimization_barrier((swapped, w_gate, w_up, w_down))
    weights = [
        pltpu.with_memory_space_constraint(pair_gather(table), pltpu.HBM)
        for table in (w_gate, w_up)
    ]
    down = pair_gather(w_down)
    width = 2 * feat_here
    groups = [[0]] + [[d, chips - d] for d in range(1, far)] + [[far]]

    for distance in range(1, far):
        for sign in (-1, 1):
            blocks[sign * distance] = [
                ring_shift(part, ring, -sign) for part in blocks[sign * (distance - 1)]
            ]
    gain_rows = norm_gain.reshape(chips, 1, width)
    carried, owns, positions = None, [], []
    for group in groups:
        if group == [far]:
            headers = [blocks[d if d <= far else d - chips][0] for d in range(chips)]
        parts = [blocks[d if d <= far else d - chips] for d in group]
        made, carried = accumulate(
            where, group, parts, gain_rows, weights, carried, headers if group == [far] else None
        )
        owns.extend(made)
        positions.extend(group)
        if group == groups[max(far - 2, 0)]:
            zero = carried[2][0]
            blocks[far] = []
            for lower, upper in zip(blocks[1 - far], blocks[far - 1]):
                size = far * tok_here // 2
                cut = lower.shape[0] - size
                first = lax.dynamic_slice_in_dim(lower, zero, cut, axis=0)
                second = lax.dynamic_slice_in_dim(upper, cut + zero, size, axis=0)
                blocks[far].append(ring_shift(first, ring, 1))
                blocks[far].append(ring_shift(second, ring, -1))
    hidden = carried[0]

    def contribution(rows, part):
        cols = down[:, part * half : (part + 1) * half]
        return jnp.dot(rows, cols, preferred_element_type=jnp.float32).astype(jnp.bfloat16)

    hidden, lower, upper = farthest_rows(where, far, hidden, down)
    moving = {1: [ring_shift(lower, ring, 1), None], -1: [None, ring_shift(upper, ring, -1)]}
    everything = [contribution(hidden, part) for part in range(2)]
    base = own_rows(where, positions, owns, everything)
    for distance in range(far - 1, 0, -1):
        for sign, order in ((1, (1, 0)), (-1, (0, 1))):
            position = (sign * distance) % chips
            sent = [None, None]
            for part in order:
                if moving[sign][part] is None:
                    value = lax.dynamic_slice_in_dim(
                        everything[part], where[position] * tok_here, tok_here, axis=0
                    )
                else:
                    value = add_rows(where, position, everything[part], moving[sign][part])
                sent[part] = ring_shift(value, ring, sign)
            moving[sign] = sent
    arrived = [
        [moving[sign][part] for sign in (1, -1) if moving[sign][part] is not None]
        for part in range(2)
    ]
    return final_sum(base, arrived)


def body(residual, attn_out, norm_gain, expert_routes, route_gain, w_gate, w_up, w_down):
    tok_here, route_slots = expert_routes.shape
    devices = lax.axis_size("ep")
    capacity = route_slots * tok_here // (devices // FSPLIT)
    dense = capacity >= tok_here and devices % 4 == 0 and devices & (devices - 1) == 0
    chosen = dense_body if dense else routed_body
    return chosen(residual, attn_out, norm_gain, expert_routes, route_gain, w_gate, w_up, w_down)


def solution(mesh):
    in_specs = (
        P("groups", "ep"),
        P("groups", "ep"),
        P(),
        P(("groups", "ep"), None),
        P(("groups", "ep"), None),
        P(None, "ep"),
        P(None, "ep"),
        P("ep", None),
    )
    out_specs = P(("groups", "ep"), None)
    return jax.shard_map(body, mesh=mesh, in_specs=in_specs, out_specs=out_specs, check_vma=False)
```

```python
import jax
import jax.numpy as jnp
from jax import lax
from jax.experimental import pallas as pl
from jax.experimental.pallas import tpu as pltpu
from jax.sharding import PartitionSpec as P

FSPLIT = 8


epsilon = 1e-06


def normalize(stream_rows, norm_gain):
    values = stream_rows.astype(jnp.float32)
    inv_rms = lax.rsqrt(jnp.mean(values * values, axis=-1, keepdims=True) + epsilon)
    return (values * inv_rms * norm_gain).astype(jnp.bfloat16)


def route_match(routes, experts, capacity):
    flat_ids = routes.reshape(-1)
    onehot = (flat_ids[:, None] == jnp.arange(experts, dtype=jnp.int32)[None, :]).astype(jnp.int32)
    earlier = jnp.cumsum(onehot, axis=0) - onehot
    slot_pos = jnp.sum(earlier * onehot, axis=1)
    slot_code = jnp.where(flat_ids < experts, flat_ids * capacity + slot_pos, -1)
    target = jnp.arange(experts * capacity, dtype=jnp.int32)
    return slot_code[None, :] == target[:, None]


def selection(routes, experts, capacity):
    matched = route_match(routes, experts, capacity).astype(jnp.int32)
    return matched.reshape(experts * capacity, routes.shape[0], routes.shape[1]).sum(axis=2)


def gain_table(routes, route_gain, experts, capacity):
    matched = route_match(routes, experts, capacity)
    weighted = jnp.where(matched, route_gain.reshape(-1)[None, :], 0.0)
    return weighted.reshape(experts * capacity, routes.shape[0], routes.shape[1]).sum(axis=2).T


def expert_rows(normed, w_gate, w_up, w_down):
    gate_act = jnp.dot(normed, w_gate, preferred_element_type=jnp.float32)
    up_act = jnp.dot(normed, w_up, preferred_element_type=jnp.float32)
    hidden = (jax.nn.silu(gate_act) * up_act).astype(jnp.bfloat16)
    return jnp.dot(hidden, w_down, preferred_element_type=jnp.float32).astype(jnp.bfloat16)


def routed_body(residual, attn_out, norm_gain, expert_routes, route_gain, w_gate, w_up, w_down):
    devices = lax.axis_size("ep")
    tok_here = expert_routes.shape[0]
    route_slots = expert_routes.shape[1]
    experts = devices // FSPLIT
    capacity = route_slots * tok_here // experts
    model_width = w_gate.shape[0]
    stream_feat = (residual.astype(jnp.float32) + attn_out.astype(jnp.float32)).astype(jnp.bfloat16)
    stream_rows = lax.all_to_all(stream_feat, "ep", split_axis=0, concat_axis=1, tiled=True)
    combine_weights = gain_table(expert_routes, route_gain, experts, capacity)
    normed_rows = normalize(stream_rows, norm_gain)
    select = selection(expert_routes, experts, capacity).astype(jnp.bfloat16)
    per_expert = jnp.dot(select, normed_rows, preferred_element_type=jnp.float32).astype(
        jnp.bfloat16
    )
    per_expert = per_expert.reshape(experts, 1, capacity, model_width)
    outgoing = jnp.broadcast_to(per_expert, (experts, FSPLIT, capacity, model_width))
    outgoing = outgoing.reshape(devices, capacity, model_width)
    received = lax.all_to_all(outgoing, "ep", split_axis=0, concat_axis=0, tiled=True)
    slot_count = received.shape[1]
    partial_value = expert_rows(received.reshape(-1, model_width), w_gate, w_up, w_down)
    partial_value = partial_value.reshape(devices, slot_count, model_width)
    returned = lax.all_to_all(partial_value, "ep", split_axis=0, concat_axis=0, tiled=True)
    summed = (
        returned.reshape(experts, FSPLIT, capacity, model_width).astype(jnp.float32).sum(axis=1)
    )
    summed = summed.reshape(experts * capacity, model_width)
    routed_sum = jnp.dot(combine_weights, summed, precision=lax.Precision.HIGHEST)
    return (stream_rows.astype(jnp.float32) + routed_sum).astype(jnp.bfloat16)


def ring_order(chips):
    return list(range(0, chips, 2)) + list(reversed(range(1, chips, 2)))


def swap_cores(value):
    return lax.ppermute(value, "ep", [(i, i ^ 1) for i in range(lax.axis_size("ep"))])


def pair_gather(value):
    pairs = [[i, i + 1] for i in range(0, lax.axis_size("ep"), 2)]
    both = lax.all_gather(value, "ep", axis_index_groups=pairs, axis=0, tiled=True)
    return pltpu.with_memory_space_constraint(both, pltpu.HBM)


def ring_shift(value, ring, step):
    chips = len(ring)
    pairs = [
        (2 * ring[i] + core, 2 * ring[(i + step) % chips] + core)
        for i in range(chips)
        for core in range(2)
    ]
    return lax.ppermute(value, "ep", pairs)


COST_SCALE = 3
VMEM_BYTES = 32 * 1024 * 1024
IN_VMEM = pl.BlockSpec(memory_space=pltpu.VMEM)
IN_SMEM = pl.BlockSpec(memory_space=pltpu.SMEM)
IN_HBM = pl.BlockSpec(memory_space=pltpu.HBM)


def local_call(
    kernel, out_shape, operands, flops, bytes_accessed, aliases=None, scratch=(), far=()
):
    return pl.pallas_call(
        kernel,
        out_shape=out_shape,
        in_specs=[
            IN_SMEM if k == 0 else IN_HBM if k in far else IN_VMEM for k in range(len(operands))
        ],
        out_specs=jax.tree.map(
            lambda made: IN_SMEM if made.dtype == jnp.int32 else IN_VMEM, out_shape
        ),
        scratch_shapes=list(scratch),
        input_output_aliases=aliases or {},
        compiler_params=pltpu.CompilerParams(vmem_limit_bytes=VMEM_BYTES),
        cost_estimate=pl.CostEstimate(
            flops=flops, bytes_accessed=bytes_accessed, transcendentals=0
        ),
    )(*operands)


def first_blocks(where, stream, swapped, routes, route_gain, experts):
    chips, _, tok_here, feat_here = stream.shape
    width = 2 * feat_here
    rows = chips * tok_here // 2
    head = -(-3 * experts // 16) * 16

    def kernel(where_ref, stream_ref, swapped_ref, routes_ref, gain_ref, *outs):
        core = where_ref[chips + 1]
        for q in range(chips):
            mine = stream_ref[q, core]
            other = swapped_ref[q]
            left = jnp.where(core == 0, mine, other)
            right = jnp.where(core == 0, other, mine)
            out_ref = outs[2 * q // chips]
            at = q * tok_here - (2 * q // chips) * rows + (head if 2 * q < chips else 0)
            out_ref[at : at + tok_here, :] = jnp.concatenate([left, right], axis=1)
        square = (tok_here, tok_here)
        diagonal = lax.broadcasted_iota(jnp.int32, square, 0) == lax.broadcasted_iota(
            jnp.int32, square, 1
        )
        row_at = lax.broadcasted_iota(jnp.int32, (head, tok_here), 0)
        top = jnp.zeros((head, tok_here), jnp.float32)
        for expert in range(experts):
            gains = jnp.where(routes_ref[...] == expert, gain_ref[...], 0.0)
            gains = jnp.sum(gains, axis=1, keepdims=True)
            left = jnp.sum(jnp.where(diagonal, gains, 0.0), axis=0, keepdims=True)
            for part in range(3):
                piece = left.astype(jnp.bfloat16).astype(jnp.float32)
                top = jnp.where(row_at == 3 * expert + part, piece, top)
                left = left - piece
        outs[0][:head, :] = jnp.zeros((head, width), jnp.bfloat16)
        outs[0][:head, :tok_here] = top.astype(jnp.bfloat16)

    return local_call(
        kernel,
        [
            jax.ShapeDtypeStruct((head + rows, width), jnp.bfloat16),
            jax.ShapeDtypeStruct((rows, width), jnp.bfloat16),
        ],
        [where, stream, swapped, routes, route_gain],
        flops=2 * rows * width,
        bytes_accessed=8 * rows * width,
    )


def accumulate(where, positions, parts, norm_gain, tables, carried, headers, fetched=None):
    count = len(positions)
    width = parts[0][0].shape[1]
    chips = norm_gain.shape[0]
    model_width = chips * width
    hidden_here = tables[0].shape[1]
    both = 2 * hidden_here
    rows = parts[0][1].shape[0]
    head = parts[0][0].shape[0] - rows
    tokens = 2 * rows
    tok_here = tokens // chips
    side = 128
    last = headers is not None
    first = carried is None
    slots = 4 * count

    def kernel(where_ref, *refs):
        refs = list(refs)
        xs = [[refs.pop(0) for _ in range(2)] for _ in range(count)]
        scale_ref = refs.pop(0)
        stored = [refs.pop(0), refs.pop(0)]
        acc_in, sq_in = (None, None) if first else (refs.pop(0), refs.pop(0))
        tops = [refs.pop(0) for _ in headers] if last else []
        source_ref = refs.pop(0) if fetched is not None else None
        owns = [refs.pop(0) for _ in range(count)]
        if last:
            hidden_ref = refs.pop(0)
        else:
            acc_out, sq_out, done_ref = refs.pop(0), refs.pop(0), refs.pop(0)
            done_ref[0] = 0
        brought_ref = refs.pop(0) if fetched is not None else None
        table_ref, sems = refs.pop(0), refs.pop(0)
        gain_ref = refs.pop(0) if last else None
        copies = {}
        for core in range(2):
            for which in range(2):
                for b in range(count):
                    row = (core * chips + where_ref[positions[b]]) * width
                    slot = (core * 2 + which) * count + b
                    copies[core, which, b] = pltpu.make_async_copy(
                        stored[which].at[pl.ds(pl.multiple_of(row, width), width), :],
                        table_ref.at[slot],
                        sems.at[slot],
                    )
                    copies[core, which, b].start()
        if fetched is not None:
            bringing = pltpu.make_async_copy(source_ref, brought_ref, sems.at[slots])
            bringing.start()
        begin = where_ref[0] * tok_here
        for b in range(count):
            for k in range(2):

                @pl.when((begin >= k * rows) & (begin < (k + 1) * rows))
                def _():
                    row = begin - k * rows + (head if k == 0 else 0)
                    owns[b][...] = xs[b][k][pl.ds(pl.multiple_of(row, 16), tok_here), :]

        if last:
            expert = where_ref[chips]
            square = (tok_here, tok_here)
            row_at = lax.broadcasted_iota(jnp.int32, (head, tok_here), 0)
            diagonal = lax.broadcasted_iota(jnp.int32, square, 0) == lax.broadcasted_iota(
                jnp.int32, square, 1
            )
            for d in range(chips):
                parts_of = tops[d][:head, :tok_here].astype(jnp.float32)
                named = (row_at >= 3 * expert) & (row_at < 3 * expert + 3)
                along = jnp.sum(jnp.where(named, parts_of, 0.0), axis=0, keepdims=True)
                column = jnp.sum(jnp.where(diagonal, along, 0.0), axis=1, keepdims=True)
                at = pl.multiple_of(where_ref[d] * tok_here, tok_here)
                gain_ref[pl.ds(at, tok_here), :] = column

        scaled, squared = [], []
        for k in range(2):
            span = slice(k * rows, (k + 1) * rows)
            squares = None if first else sq_in[span, :]
            for b in range(count):
                at = head if k == 0 else 0
                values = xs[b][k][at : at + rows, :].astype(jnp.float32)
                for lane in range(0, width, side):
                    piece = values[:, lane : lane + side]
                    squares = piece * piece if squares is None else squares + piece * piece
                scale = scale_ref[where_ref[positions[b]]]
                scaled.append((values * scale).astype(jnp.bfloat16))
            squared.append(squares)
            if not last:
                sq_out[span, :] = squares
        for core in range(2):
            acts = []
            for which in range(2):
                for b in range(count):
                    copies[core, which, b].wait()
                for k in range(2):
                    span = slice(k * rows, (k + 1) * rows)
                    at = core * both + which * hidden_here
                    cols = slice(at, at + hidden_here)
                    total = None if first else acc_in[span, cols]
                    for b in range(count):
                        product = jnp.dot(
                            scaled[k * count + b],
                            table_ref[(core * 2 + which) * count + b],
                            preferred_element_type=jnp.float32,
                        )
                        total = product if total is None else total + product
                    if last:
                        acts.append(total)
                    else:
                        acc_out[span, cols] = total
            if last:
                for k in range(2):
                    span = slice(k * rows, (k + 1) * rows)
                    mean = jnp.sum(squared[k], axis=1, keepdims=True) / model_width
                    inv_rms = lax.rsqrt(mean + epsilon)
                    gate_act, up_act = acts[k] * inv_rms, acts[2 + k] * inv_rms
                    act = gate_act * jax.nn.sigmoid(gate_act) * up_act * gain_ref[span, :]
                    cols = slice(core * hidden_here, (core + 1) * hidden_here)
                    hidden_ref[span, cols] = act.astype(jnp.bfloat16)
        if fetched is not None:
            bringing.wait()

    operands = [where] + [piece for block in parts for piece in block]
    operands.append(norm_gain)
    distant = [len(operands), len(operands) + 1]
    operands.extend(tables)
    aliases = {}
    if not first:
        if not last:
            aliases = {len(operands): count, len(operands) + 1: count + 1}
        operands.extend(carried[:2])
    out_shape = [jax.ShapeDtypeStruct((tok_here, width), jnp.bfloat16)] * count
    if last:
        operands.extend(headers)
        out_shape.append(jax.ShapeDtypeStruct((tokens, both), jnp.bfloat16))
    else:
        out_shape.append(jax.ShapeDtypeStruct((tokens, 2 * both), jnp.float32))
        out_shape.append(jax.ShapeDtypeStruct((tokens, side), jnp.float32))
        out_shape.append(jax.ShapeDtypeStruct((1,), jnp.int32))
    if fetched is not None:
        distant.append(len(operands))
        operands.append(fetched)
        out_shape.append(jax.ShapeDtypeStruct(fetched.shape, fetched.dtype))
    scratch = [
        pltpu.VMEM((slots, width, hidden_here), jnp.bfloat16),
        pltpu.SemaphoreType.DMA((slots + 1,)),
    ]
    if last:
        scratch.append(pltpu.VMEM((tokens, 1), jnp.float32))
    made = local_call(
        kernel,
        out_shape,
        operands,
        flops=COST_SCALE * 4 * count * tokens * width * both,
        bytes_accessed=count * width * (tokens + 2 * both) * 2 + tokens * both * 16,
        aliases=aliases,
        scratch=scratch,
        far=distant,
    )
    return made[:count], made[count:]


def leading_rows(where, wanted, hidden, down, chips):
    tokens, units = hidden.shape
    model_width = down.shape[1]
    half = model_width // 2
    rows = tokens // chips

    def kernel(where_ref, hidden_ref, down_ref, kept_ref, *outs):
        kept_ref[...] = hidden_ref[...]
        for (position, part), out_ref in zip(wanted, outs):
            at = pl.multiple_of(where_ref[position] * rows, rows)
            out = jnp.dot(
                hidden_ref[pl.ds(at, rows), :],
                down_ref[:, part * half : (part + 1) * half],
                preferred_element_type=jnp.float32,
            )
            out_ref[...] = out.astype(jnp.bfloat16)

    return local_call(
        kernel,
        [jax.ShapeDtypeStruct(hidden.shape, hidden.dtype)]
        + [jax.ShapeDtypeStruct((rows, half), jnp.bfloat16)] * len(wanted),
        [where, hidden, down],
        flops=2 * rows * units * half * len(wanted),
        bytes_accessed=2 * units * model_width,
    )


def contribution(where, hidden, down, part):
    tokens, units = hidden.shape
    half = down.shape[1] // 2
    tile = 512 if half % 512 == 0 else half

    def kernel(where_ref, hidden_ref, down_ref, out_ref):
        for start in range(0, half, tile):
            out = jnp.dot(
                hidden_ref[...],
                down_ref[:, part * half + start : part * half + start + tile],
                preferred_element_type=jnp.float32,
            )
            out_ref[:, start : start + tile] = out.astype(jnp.bfloat16)

    return local_call(
        kernel,
        jax.ShapeDtypeStruct((tokens, half), jnp.bfloat16),
        [where, hidden, down],
        flops=2 * tokens * units * half,
        bytes_accessed=2 * half * (units + tokens),
    )


def add_rows(where, position, table, moved):
    rows, width = moved.shape

    def kernel(where_ref, table_ref, moved_ref, out_ref):
        at = pl.multiple_of(where_ref[position] * rows, rows)
        total = table_ref[pl.ds(at, rows), :].astype(jnp.float32)
        out_ref[...] = (total + moved_ref[...].astype(jnp.float32)).astype(jnp.bfloat16)

    return local_call(
        kernel,
        jax.ShapeDtypeStruct((rows, width), jnp.bfloat16),
        [where, table, moved],
        flops=rows * width,
        bytes_accessed=rows * width * 6,
    )


def own_rows(where, positions, pieces, tables):
    rows, width = pieces[0].shape
    chips = len(pieces)
    model_width = chips * width
    half = model_width // 2

    def kernel(where_ref, *refs):
        out_ref = refs[-1]
        at = pl.multiple_of(where_ref[0] * rows, rows)
        for part in range(2):
            out_ref[:, part * half : (part + 1) * half] = refs[chips + part][
                pl.ds(at, rows), :
            ].astype(jnp.float32)
        for k in range(chips):
            start = pl.multiple_of(where_ref[positions[k]] * width, width)
            out_ref[:, pl.ds(start, width)] += refs[k][...].astype(jnp.float32)

    return local_call(
        kernel,
        jax.ShapeDtypeStruct((rows, model_width), jnp.float32),
        [where, *pieces, *tables],
        flops=rows * model_width,
        bytes_accessed=rows * model_width * 8,
    )


def final_sum(where, base, arrived):
    rows, model_width = base.shape
    half = model_width // 2

    def kernel(where_ref, base_ref, *refs):
        out_ref = refs[-1]
        for part in range(2):
            cols = slice(part * half, (part + 1) * half)
            total = base_ref[:, cols]
            for k in range(len(arrived[part])):
                total = total + refs[k + part * len(arrived[0])][...].astype(jnp.float32)
            out_ref[:, cols] = total.astype(jnp.bfloat16)

    return local_call(
        kernel,
        jax.ShapeDtypeStruct((rows, model_width), jnp.bfloat16),
        [where, base, *arrived[0], *arrived[1]],
        flops=rows * model_width * 3,
        bytes_accessed=rows * model_width * 10,
    )


def dense_body(residual, attn_out, norm_gain, expert_routes, route_gain, w_gate, w_up, w_down):
    devices = lax.axis_size("ep")
    experts = devices // FSPLIT
    chips = devices // 2
    far = chips // 2
    tok_here = expert_routes.shape[0]
    feat_here = residual.shape[1]
    model_width = w_gate.shape[0]
    width = 2 * feat_here
    ring = ring_order(chips)
    me = lax.axis_index("ep")
    core = me % 2
    seen = [
        [ring[(ring.index(i // 2) + d) % chips] for d in range(chips)] + [i // FSPLIT, i % 2]
        for i in range(devices)
    ]
    where = lax.dynamic_index_in_dim(jnp.asarray(seen, jnp.int32), me, 0, keepdims=False)

    stream_feat = (residual.astype(jnp.float32) + attn_out.astype(jnp.float32)).astype(jnp.bfloat16)
    by_core = stream_feat.reshape(chips, 2, tok_here, feat_here)
    swapped = swap_cores(lax.dynamic_index_in_dim(by_core, 1 - core, 1, keepdims=False))

    swapped, w_gate, w_up, w_down = lax.optimization_barrier((swapped, w_gate, w_up, w_down))
    tables = [pair_gather(w_gate), pair_gather(w_up)]
    down = pair_gather(w_down)
    blocks = {0: first_blocks(where, by_core, swapped, expert_routes, route_gain, experts)}

    for distance in range(1, far):
        for sign in (-1, 1):
            blocks[sign * distance] = [
                ring_shift(part, ring, -sign) for part in blocks[sign * (distance - 1)]
            ]
    groups = [[0]] + [[d, chips - d] for d in range(1, far)] + [[far]]
    gain_rows = norm_gain.reshape(chips, 1, width)
    carried, owns, positions, headers = None, [], [], None
    for group in groups:
        if group == [far]:
            headers = [blocks[d if d <= far else d - chips][0] for d in range(chips)]
        parts = [blocks[d if d <= far else d - chips] for d in group]
        made, carried = accumulate(
            where,
            group,
            parts,
            gain_rows,
            tables,
            carried,
            headers,
            down if group == groups[-2] else None,
        )
        owns.extend(made)
        positions.extend(group)
        if group == groups[max(far - 3, 0)]:
            lower, upper, *carried = lax.optimization_barrier(
                (blocks[1 - far][0], blocks[far - 1][1], *carried)
            )
            blocks[far] = [ring_shift(lower, ring, 1), ring_shift(upper, ring, -1)]
        if group == groups[-2]:
            down = carried[-1]

    leading = [(far, 0), (far, 1), (far - 1, 1), (chips - far + 1, 0)]
    hidden, lower, upper, after, before = leading_rows(where, leading, carried[0], down, chips)
    moving = {1: [ring_shift(lower, ring, 1), None], -1: [None, ring_shift(upper, ring, -1)]}
    second = {1: ring_shift(after, ring, 1), -1: ring_shift(before, ring, -1)}
    everything = [contribution(where, hidden, down, part) for part in range(2)]
    base = own_rows(where, positions, owns, everything)
    for distance in range(far - 1, 0, -1):
        for sign, order in ((1, (1, 0)), (-1, (0, 1))):
            position = (sign * distance) % chips
            sent = [None, None]
            for part in order:
                if moving[sign][part] is None:
                    sent[part] = second[sign]
                else:
                    value = add_rows(where, position, everything[part], moving[sign][part])
                    sent[part] = ring_shift(value, ring, sign)
            moving[sign] = sent
    arrived = [
        [moving[sign][part] for sign in (1, -1) if moving[sign][part] is not None]
        for part in range(2)
    ]
    return final_sum(where, base, arrived)


def body(residual, attn_out, norm_gain, expert_routes, route_gain, w_gate, w_up, w_down):
    tok_here, route_slots = expert_routes.shape
    devices = lax.axis_size("ep")
    capacity = route_slots * tok_here // (devices // FSPLIT)
    dense = capacity >= tok_here and devices % 8 == 0
    chosen = dense_body if dense else routed_body
    return chosen(residual, attn_out, norm_gain, expert_routes, route_gain, w_gate, w_up, w_down)


def solution(mesh):
    in_specs = (
        P("groups", "ep"),
        P("groups", "ep"),
        P(),
        P(("groups", "ep"), None),
        P(("groups", "ep"), None),
        P(None, "ep"),
        P(None, "ep"),
        P("ep", None),
    )
    out_specs = P(("groups", "ep"), None)
    return jax.shard_map(body, mesh=mesh, in_specs=in_specs, out_specs=out_specs, check_vma=False)
```

```python
import jax
import jax.numpy as jnp
from jax import lax
from jax.experimental import pallas as pl
from jax.experimental.pallas import tpu as pltpu
from jax.sharding import PartitionSpec as P

FSPLIT = 8


epsilon = 1e-06


def normalize(stream_rows, norm_gain):
    values = stream_rows.astype(jnp.float32)
    inv_rms = lax.rsqrt(jnp.mean(values * values, axis=-1, keepdims=True) + epsilon)
    return (values * inv_rms * norm_gain).astype(jnp.bfloat16)


def route_match(routes, experts, capacity):
    flat_ids = routes.reshape(-1)
    onehot = (flat_ids[:, None] == jnp.arange(experts, dtype=jnp.int32)[None, :]).astype(jnp.int32)
    earlier = jnp.cumsum(onehot, axis=0) - onehot
    slot_pos = jnp.sum(earlier * onehot, axis=1)
    slot_code = jnp.where(flat_ids < experts, flat_ids * capacity + slot_pos, -1)
    target = jnp.arange(experts * capacity, dtype=jnp.int32)
    return slot_code[None, :] == target[:, None]


def selection(routes, experts, capacity):
    matched = route_match(routes, experts, capacity).astype(jnp.int32)
    return matched.reshape(experts * capacity, routes.shape[0], routes.shape[1]).sum(axis=2)


def gain_table(routes, route_gain, experts, capacity):
    matched = route_match(routes, experts, capacity)
    weighted = jnp.where(matched, route_gain.reshape(-1)[None, :], 0.0)
    return weighted.reshape(experts * capacity, routes.shape[0], routes.shape[1]).sum(axis=2).T


def expert_rows(normed, w_gate, w_up, w_down):
    gate_act = jnp.dot(normed, w_gate, preferred_element_type=jnp.float32)
    up_act = jnp.dot(normed, w_up, preferred_element_type=jnp.float32)
    hidden = (jax.nn.silu(gate_act) * up_act).astype(jnp.bfloat16)
    return jnp.dot(hidden, w_down, preferred_element_type=jnp.float32).astype(jnp.bfloat16)


def routed_body(residual, attn_out, norm_gain, expert_routes, route_gain, w_gate, w_up, w_down):
    devices = lax.axis_size("ep")
    tok_here = expert_routes.shape[0]
    route_slots = expert_routes.shape[1]
    experts = devices // FSPLIT
    capacity = route_slots * tok_here // experts
    model_width = w_gate.shape[0]
    stream_feat = (residual.astype(jnp.float32) + attn_out.astype(jnp.float32)).astype(jnp.bfloat16)
    stream_rows = lax.all_to_all(stream_feat, "ep", split_axis=0, concat_axis=1, tiled=True)
    combine_weights = gain_table(expert_routes, route_gain, experts, capacity)
    normed_rows = normalize(stream_rows, norm_gain)
    select = selection(expert_routes, experts, capacity).astype(jnp.bfloat16)
    per_expert = jnp.dot(select, normed_rows, preferred_element_type=jnp.float32).astype(
        jnp.bfloat16
    )
    per_expert = per_expert.reshape(experts, 1, capacity, model_width)
    outgoing = jnp.broadcast_to(per_expert, (experts, FSPLIT, capacity, model_width))
    outgoing = outgoing.reshape(devices, capacity, model_width)
    received = lax.all_to_all(outgoing, "ep", split_axis=0, concat_axis=0, tiled=True)
    slot_count = received.shape[1]
    partial_value = expert_rows(received.reshape(-1, model_width), w_gate, w_up, w_down)
    partial_value = partial_value.reshape(devices, slot_count, model_width)
    returned = lax.all_to_all(partial_value, "ep", split_axis=0, concat_axis=0, tiled=True)
    summed = (
        returned.reshape(experts, FSPLIT, capacity, model_width).astype(jnp.float32).sum(axis=1)
    )
    summed = summed.reshape(experts * capacity, model_width)
    routed_sum = jnp.dot(combine_weights, summed, precision=lax.Precision.HIGHEST)
    return (stream_rows.astype(jnp.float32) + routed_sum).astype(jnp.bfloat16)


def ring_order(chips):
    return list(range(0, chips, 2)) + list(reversed(range(1, chips, 2)))


def swap_cores(value):
    return lax.ppermute(value, "ep", [(i, i ^ 1) for i in range(lax.axis_size("ep"))])


def ring_shift(value, ring, step):
    chips = len(ring)
    pairs = [
        (2 * ring[i] + core, 2 * ring[(i + step) % chips] + core)
        for i in range(chips)
        for core in range(2)
    ]
    return lax.ppermute(value, "ep", pairs)


COST_SCALE = 3
VMEM_BYTES = 20 * 1024 * 1024
IN_VMEM = pl.BlockSpec(memory_space=pltpu.VMEM)
IN_SMEM = pl.BlockSpec(memory_space=pltpu.SMEM)
IN_HBM = pl.BlockSpec(memory_space=pltpu.HBM)


def local_call(
    kernel, out_shape, operands, flops, bytes_accessed, aliases=None, scratch=(), far=()
):
    return pl.pallas_call(
        kernel,
        out_shape=out_shape,
        in_specs=[
            IN_SMEM if k == 0 else IN_HBM if k in far else IN_VMEM for k in range(len(operands))
        ],
        out_specs=jax.tree.map(
            lambda made: IN_SMEM if made.dtype == jnp.int32 else IN_VMEM, out_shape
        ),
        scratch_shapes=list(scratch),
        input_output_aliases=aliases or {},
        compiler_params=pltpu.CompilerParams(vmem_limit_bytes=VMEM_BYTES),
        cost_estimate=pl.CostEstimate(
            flops=flops, bytes_accessed=bytes_accessed, transcendentals=0
        ),
    )(*operands)


def first_blocks(where, stream, swapped, routes, route_gain, experts):
    chips, _, tok_here, feat_here = stream.shape
    width = 2 * feat_here
    tokens = chips * tok_here
    head = -(-3 * (experts + 1) // 16) * 16

    def kernel(where_ref, stream_ref, swapped_ref, routes_ref, gain_ref, out_ref):
        core = where_ref[chips + 1]
        square = (tok_here, tok_here)
        diagonal = lax.broadcasted_iota(jnp.int32, square, 0) == lax.broadcasted_iota(
            jnp.int32, square, 1
        )

        def along(column):
            return jnp.sum(jnp.where(diagonal, column, 0.0), axis=0, keepdims=True)

        def split(left):
            for _ in range(3):
                piece = left.astype(jnp.bfloat16).astype(jnp.float32)
                left = left - piece
                yield piece

        row_at = lax.broadcasted_iota(jnp.int32, (head, tok_here), 0)
        for q in range(chips):
            mine = stream_ref[q, core]
            other = swapped_ref[q]
            left = jnp.where(core == 0, mine, other)
            right = jnp.where(core == 0, other, mine)
            at = head + q * tok_here
            out_ref[at : at + tok_here, :] = jnp.concatenate([left, right], axis=1)
            left, right = left.astype(jnp.float32), right.astype(jnp.float32)
            squares = jnp.sum(left * left + right * right, axis=1, keepdims=True)
            top = jnp.zeros((head, tok_here), jnp.float32)
            for row, piece in enumerate(split(along(squares))):
                top = jnp.where(row_at == row, piece, top)
            if q == 0:
                for expert in range(experts):
                    gains = jnp.where(routes_ref[...] == expert, gain_ref[...], 0.0)
                    gains = jnp.sum(gains, axis=1, keepdims=True)
                    for row, piece in enumerate(split(along(gains))):
                        top = jnp.where(row_at == 3 * (expert + 1) + row, piece, top)
            out_ref[:head, q * tok_here : (q + 1) * tok_here] = top.astype(jnp.bfloat16)
        if width > tokens:
            out_ref[:head, tokens:] = jnp.zeros((head, width - tokens), jnp.bfloat16)

    return local_call(
        kernel,
        jax.ShapeDtypeStruct((head + tokens, width), jnp.bfloat16),
        [where, stream, swapped, routes, route_gain],
        flops=4 * tokens * width,
        bytes_accessed=4 * tokens * width,
    )


def accumulate(where, positions, parts, norm_gain, tables, tok_here, carried, headers, ahead):
    count = len(positions)
    width = parts[0][0].shape[1]
    chips = norm_gain.shape[0]
    model_width = chips * width
    hidden_here = tables[0].shape[-1]
    both = 2 * hidden_here
    tokens = chips * tok_here
    sizes = [piece.shape[0] for piece in parts[0]]
    head = sum(sizes) - tokens
    offsets = [head] + [0] * (len(sizes) - 1)
    sizes = [size - at for size, at in zip(sizes, offsets)]
    starts = [sum(sizes[:k]) for k in range(len(sizes))]
    last = headers is not None
    first = carried is None
    slots = 0 if last else 4 * count

    def kernel(where_ref, *refs):
        refs = list(refs)
        xs = [[refs.pop(0) for _ in sizes] for _ in range(count)]
        scale_ref = refs.pop(0)
        stored = [refs.pop(0) for _ in tables]
        acc_in = None if first else refs.pop(0)
        tops = [refs.pop(0) for _ in headers] if last else []
        sources = [refs.pop(0) for _ in ahead[1]] if ahead else []
        owns = [refs.pop(0) for _ in range(count)]
        if last:
            hidden_ref = refs.pop(0)
        else:
            acc_out = refs.pop(0)
        if ahead:
            next_ref, down_ref = refs.pop(0), refs.pop(0)
        if last:
            column_ref = refs.pop(0)
        else:
            table_ref, sems = refs.pop(0), refs.pop(0)

        def fetch(which, position, target, sem):
            row = pl.multiple_of(where_ref[position] * width, width)
            copy = pltpu.make_async_copy(stored[which].at[pl.ds(row, width), :], target, sem)
            copy.start()
            return copy

        copies, later = {}, []
        if not last:
            for which in range(4):
                for b in range(count):
                    slot = which * count + b
                    copies[which, b] = fetch(
                        which, positions[b], table_ref.at[slot], sems.at[slot]
                    )
        if ahead:
            for which in range(4):
                later.append(fetch(which, ahead[0], next_ref.at[which], sems.at[slots + which]))
            for k, source in enumerate(sources):
                target = down_ref.at[k * hidden_here : (k + 1) * hidden_here, :]
                copy = pltpu.make_async_copy(source, target, sems.at[slots + 4 + k])
                copy.start()
                later.append(copy)
        begin = where_ref[0] * tok_here
        for b in range(count):
            for k, size in enumerate(sizes):

                @pl.when((begin >= starts[k]) & (begin < starts[k] + size))
                def _():
                    row = begin - starts[k] + offsets[k]
                    owns[b][...] = xs[b][k][pl.ds(pl.multiple_of(row, 16), tok_here), :]

        if last:
            expert = where_ref[chips]
            square = (tok_here, tok_here)
            row_at = lax.broadcasted_iota(jnp.int32, (head, tok_here), 0)
            diagonal = lax.broadcasted_iota(jnp.int32, square, 0) == lax.broadcasted_iota(
                jnp.int32, square, 1
            )

            def column(row, values):
                named = (row_at >= row) & (row_at < row + 3)
                along = jnp.sum(jnp.where(named, values, 0.0), axis=0, keepdims=True)
                return jnp.sum(jnp.where(diagonal, along, 0.0), axis=1, keepdims=True)

            for d in range(chips):
                values = tops[d][:head, :tok_here].astype(jnp.float32)
                at = pl.multiple_of(where_ref[d] * tok_here, tok_here)
                column_ref[pl.ds(at, tok_here), 0:1] = column(3 * (expert + 1), values)
            for q in range(chips):
                span = slice(q * tok_here, (q + 1) * tok_here)
                total = tops[0][:head, span].astype(jnp.float32)
                for d in range(1, chips):
                    total = total + tops[d][:head, span].astype(jnp.float32)
                mean = column(0, total) / model_width
                column_ref[span, 1:2] = lax.rsqrt(mean + epsilon)

        scaled = []
        for k, size in enumerate(sizes):
            for b in range(count):
                values = xs[b][k][offsets[k] : offsets[k] + size, :].astype(jnp.float32)
                scale = scale_ref[where_ref[positions[b]]]
                scaled.append((values * scale).astype(jnp.bfloat16))
        acts = {}
        for which in range(4):
            cols = slice(which * hidden_here, (which + 1) * hidden_here)
            for b in range(count):
                if not last:
                    copies[which, b].wait()
            for k, size in enumerate(sizes):
                span = slice(starts[k], starts[k] + size)
                total = None if first else acc_in[span, cols]
                for b in range(count):
                    if last:
                        table = stored[0][which]
                    else:
                        table = table_ref[which * count + b]
                    product = jnp.dot(
                        scaled[k * count + b], table, preferred_element_type=jnp.float32
                    )
                    total = product if total is None else total + product
                if not last:
                    acc_out[span, cols] = total
                elif which % 2 == 0:
                    acts[k] = total
                else:
                    gain, inv_rms = column_ref[span, 0:1], column_ref[span, 1:2]
                    gate_act, up_act = acts[k] * inv_rms, total * inv_rms
                    act = gate_act * jax.nn.sigmoid(gate_act) * up_act * gain
                    core = which // 2
                    out_cols = slice(core * hidden_here, (core + 1) * hidden_here)
                    hidden_ref[span, out_cols] = act.astype(jnp.bfloat16)
        for copy in later:
            copy.wait()

    operands = [where] + [piece for block in parts for piece in block]
    operands.append(norm_gain)
    distant = [] if last else list(range(len(operands), len(operands) + len(tables)))
    operands.extend(tables)
    aliases = {}
    if not first:
        if not last:
            aliases = {len(operands): count}
        operands.append(carried)
    out_shape = [jax.ShapeDtypeStruct((tok_here, width), jnp.bfloat16)] * count
    if last:
        operands.extend(headers)
        out_shape.append(jax.ShapeDtypeStruct((tokens, both), jnp.bfloat16))
    else:
        out_shape.append(jax.ShapeDtypeStruct((tokens, 2 * both), jnp.float32))
    if ahead:
        for source in ahead[1]:
            distant.append(len(operands))
            operands.append(source)
        out_shape.append(jax.ShapeDtypeStruct((4, width, hidden_here), jnp.bfloat16))
        out_shape.append(jax.ShapeDtypeStruct((both, model_width), jnp.bfloat16))
    if last:
        scratch = [pltpu.VMEM((tokens, 2), jnp.float32)]
    else:
        scratch = [
            pltpu.VMEM((slots, width, hidden_here), jnp.bfloat16),
            pltpu.SemaphoreType.DMA((slots + 6,)),
        ]
    made = local_call(
        kernel,
        out_shape,
        operands,
        flops=COST_SCALE * 4 * count * tokens * width * both,
        bytes_accessed=count * width * (tokens + 2 * both) * 2 + tokens * both * 16,
        aliases=aliases,
        scratch=scratch,
        far=distant,
    )
    return made[:count], made[count:]


def leading_rows(where, wanted, hidden, down, chips):
    tokens, units = hidden.shape
    model_width = down.shape[1]
    half = model_width // 2
    rows = tokens // chips

    def kernel(where_ref, hidden_ref, down_ref, kept_ref, *outs):
        kept_ref[...] = hidden_ref[...]
        for part in range(2):
            chosen = [k for k, (_, at) in enumerate(wanted) if at == part]
            taken = [
                hidden_ref[pl.ds(pl.multiple_of(where_ref[wanted[k][0]] * rows, rows), rows), :]
                for k in chosen
            ]
            out = jnp.dot(
                jnp.concatenate(taken, axis=0),
                down_ref[:, part * half : (part + 1) * half],
                preferred_element_type=jnp.float32,
            ).astype(jnp.bfloat16)
            for at, k in enumerate(chosen):
                outs[k][...] = out[at * rows : (at + 1) * rows, :]

    return local_call(
        kernel,
        [jax.ShapeDtypeStruct(hidden.shape, hidden.dtype)]
        + [jax.ShapeDtypeStruct((rows, half), jnp.bfloat16)] * len(wanted),
        [where, hidden, down],
        flops=2 * rows * units * half * len(wanted),
        bytes_accessed=2 * units * model_width,
    )


def contribution(where, hidden, down, part):
    tokens, units = hidden.shape
    half = down.shape[1] // 2
    tile = 512 if half % 512 == 0 else half

    def kernel(where_ref, hidden_ref, down_ref, out_ref):
        for start in range(0, half, tile):
            out = jnp.dot(
                hidden_ref[...],
                down_ref[:, part * half + start : part * half + start + tile],
                preferred_element_type=jnp.float32,
            )
            out_ref[:, start : start + tile] = out.astype(jnp.bfloat16)

    return local_call(
        kernel,
        jax.ShapeDtypeStruct((tokens, half), jnp.bfloat16),
        [where, hidden, down],
        flops=2 * tokens * units * half,
        bytes_accessed=2 * half * (units + tokens),
    )


def add_rows(where, position, table, moved):
    rows, width = moved.shape

    def kernel(where_ref, table_ref, moved_ref, out_ref):
        at = pl.multiple_of(where_ref[position] * rows, rows)
        total = table_ref[pl.ds(at, rows), :].astype(jnp.float32)
        out_ref[...] = (total + moved_ref[...].astype(jnp.float32)).astype(jnp.bfloat16)

    return local_call(
        kernel,
        jax.ShapeDtypeStruct((rows, width), jnp.bfloat16),
        [where, table, moved],
        flops=rows * width,
        bytes_accessed=rows * width * 6,
    )


def own_rows(where, positions, pieces, tables):
    rows, width = pieces[0].shape
    chips = len(pieces)
    model_width = chips * width
    half = model_width // 2

    def kernel(where_ref, *refs):
        out_ref = refs[-1]
        at = pl.multiple_of(where_ref[0] * rows, rows)
        for part in range(2):
            out_ref[:, part * half : (part + 1) * half] = refs[chips + part][
                pl.ds(at, rows), :
            ].astype(jnp.float32)
        for k in range(chips):
            start = pl.multiple_of(where_ref[positions[k]] * width, width)
            out_ref[:, pl.ds(start, width)] += refs[k][...].astype(jnp.float32)

    return local_call(
        kernel,
        jax.ShapeDtypeStruct((rows, model_width), jnp.float32),
        [where, *pieces, *tables],
        flops=rows * model_width,
        bytes_accessed=rows * model_width * 8,
    )


def final_sum(where, base, arrived):
    rows, model_width = base.shape
    half = model_width // 2

    def kernel(where_ref, base_ref, *refs):
        out_ref = refs[-1]
        for part in range(2):
            cols = slice(part * half, (part + 1) * half)
            total = base_ref[:, cols]
            for k in range(len(arrived[part])):
                total = total + refs[k + part * len(arrived[0])][...].astype(jnp.float32)
            out_ref[:, cols] = total.astype(jnp.bfloat16)

    return local_call(
        kernel,
        jax.ShapeDtypeStruct((rows, model_width), jnp.bfloat16),
        [where, base, *arrived[0], *arrived[1]],
        flops=rows * model_width * 3,
        bytes_accessed=rows * model_width * 10,
    )


def dense_body(residual, attn_out, norm_gain, expert_routes, route_gain, w_gate, w_up, w_down):
    devices = lax.axis_size("ep")
    experts = devices // FSPLIT
    chips = devices // 2
    far = chips // 2
    tok_here = expert_routes.shape[0]
    feat_here = residual.shape[1]
    model_width = w_gate.shape[0]
    width = 2 * feat_here
    ring = ring_order(chips)
    me = lax.axis_index("ep")
    core = me % 2
    seen = [
        [ring[(ring.index(i // 2) + d) % chips] for d in range(chips)] + [i // FSPLIT, i % 2]
        for i in range(devices)
    ]
    where = lax.dynamic_index_in_dim(jnp.asarray(seen, jnp.int32), me, 0, keepdims=False)

    stream_feat = (residual.astype(jnp.float32) + attn_out.astype(jnp.float32)).astype(jnp.bfloat16)
    by_core = stream_feat.reshape(chips, 2, tok_here, feat_here)
    swapped = swap_cores(lax.dynamic_index_in_dim(by_core, 1 - core, 1, keepdims=False))

    swapped, w_gate, w_up = lax.optimization_barrier((swapped, w_gate, w_up))
    tables = [pltpu.with_memory_space_constraint(table, pltpu.HBM) for table in (w_gate, w_up)]
    tables += [swap_cores(w_gate), swap_cores(w_up)]
    blocks = {0: first_blocks(where, by_core, swapped, expert_routes, route_gain, experts)}
    w_down = lax.optimization_barrier((swapped, w_down))[1]
    down = [pltpu.with_memory_space_constraint(w_down, pltpu.HBM), swap_cores(w_down)]

    for distance in range(1, far):
        for sign in (-1, 1):
            blocks[sign * distance] = ring_shift(blocks[sign * (distance - 1)], ring, -sign)
    groups = [[0]] + [[d, chips - d] for d in range(1, far)] + [[far]]
    gain_rows = norm_gain.reshape(chips, 1, width)
    carried, owns, positions, headers, ahead = None, [], [], None, None
    for group in groups:
        parts = [[blocks[d if d <= far else d - chips]] for d in group]
        if group == [far]:
            parts = [blocks[far]]
            headers = [blocks[d if d < far else d - chips] for d in range(chips) if d != far]
            headers.insert(far, blocks[far][0])
        if group == groups[-2]:
            ahead = (far, down)
        made, (carried, *rest) = accumulate(
            where, group, parts, gain_rows, tables, tok_here, carried, headers, ahead
        )
        owns.extend(made)
        positions.extend(group)
        if group == groups[max(far - 3, 0)]:
            lower, upper, carried = lax.optimization_barrier(
                (blocks[1 - far], blocks[far - 1], carried)
            )
            cut = lower.shape[0] - far * tok_here
            blocks[far] = [ring_shift(lower[:cut], ring, 1), ring_shift(upper[cut:], ring, -1)]
        if group == groups[-2]:
            tables, down, ahead = [rest[0]], rest[1], None

    leading = [(far, 0), (far, 1), (far - 1, 1), (chips - far + 1, 0)]
    hidden, lower, upper, after, before = leading_rows(where, leading, carried, down, chips)
    moving = {1: [ring_shift(lower, ring, 1), None], -1: [None, ring_shift(upper, ring, -1)]}
    second = {1: ring_shift(after, ring, 1), -1: ring_shift(before, ring, -1)}
    everything = [contribution(where, hidden, down, part) for part in range(2)]
    base = own_rows(where, positions, owns, everything)
    for distance in range(far - 1, 0, -1):
        for sign, order in ((1, (1, 0)), (-1, (0, 1))):
            position = (sign * distance) % chips
            sent = [None, None]
            for part in order:
                if moving[sign][part] is None:
                    sent[part] = second[sign]
                else:
                    value = add_rows(where, position, everything[part], moving[sign][part])
                    sent[part] = ring_shift(value, ring, sign)
            moving[sign] = sent
    arrived = [
        [moving[sign][part] for sign in (1, -1) if moving[sign][part] is not None]
        for part in range(2)
    ]
    return final_sum(where, base, arrived)


def body(residual, attn_out, norm_gain, expert_routes, route_gain, w_gate, w_up, w_down):
    tok_here, route_slots = expert_routes.shape
    devices = lax.axis_size("ep")
    capacity = route_slots * tok_here // (devices // FSPLIT)
    dense = capacity >= tok_here and devices % 8 == 0
    dense = dense and devices * tok_here <= 4 * residual.shape[1]
    chosen = dense_body if dense else routed_body
    return chosen(residual, attn_out, norm_gain, expert_routes, route_gain, w_gate, w_up, w_down)


def solution(mesh):
    in_specs = (
        P("groups", "ep"),
        P("groups", "ep"),
        P(),
        P(("groups", "ep"), None),
        P(("groups", "ep"), None),
        P(None, "ep"),
        P(None, "ep"),
        P("ep", None),
    )
    out_specs = P(("groups", "ep"), None)
    return jax.shard_map(body, mesh=mesh, in_specs=in_specs, out_specs=out_specs, check_vma=False)
```

```python
import jax
import jax.numpy as jnp
from jax import lax
from jax.experimental import pallas as pl
from jax.experimental.pallas import tpu as pltpu
from jax.sharding import PartitionSpec as P

FSPLIT = 8


epsilon = 1e-06


def normalize(stream_rows, norm_gain):
    values = stream_rows.astype(jnp.float32)
    inv_rms = lax.rsqrt(jnp.mean(values * values, axis=-1, keepdims=True) + epsilon)
    return (values * inv_rms * norm_gain).astype(jnp.bfloat16)


def route_match(routes, experts, capacity):
    flat_ids = routes.reshape(-1)
    onehot = (flat_ids[:, None] == jnp.arange(experts, dtype=jnp.int32)[None, :]).astype(jnp.int32)
    earlier = jnp.cumsum(onehot, axis=0) - onehot
    slot_pos = jnp.sum(earlier * onehot, axis=1)
    slot_code = jnp.where(flat_ids < experts, flat_ids * capacity + slot_pos, -1)
    target = jnp.arange(experts * capacity, dtype=jnp.int32)
    return slot_code[None, :] == target[:, None]


def selection(routes, experts, capacity):
    matched = route_match(routes, experts, capacity).astype(jnp.int32)
    return matched.reshape(experts * capacity, routes.shape[0], routes.shape[1]).sum(axis=2)


def gain_table(routes, route_gain, experts, capacity):
    matched = route_match(routes, experts, capacity)
    weighted = jnp.where(matched, route_gain.reshape(-1)[None, :], 0.0)
    return weighted.reshape(experts * capacity, routes.shape[0], routes.shape[1]).sum(axis=2).T


def expert_rows(normed, w_gate, w_up, w_down):
    gate_act = jnp.dot(normed, w_gate, preferred_element_type=jnp.float32)
    up_act = jnp.dot(normed, w_up, preferred_element_type=jnp.float32)
    hidden = (jax.nn.silu(gate_act) * up_act).astype(jnp.bfloat16)
    return jnp.dot(hidden, w_down, preferred_element_type=jnp.float32).astype(jnp.bfloat16)


def routed_body(residual, attn_out, norm_gain, expert_routes, route_gain, w_gate, w_up, w_down):
    devices = lax.axis_size("ep")
    tok_here = expert_routes.shape[0]
    route_slots = expert_routes.shape[1]
    experts = devices // FSPLIT
    capacity = route_slots * tok_here // experts
    model_width = w_gate.shape[0]
    stream_feat = (residual.astype(jnp.float32) + attn_out.astype(jnp.float32)).astype(jnp.bfloat16)
    stream_rows = lax.all_to_all(stream_feat, "ep", split_axis=0, concat_axis=1, tiled=True)
    combine_weights = gain_table(expert_routes, route_gain, experts, capacity)
    normed_rows = normalize(stream_rows, norm_gain)
    select = selection(expert_routes, experts, capacity).astype(jnp.bfloat16)
    per_expert = jnp.dot(select, normed_rows, preferred_element_type=jnp.float32).astype(
        jnp.bfloat16
    )
    per_expert = per_expert.reshape(experts, 1, capacity, model_width)
    outgoing = jnp.broadcast_to(per_expert, (experts, FSPLIT, capacity, model_width))
    outgoing = outgoing.reshape(devices, capacity, model_width)
    received = lax.all_to_all(outgoing, "ep", split_axis=0, concat_axis=0, tiled=True)
    slot_count = received.shape[1]
    partial_value = expert_rows(received.reshape(-1, model_width), w_gate, w_up, w_down)
    partial_value = partial_value.reshape(devices, slot_count, model_width)
    returned = lax.all_to_all(partial_value, "ep", split_axis=0, concat_axis=0, tiled=True)
    summed = (
        returned.reshape(experts, FSPLIT, capacity, model_width).astype(jnp.float32).sum(axis=1)
    )
    summed = summed.reshape(experts * capacity, model_width)
    routed_sum = jnp.dot(combine_weights, summed, precision=lax.Precision.HIGHEST)
    return (stream_rows.astype(jnp.float32) + routed_sum).astype(jnp.bfloat16)


def ring_order(chips):
    return list(range(0, chips, 2)) + list(reversed(range(1, chips, 2)))


def swap_cores(value):
    return lax.ppermute(value, "ep", [(i, i ^ 1) for i in range(lax.axis_size("ep"))])


def ring_shift(value, ring, step):
    chips = len(ring)
    pairs = [
        (2 * ring[i] + core, 2 * ring[(i + step) % chips] + core)
        for i in range(chips)
        for core in range(2)
    ]
    return lax.ppermute(value, "ep", pairs)


COST_SCALE = 3
VMEM_BYTES = 20 * 1024 * 1024
WIDE_VMEM_BYTES = 60 * 1024 * 1024
IN_VMEM = pl.BlockSpec(memory_space=pltpu.VMEM)
IN_SMEM = pl.BlockSpec(memory_space=pltpu.SMEM)
IN_HBM = pl.BlockSpec(memory_space=pltpu.HBM)


def local_call(
    kernel, out_shape, operands, flops, bytes_accessed, aliases=None, scratch=(), far=(), vmem_bytes=None
):
    return pl.pallas_call(
        kernel,
        out_shape=out_shape,
        in_specs=[
            IN_SMEM if k == 0 else IN_HBM if k in far else IN_VMEM for k in range(len(operands))
        ],
        out_specs=jax.tree.map(
            lambda made: IN_SMEM if made.dtype == jnp.int32 else IN_VMEM, out_shape
        ),
        scratch_shapes=list(scratch),
        input_output_aliases=aliases or {},
        compiler_params=pltpu.CompilerParams(vmem_limit_bytes=vmem_bytes or VMEM_BYTES),
        cost_estimate=pl.CostEstimate(
            flops=flops, bytes_accessed=bytes_accessed, transcendentals=0
        ),
    )(*operands)


def first_blocks(where, stream, swapped, routes, route_gain, experts):
    chips, _, tok_here, feat_here = stream.shape
    width = 2 * feat_here
    tokens = chips * tok_here
    head = -(-3 * (experts + 1) // 16) * 16

    def kernel(where_ref, stream_ref, swapped_ref, routes_ref, gain_ref, out_ref):
        core = where_ref[chips + 1]
        square = (tok_here, tok_here)
        diagonal = lax.broadcasted_iota(jnp.int32, square, 0) == lax.broadcasted_iota(
            jnp.int32, square, 1
        )

        def along(column):
            return jnp.sum(jnp.where(diagonal, column, 0.0), axis=0, keepdims=True)

        def split(left):
            for _ in range(3):
                piece = left.astype(jnp.bfloat16).astype(jnp.float32)
                left = left - piece
                yield piece

        row_at = lax.broadcasted_iota(jnp.int32, (head, tok_here), 0)
        for q in range(chips):
            mine = stream_ref[q, core]
            other = swapped_ref[q]
            left = jnp.where(core == 0, mine, other)
            right = jnp.where(core == 0, other, mine)
            at = head + q * tok_here
            out_ref[at : at + tok_here, :] = jnp.concatenate([left, right], axis=1)
            left, right = left.astype(jnp.float32), right.astype(jnp.float32)
            squares = jnp.sum(left * left + right * right, axis=1, keepdims=True)
            top = jnp.zeros((head, tok_here), jnp.float32)
            for row, piece in enumerate(split(along(squares))):
                top = jnp.where(row_at == row, piece, top)
            if q == 0:
                for expert in range(experts):
                    gains = jnp.where(routes_ref[...] == expert, gain_ref[...], 0.0)
                    gains = jnp.sum(gains, axis=1, keepdims=True)
                    for row, piece in enumerate(split(along(gains))):
                        top = jnp.where(row_at == 3 * (expert + 1) + row, piece, top)
            out_ref[:head, q * tok_here : (q + 1) * tok_here] = top.astype(jnp.bfloat16)
        if width > tokens:
            out_ref[:head, tokens:] = jnp.zeros((head, width - tokens), jnp.bfloat16)

    return local_call(
        kernel,
        jax.ShapeDtypeStruct((head + tokens, width), jnp.bfloat16),
        [where, stream, swapped, routes, route_gain],
        flops=4 * tokens * width,
        bytes_accessed=4 * tokens * width,
    )


def accumulate(where, positions, parts, norm_gain, tables, tok_here, carried, headers, ahead):
    count = len(positions)
    width = parts[0][0].shape[1]
    chips = norm_gain.shape[0]
    model_width = chips * width
    hidden_here = tables[0].shape[-1]
    both = 2 * hidden_here
    tokens = chips * tok_here
    sizes = [piece.shape[0] for piece in parts[0]]
    head = sum(sizes) - tokens
    offsets = [head] + [0] * (len(sizes) - 1)
    sizes = [size - at for size, at in zip(sizes, offsets)]
    starts = [sum(sizes[:k]) for k in range(len(sizes))]
    last = headers is not None
    first = carried is None
    slots = 0 if last else 4 * count

    def kernel(where_ref, *refs):
        refs = list(refs)
        xs = [[refs.pop(0) for _ in sizes] for _ in range(count)]
        scale_ref = refs.pop(0)
        stored = [refs.pop(0) for _ in tables]
        acc_in = None if first else refs.pop(0)
        tops = [refs.pop(0) for _ in headers] if last else []
        sources = [refs.pop(0) for _ in ahead[1]] if ahead else []
        owns = [refs.pop(0) for _ in range(count)]
        if last:
            hidden_ref = refs.pop(0)
        else:
            acc_out = refs.pop(0)
        if ahead:
            next_ref, down_ref = refs.pop(0), refs.pop(0)
        if last:
            column_ref = refs.pop(0)
        else:
            table_ref, sems = refs.pop(0), refs.pop(0)

        def fetch(which, position, target, sem):
            row = pl.multiple_of(where_ref[position] * width, width)
            copy = pltpu.make_async_copy(stored[which].at[pl.ds(row, width), :], target, sem)
            copy.start()
            return copy

        copies, later = {}, []
        if not last:
            for which in range(4):
                for b in range(count):
                    slot = which * count + b
                    copies[which, b] = fetch(
                        which, positions[b], table_ref.at[slot], sems.at[slot]
                    )
        if ahead:
            for which in range(4):
                later.append(fetch(which, ahead[0], next_ref.at[which], sems.at[slots + which]))
            for k, source in enumerate(sources):
                target = down_ref.at[k * hidden_here : (k + 1) * hidden_here, :]
                copy = pltpu.make_async_copy(source, target, sems.at[slots + 4 + k])
                copy.start()
                later.append(copy)
        begin = where_ref[0] * tok_here
        for b in range(count):
            for k, size in enumerate(sizes):

                @pl.when((begin >= starts[k]) & (begin < starts[k] + size))
                def _():
                    row = begin - starts[k] + offsets[k]
                    owns[b][...] = xs[b][k][pl.ds(pl.multiple_of(row, 16), tok_here), :]

        if last:
            expert = where_ref[chips]
            square = (tok_here, tok_here)
            row_at = lax.broadcasted_iota(jnp.int32, (head, tok_here), 0)
            diagonal = lax.broadcasted_iota(jnp.int32, square, 0) == lax.broadcasted_iota(
                jnp.int32, square, 1
            )

            def column(row, values):
                named = (row_at >= row) & (row_at < row + 3)
                along = jnp.sum(jnp.where(named, values, 0.0), axis=0, keepdims=True)
                return jnp.sum(jnp.where(diagonal, along, 0.0), axis=1, keepdims=True)

            for d in range(chips):
                values = tops[d][:head, :tok_here].astype(jnp.float32)
                at = pl.multiple_of(where_ref[d] * tok_here, tok_here)
                column_ref[pl.ds(at, tok_here), 0:1] = column(3 * (expert + 1), values)
            for q in range(chips):
                span = slice(q * tok_here, (q + 1) * tok_here)
                total = tops[0][:head, span].astype(jnp.float32)
                for d in range(1, chips):
                    total = total + tops[d][:head, span].astype(jnp.float32)
                mean = column(0, total) / model_width
                column_ref[span, 1:2] = lax.rsqrt(mean + epsilon)

        scaled = []
        for k, size in enumerate(sizes):
            for b in range(count):
                values = xs[b][k][offsets[k] : offsets[k] + size, :].astype(jnp.float32)
                scale = scale_ref[where_ref[positions[b]]]
                scaled.append((values * scale).astype(jnp.bfloat16))
        acts = {}
        for which in range(4):
            cols = slice(which * hidden_here, (which + 1) * hidden_here)
            for b in range(count):
                if not last:
                    copies[which, b].wait()
            for k, size in enumerate(sizes):
                span = slice(starts[k], starts[k] + size)
                total = None if first else acc_in[span, cols]
                for b in range(count):
                    if last:
                        table = stored[0][which]
                    else:
                        table = table_ref[which * count + b]
                    product = jnp.dot(
                        scaled[k * count + b], table, preferred_element_type=jnp.float32
                    )
                    total = product if total is None else total + product
                if not last:
                    acc_out[span, cols] = total
                elif which % 2 == 0:
                    acts[k] = total
                else:
                    gain, inv_rms = column_ref[span, 0:1], column_ref[span, 1:2]
                    gate_act, up_act = acts[k] * inv_rms, total * inv_rms
                    act = gate_act * jax.nn.sigmoid(gate_act) * up_act * gain
                    core = which // 2
                    out_cols = slice(core * hidden_here, (core + 1) * hidden_here)
                    hidden_ref[span, out_cols] = act.astype(jnp.bfloat16)
        for copy in later:
            copy.wait()

    operands = [where] + [piece for block in parts for piece in block]
    operands.append(norm_gain)
    distant = [] if last else list(range(len(operands), len(operands) + len(tables)))
    operands.extend(tables)
    aliases = {}
    if not first:
        if not last:
            aliases = {len(operands): count}
        operands.append(carried)
    out_shape = [jax.ShapeDtypeStruct((tok_here, width), jnp.bfloat16)] * count
    if last:
        operands.extend(headers)
        out_shape.append(jax.ShapeDtypeStruct((tokens, both), jnp.bfloat16))
    else:
        out_shape.append(jax.ShapeDtypeStruct((tokens, 2 * both), jnp.float32))
    if ahead:
        for source in ahead[1]:
            distant.append(len(operands))
            operands.append(source)
        out_shape.append(jax.ShapeDtypeStruct((4, width, hidden_here), jnp.bfloat16))
        out_shape.append(jax.ShapeDtypeStruct((both, model_width), jnp.bfloat16))
    if last:
        scratch = [pltpu.VMEM((tokens, 2), jnp.float32)]
    else:
        scratch = [
            pltpu.VMEM((slots, width, hidden_here), jnp.bfloat16),
            pltpu.SemaphoreType.DMA((slots + 6,)),
        ]
    made = local_call(
        kernel,
        out_shape,
        operands,
        flops=COST_SCALE * 4 * count * tokens * width * both,
        bytes_accessed=count * width * (tokens + 2 * both) * 2 + tokens * both * 16,
        aliases=aliases,
        scratch=scratch,
        far=distant,
    )
    return made[:count], made[count:]


def leading_rows(where, wanted, hidden, down, chips):
    tokens, units = hidden.shape
    model_width = down.shape[1]
    half = model_width // 2
    rows = tokens // chips

    def kernel(where_ref, hidden_ref, down_ref, kept_ref, *outs):
        kept_ref[...] = hidden_ref[...]
        for part in range(2):
            chosen = [k for k, (_, at) in enumerate(wanted) if at == part]
            taken = [
                hidden_ref[pl.ds(pl.multiple_of(where_ref[wanted[k][0]] * rows, rows), rows), :]
                for k in chosen
            ]
            out = jnp.dot(
                jnp.concatenate(taken, axis=0),
                down_ref[:, part * half : (part + 1) * half],
                preferred_element_type=jnp.float32,
            ).astype(jnp.bfloat16)
            for at, k in enumerate(chosen):
                outs[k][...] = out[at * rows : (at + 1) * rows, :]

    return local_call(
        kernel,
        [jax.ShapeDtypeStruct(hidden.shape, hidden.dtype)]
        + [jax.ShapeDtypeStruct((rows, half), jnp.bfloat16)] * len(wanted),
        [where, hidden, down],
        flops=2 * rows * units * half * len(wanted),
        bytes_accessed=2 * units * model_width,
    )


def contribution(where, hidden, down, part):
    tokens, units = hidden.shape
    half = down.shape[1] // 2
    tile = 512 if half % 512 == 0 else half

    def kernel(where_ref, hidden_ref, down_ref, out_ref):
        for start in range(0, half, tile):
            out = jnp.dot(
                hidden_ref[...],
                down_ref[:, part * half + start : part * half + start + tile],
                preferred_element_type=jnp.float32,
            )
            out_ref[:, start : start + tile] = out.astype(jnp.bfloat16)

    return local_call(
        kernel,
        jax.ShapeDtypeStruct((tokens, half), jnp.bfloat16),
        [where, hidden, down],
        flops=2 * tokens * units * half,
        bytes_accessed=2 * half * (units + tokens),
    )


def add_rows(where, position, table, moved):
    rows, width = moved.shape

    def kernel(where_ref, table_ref, moved_ref, out_ref):
        at = pl.multiple_of(where_ref[position] * rows, rows)
        total = table_ref[pl.ds(at, rows), :].astype(jnp.float32)
        out_ref[...] = (total + moved_ref[...].astype(jnp.float32)).astype(jnp.bfloat16)

    return local_call(
        kernel,
        jax.ShapeDtypeStruct((rows, width), jnp.bfloat16),
        [where, table, moved],
        flops=rows * width,
        bytes_accessed=rows * width * 6,
        vmem_bytes=WIDE_VMEM_BYTES,
    )


def own_rows(where, positions, pieces, tables):
    rows, width = pieces[0].shape
    chips = len(pieces)
    model_width = chips * width
    half = model_width // 2

    def kernel(where_ref, *refs):
        out_ref = refs[-1]
        at = pl.multiple_of(where_ref[0] * rows, rows)
        for part in range(2):
            out_ref[:, part * half : (part + 1) * half] = refs[chips + part][
                pl.ds(at, rows), :
            ].astype(jnp.float32)
        for k in range(chips):
            start = pl.multiple_of(where_ref[positions[k]] * width, width)
            out_ref[:, pl.ds(start, width)] += refs[k][...].astype(jnp.float32)

    return local_call(
        kernel,
        jax.ShapeDtypeStruct((rows, model_width), jnp.float32),
        [where, *pieces, *tables],
        flops=rows * model_width,
        bytes_accessed=rows * model_width * 8,
    )


def final_sum(where, base, arrived):
    rows, model_width = base.shape
    half = model_width // 2

    def kernel(where_ref, base_ref, *refs):
        out_ref = refs[-1]
        for part in range(2):
            cols = slice(part * half, (part + 1) * half)
            total = base_ref[:, cols]
            for k in range(len(arrived[part])):
                total = total + refs[k + part * len(arrived[0])][...].astype(jnp.float32)
            out_ref[:, cols] = total.astype(jnp.bfloat16)

    return local_call(
        kernel,
        jax.ShapeDtypeStruct((rows, model_width), jnp.bfloat16),
        [where, base, *arrived[0], *arrived[1]],
        flops=rows * model_width * 3,
        bytes_accessed=rows * model_width * 10,
    )


def dense_body(residual, attn_out, norm_gain, expert_routes, route_gain, w_gate, w_up, w_down):
    devices = lax.axis_size("ep")
    experts = devices // FSPLIT
    chips = devices // 2
    far = chips // 2
    tok_here = expert_routes.shape[0]
    feat_here = residual.shape[1]
    model_width = w_gate.shape[0]
    width = 2 * feat_here
    ring = ring_order(chips)
    me = lax.axis_index("ep")
    core = me % 2
    seen = [
        [ring[(ring.index(i // 2) + d) % chips] for d in range(chips)] + [i // FSPLIT, i % 2]
        for i in range(devices)
    ]
    where = lax.dynamic_index_in_dim(jnp.asarray(seen, jnp.int32), me, 0, keepdims=False)

    stream_feat = (residual.astype(jnp.float32) + attn_out.astype(jnp.float32)).astype(jnp.bfloat16)
    by_core = stream_feat.reshape(chips, 2, tok_here, feat_here)
    swapped = swap_cores(lax.dynamic_index_in_dim(by_core, 1 - core, 1, keepdims=False))

    swapped, w_gate, w_up = lax.optimization_barrier((swapped, w_gate, w_up))
    tables = [pltpu.with_memory_space_constraint(table, pltpu.HBM) for table in (w_gate, w_up)]
    tables += [swap_cores(w_gate), swap_cores(w_up)]
    blocks = {0: first_blocks(where, by_core, swapped, expert_routes, route_gain, experts)}
    w_down = lax.optimization_barrier((swapped, w_down))[1]
    down = [pltpu.with_memory_space_constraint(w_down, pltpu.HBM), swap_cores(w_down)]

    for distance in range(1, far):
        for sign in (-1, 1):
            blocks[sign * distance] = ring_shift(blocks[sign * (distance - 1)], ring, -sign)
    groups = [[0]] + [[d, chips - d] for d in range(1, far)] + [[far]]
    gain_rows = norm_gain.reshape(chips, 1, width)
    carried, owns, positions, headers, ahead = None, [], [], None, None
    for group in groups:
        parts = [[blocks[d if d <= far else d - chips]] for d in group]
        if group == [far]:
            parts = [blocks[far]]
            headers = [blocks[d if d < far else d - chips] for d in range(chips) if d != far]
            headers.insert(far, blocks[far][0])
        if group == groups[-2]:
            ahead = (far, down)
        made, (carried, *rest) = accumulate(
            where, group, parts, gain_rows, tables, tok_here, carried, headers, ahead
        )
        owns.extend(made)
        positions.extend(group)
        if group == groups[max(far - 2, 0)]:
            lower, upper, carried = lax.optimization_barrier(
                (blocks[1 - far], blocks[far - 1], carried)
            )
            cut = lower.shape[0] - far * tok_here
            blocks[far] = [ring_shift(lower[:cut], ring, 1), ring_shift(upper[cut:], ring, -1)]
        if group == groups[-2]:
            tables, down, ahead = [rest[0]], rest[1], None

    leading = [(far, 0), (far, 1), (far - 1, 1), (chips - far + 1, 0)]
    hidden, lower, upper, after, before = leading_rows(where, leading, carried, down, chips)
    moving = {1: [ring_shift(lower, ring, 1), None], -1: [None, ring_shift(upper, ring, -1)]}
    second = {1: ring_shift(after, ring, 1), -1: ring_shift(before, ring, -1)}
    everything = [contribution(where, hidden, down, part) for part in range(2)]
    base = own_rows(where, positions, owns, everything)
    for distance in range(far - 1, 0, -1):
        for sign, order in ((1, (1, 0)), (-1, (0, 1))):
            position = (sign * distance) % chips
            sent = [None, None]
            for part in order:
                if moving[sign][part] is None:
                    sent[part] = second[sign]
                else:
                    value = add_rows(where, position, everything[part], moving[sign][part])
                    sent[part] = ring_shift(value, ring, sign)
            moving[sign] = sent
    arrived = [
        [moving[sign][part] for sign in (1, -1) if moving[sign][part] is not None]
        for part in range(2)
    ]
    return final_sum(where, base, arrived)


def body(residual, attn_out, norm_gain, expert_routes, route_gain, w_gate, w_up, w_down):
    tok_here, route_slots = expert_routes.shape
    devices = lax.axis_size("ep")
    capacity = route_slots * tok_here // (devices // FSPLIT)
    dense = capacity >= tok_here and devices % 8 == 0
    dense = dense and devices * tok_here <= 4 * residual.shape[1]
    chosen = dense_body if dense else routed_body
    return chosen(residual, attn_out, norm_gain, expert_routes, route_gain, w_gate, w_up, w_down)


def solution(mesh):
    in_specs = (
        P("groups", "ep"),
        P("groups", "ep"),
        P(),
        P(("groups", "ep"), None),
        P(("groups", "ep"), None),
        P(None, "ep"),
        P(None, "ep"),
        P("ep", None),
    )
    out_specs = P(("groups", "ep"), None)
    return jax.shard_map(body, mesh=mesh, in_specs=in_specs, out_specs=out_specs, check_vma=False)
```

```python
import jax
import jax.numpy as jnp
from jax import lax
from jax.experimental import pallas as pl
from jax.experimental.pallas import tpu as pltpu
from jax.sharding import PartitionSpec as P

FSPLIT = 8


epsilon = 1e-06


def normalize(stream_rows, norm_gain):
    values = stream_rows.astype(jnp.float32)
    inv_rms = lax.rsqrt(jnp.mean(values * values, axis=-1, keepdims=True) + epsilon)
    return (values * inv_rms * norm_gain).astype(jnp.bfloat16)


def route_match(routes, experts, capacity):
    flat_ids = routes.reshape(-1)
    onehot = (flat_ids[:, None] == jnp.arange(experts, dtype=jnp.int32)[None, :]).astype(jnp.int32)
    earlier = jnp.cumsum(onehot, axis=0) - onehot
    slot_pos = jnp.sum(earlier * onehot, axis=1)
    slot_code = jnp.where(flat_ids < experts, flat_ids * capacity + slot_pos, -1)
    target = jnp.arange(experts * capacity, dtype=jnp.int32)
    return slot_code[None, :] == target[:, None]


def selection(routes, experts, capacity):
    matched = route_match(routes, experts, capacity).astype(jnp.int32)
    return matched.reshape(experts * capacity, routes.shape[0], routes.shape[1]).sum(axis=2)


def gain_table(routes, route_gain, experts, capacity):
    matched = route_match(routes, experts, capacity)
    weighted = jnp.where(matched, route_gain.reshape(-1)[None, :], 0.0)
    return weighted.reshape(experts * capacity, routes.shape[0], routes.shape[1]).sum(axis=2).T


def expert_rows(normed, w_gate, w_up, w_down):
    gate_act = jnp.dot(normed, w_gate, preferred_element_type=jnp.float32)
    up_act = jnp.dot(normed, w_up, preferred_element_type=jnp.float32)
    hidden = (jax.nn.silu(gate_act) * up_act).astype(jnp.bfloat16)
    return jnp.dot(hidden, w_down, preferred_element_type=jnp.float32).astype(jnp.bfloat16)


def routed_body(residual, attn_out, norm_gain, expert_routes, route_gain, w_gate, w_up, w_down):
    devices = lax.axis_size("ep")
    tok_here = expert_routes.shape[0]
    route_slots = expert_routes.shape[1]
    experts = devices // FSPLIT
    capacity = route_slots * tok_here // experts
    model_width = w_gate.shape[0]
    stream_feat = (residual.astype(jnp.float32) + attn_out.astype(jnp.float32)).astype(jnp.bfloat16)
    stream_rows = lax.all_to_all(stream_feat, "ep", split_axis=0, concat_axis=1, tiled=True)
    combine_weights = gain_table(expert_routes, route_gain, experts, capacity)
    normed_rows = normalize(stream_rows, norm_gain)
    select = selection(expert_routes, experts, capacity).astype(jnp.bfloat16)
    per_expert = jnp.dot(select, normed_rows, preferred_element_type=jnp.float32).astype(
        jnp.bfloat16
    )
    per_expert = per_expert.reshape(experts, 1, capacity, model_width)
    outgoing = jnp.broadcast_to(per_expert, (experts, FSPLIT, capacity, model_width))
    outgoing = outgoing.reshape(devices, capacity, model_width)
    received = lax.all_to_all(outgoing, "ep", split_axis=0, concat_axis=0, tiled=True)
    slot_count = received.shape[1]
    partial_value = expert_rows(received.reshape(-1, model_width), w_gate, w_up, w_down)
    partial_value = partial_value.reshape(devices, slot_count, model_width)
    returned = lax.all_to_all(partial_value, "ep", split_axis=0, concat_axis=0, tiled=True)
    summed = (
        returned.reshape(experts, FSPLIT, capacity, model_width).astype(jnp.float32).sum(axis=1)
    )
    summed = summed.reshape(experts * capacity, model_width)
    routed_sum = jnp.dot(combine_weights, summed, precision=lax.Precision.HIGHEST)
    return (stream_rows.astype(jnp.float32) + routed_sum).astype(jnp.bfloat16)


def ring_order(chips):
    return list(range(0, chips, 2)) + list(reversed(range(1, chips, 2)))


def swap_cores(value):
    return lax.ppermute(value, "ep", [(i, i ^ 1) for i in range(lax.axis_size("ep"))])


def ring_shift(value, ring, step):
    chips = len(ring)
    pairs = [
        (2 * ring[i] + core, 2 * ring[(i + step) % chips] + core)
        for i in range(chips)
        for core in range(2)
    ]
    return lax.ppermute(value, "ep", pairs)


COST_SCALE = 3
VMEM_BYTES = 20 * 1024 * 1024
IN_VMEM = pl.BlockSpec(memory_space=pltpu.VMEM)
IN_SMEM = pl.BlockSpec(memory_space=pltpu.SMEM)
IN_HBM = pl.BlockSpec(memory_space=pltpu.HBM)


def local_call(
    kernel, out_shape, operands, flops, bytes_accessed, aliases=None, scratch=(), far=()
):
    return pl.pallas_call(
        kernel,
        out_shape=out_shape,
        in_specs=[
            IN_SMEM if k == 0 else IN_HBM if k in far else IN_VMEM for k in range(len(operands))
        ],
        out_specs=jax.tree.map(
            lambda made: IN_SMEM if made.dtype == jnp.int32 else IN_VMEM, out_shape
        ),
        scratch_shapes=list(scratch),
        input_output_aliases=aliases or {},
        compiler_params=pltpu.CompilerParams(vmem_limit_bytes=VMEM_BYTES),
        cost_estimate=pl.CostEstimate(
            flops=flops, bytes_accessed=bytes_accessed, transcendentals=0
        ),
    )(*operands)


def first_blocks(where, stream, swapped, routes, route_gain, experts):
    chips, _, tok_here, feat_here = stream.shape
    width = 2 * feat_here
    tokens = chips * tok_here
    head = -(-3 * (experts + 1) // 16) * 16

    def kernel(where_ref, stream_ref, swapped_ref, routes_ref, gain_ref, out_ref):
        core = where_ref[chips + 1]
        square = (tok_here, tok_here)
        diagonal = lax.broadcasted_iota(jnp.int32, square, 0) == lax.broadcasted_iota(
            jnp.int32, square, 1
        )

        def along(column):
            return jnp.sum(jnp.where(diagonal, column, 0.0), axis=0, keepdims=True)

        def split(left):
            for _ in range(3):
                piece = left.astype(jnp.bfloat16).astype(jnp.float32)
                left = left - piece
                yield piece

        row_at = lax.broadcasted_iota(jnp.int32, (head, tok_here), 0)
        for q in range(chips):
            mine = stream_ref[q, core]
            other = swapped_ref[q]
            left = jnp.where(core == 0, mine, other)
            right = jnp.where(core == 0, other, mine)
            at = head + q * tok_here
            out_ref[at : at + tok_here, :] = jnp.concatenate([left, right], axis=1)
            left, right = left.astype(jnp.float32), right.astype(jnp.float32)
            squares = jnp.sum(left * left + right * right, axis=1, keepdims=True)
            top = jnp.zeros((head, tok_here), jnp.float32)
            for row, piece in enumerate(split(along(squares))):
                top = jnp.where(row_at == row, piece, top)
            if q == 0:
                for expert in range(experts):
                    gains = jnp.where(routes_ref[...] == expert, gain_ref[...], 0.0)
                    gains = jnp.sum(gains, axis=1, keepdims=True)
                    for row, piece in enumerate(split(along(gains))):
                        top = jnp.where(row_at == 3 * (expert + 1) + row, piece, top)
            out_ref[:head, q * tok_here : (q + 1) * tok_here] = top.astype(jnp.bfloat16)
        if width > tokens:
            out_ref[:head, tokens:] = jnp.zeros((head, width - tokens), jnp.bfloat16)

    return local_call(
        kernel,
        pltpu.HBM((head + tokens, width), jnp.bfloat16),
        [where, stream, swapped, routes, route_gain],
        flops=4 * tokens * width,
        bytes_accessed=4 * tokens * width,
    )


def accumulate(where, positions, parts, norm_gain, tables, tok_here, carried, headers, ahead):
    count = len(positions)
    width = parts[0][0].shape[1]
    chips = norm_gain.shape[0]
    model_width = chips * width
    hidden_here = tables[0].shape[-1]
    both = 2 * hidden_here
    tokens = chips * tok_here
    sizes = [piece.shape[0] for piece in parts[0]]
    head = sum(sizes) - tokens
    offsets = [head] + [0] * (len(sizes) - 1)
    sizes = [size - at for size, at in zip(sizes, offsets)]
    starts = [sum(sizes[:k]) for k in range(len(sizes))]
    last = headers is not None
    first = carried is None
    slots = 0 if last else 4 * count

    def kernel(where_ref, *refs):
        refs = list(refs)
        xs = [[refs.pop(0) for _ in sizes] for _ in range(count)]
        scale_ref = refs.pop(0)
        stored = [refs.pop(0) for _ in tables]
        acc_in = None if first else refs.pop(0)
        tops = [refs.pop(0) for _ in headers] if last else []
        sources = [refs.pop(0) for _ in ahead[1]] if ahead else []
        owns = [refs.pop(0) for _ in range(count)]
        if last:
            hidden_ref = refs.pop(0)
        else:
            acc_out = refs.pop(0)
        if ahead:
            next_ref, down_ref = refs.pop(0), refs.pop(0)
        if last:
            column_ref = refs.pop(0)
        else:
            table_ref, sems = refs.pop(0), refs.pop(0)

        def fetch(which, position, target, sem):
            row = pl.multiple_of(where_ref[position] * width, width)
            copy = pltpu.make_async_copy(stored[which].at[pl.ds(row, width), :], target, sem)
            copy.start()
            return copy

        copies, later = {}, []
        if not last:
            for which in range(4):
                for b in range(count):
                    slot = which * count + b
                    copies[which, b] = fetch(
                        which, positions[b], table_ref.at[slot], sems.at[slot]
                    )
        if ahead:
            for which in range(4):
                later.append(fetch(which, ahead[0], next_ref.at[which], sems.at[slots + which]))
            for k, source in enumerate(sources):
                target = down_ref.at[k * hidden_here : (k + 1) * hidden_here, :]
                copy = pltpu.make_async_copy(source, target, sems.at[slots + 4 + k])
                copy.start()
                later.append(copy)
        begin = where_ref[0] * tok_here
        for b in range(count):
            for k, size in enumerate(sizes):

                @pl.when((begin >= starts[k]) & (begin < starts[k] + size))
                def _():
                    row = begin - starts[k] + offsets[k]
                    owns[b][...] = xs[b][k][pl.ds(pl.multiple_of(row, 16), tok_here), :]

        if last:
            expert = where_ref[chips]
            square = (tok_here, tok_here)
            row_at = lax.broadcasted_iota(jnp.int32, (head, tok_here), 0)
            diagonal = lax.broadcasted_iota(jnp.int32, square, 0) == lax.broadcasted_iota(
                jnp.int32, square, 1
            )

            def column(row, values):
                named = (row_at >= row) & (row_at < row + 3)
                along = jnp.sum(jnp.where(named, values, 0.0), axis=0, keepdims=True)
                return jnp.sum(jnp.where(diagonal, along, 0.0), axis=1, keepdims=True)

            for d in range(chips):
                values = tops[d][:head, :tok_here].astype(jnp.float32)
                at = pl.multiple_of(where_ref[d] * tok_here, tok_here)
                column_ref[pl.ds(at, tok_here), 0:1] = column(3 * (expert + 1), values)
            for q in range(chips):
                span = slice(q * tok_here, (q + 1) * tok_here)
                total = tops[0][:head, span].astype(jnp.float32)
                for d in range(1, chips):
                    total = total + tops[d][:head, span].astype(jnp.float32)
                mean = column(0, total) / model_width
                column_ref[span, 1:2] = lax.rsqrt(mean + epsilon)

        scaled = []
        for k, size in enumerate(sizes):
            for b in range(count):
                values = xs[b][k][offsets[k] : offsets[k] + size, :].astype(jnp.float32)
                scale = scale_ref[where_ref[positions[b]]]
                scaled.append((values * scale).astype(jnp.bfloat16))
        acts = {}
        for which in range(4):
            cols = slice(which * hidden_here, (which + 1) * hidden_here)
            for b in range(count):
                if not last:
                    copies[which, b].wait()
            for k, size in enumerate(sizes):
                span = slice(starts[k], starts[k] + size)
                total = None if first else acc_in[span, cols]
                for b in range(count):
                    if last:
                        table = stored[0][which]
                    else:
                        table = table_ref[which * count + b]
                    product = jnp.dot(
                        scaled[k * count + b], table, preferred_element_type=jnp.float32
                    )
                    total = product if total is None else total + product
                if not last:
                    acc_out[span, cols] = total
                elif which % 2 == 0:
                    acts[k] = total
                else:
                    gain, inv_rms = column_ref[span, 0:1], column_ref[span, 1:2]
                    gate_act, up_act = acts[k] * inv_rms, total * inv_rms
                    act = gate_act * jax.nn.sigmoid(gate_act) * up_act * gain
                    core = which // 2
                    out_cols = slice(core * hidden_here, (core + 1) * hidden_here)
                    hidden_ref[span, out_cols] = act.astype(jnp.bfloat16)
        for copy in later:
            copy.wait()

    operands = [where] + [piece for block in parts for piece in block]
    operands.append(norm_gain)
    distant = [] if last else list(range(len(operands), len(operands) + len(tables)))
    operands.extend(tables)
    aliases = {}
    if not first:
        if not last:
            aliases = {len(operands): count}
        operands.append(carried)
    out_shape = [jax.ShapeDtypeStruct((tok_here, width), jnp.bfloat16)] * count
    if last:
        operands.extend(headers)
        out_shape.append(jax.ShapeDtypeStruct((tokens, both), jnp.bfloat16))
    else:
        out_shape.append(jax.ShapeDtypeStruct((tokens, 2 * both), jnp.float32))
    if ahead:
        for source in ahead[1]:
            distant.append(len(operands))
            operands.append(source)
        out_shape.append(jax.ShapeDtypeStruct((4, width, hidden_here), jnp.bfloat16))
        out_shape.append(jax.ShapeDtypeStruct((both, model_width), jnp.bfloat16))
    if last:
        scratch = [pltpu.VMEM((tokens, 2), jnp.float32)]
    else:
        scratch = [
            pltpu.VMEM((slots, width, hidden_here), jnp.bfloat16),
            pltpu.SemaphoreType.DMA((slots + 6,)),
        ]
    made = local_call(
        kernel,
        out_shape,
        operands,
        flops=COST_SCALE * 4 * count * tokens * width * both,
        bytes_accessed=count * width * (tokens + 2 * both) * 2 + tokens * both * 16,
        aliases=aliases,
        scratch=scratch,
        far=distant,
    )
    return made[:count], made[count:]


def leading_rows(where, wanted, hidden, down, chips):
    tokens, units = hidden.shape
    model_width = down.shape[1]
    half = model_width // 2
    rows = tokens // chips

    def kernel(where_ref, hidden_ref, down_ref, kept_ref, *outs):
        kept_ref[...] = hidden_ref[...]
        for part in range(2):
            chosen = [k for k, (_, at) in enumerate(wanted) if at == part]
            taken = [
                hidden_ref[pl.ds(pl.multiple_of(where_ref[wanted[k][0]] * rows, rows), rows), :]
                for k in chosen
            ]
            out = jnp.dot(
                jnp.concatenate(taken, axis=0),
                down_ref[:, part * half : (part + 1) * half],
                preferred_element_type=jnp.float32,
            ).astype(jnp.bfloat16)
            for at, k in enumerate(chosen):
                outs[k][...] = out[at * rows : (at + 1) * rows, :]

    return local_call(
        kernel,
        [jax.ShapeDtypeStruct(hidden.shape, hidden.dtype)]
        + [pltpu.HBM((rows, half), jnp.bfloat16)] * len(wanted),
        [where, hidden, down],
        flops=2 * rows * units * half * len(wanted),
        bytes_accessed=2 * units * model_width,
    )


def contribution(where, hidden, down, part):
    tokens, units = hidden.shape
    half = down.shape[1] // 2
    tile = 512 if half % 512 == 0 else half

    def kernel(where_ref, hidden_ref, down_ref, out_ref):
        for start in range(0, half, tile):
            out = jnp.dot(
                hidden_ref[...],
                down_ref[:, part * half + start : part * half + start + tile],
                preferred_element_type=jnp.float32,
            )
            out_ref[:, start : start + tile] = out.astype(jnp.bfloat16)

    return local_call(
        kernel,
        jax.ShapeDtypeStruct((tokens, half), jnp.bfloat16),
        [where, hidden, down],
        flops=2 * tokens * units * half,
        bytes_accessed=2 * half * (units + tokens),
    )


def add_rows(where, position, table, moved):
    rows, width = moved.shape
    steps = 2

    def kernel(where_ref, table_ref, moved_ref, out_ref):
        total = table_ref[...].astype(jnp.float32) + moved_ref[...].astype(jnp.float32)
        out_ref[...] = total.astype(jnp.bfloat16)

    here = pl.BlockSpec((rows, width // steps), lambda i, where: (0, i))
    return pl.pallas_call(
        kernel,
        grid_spec=pltpu.PrefetchScalarGridSpec(
            num_scalar_prefetch=1,
            grid=(steps,),
            in_specs=[
                pl.BlockSpec((rows, width // steps), lambda i, where: (where[position], i)),
                here,
            ],
            out_specs=here,
        ),
        out_shape=pltpu.HBM((rows, width), jnp.bfloat16),
        compiler_params=pltpu.CompilerParams(vmem_limit_bytes=VMEM_BYTES),
        cost_estimate=pl.CostEstimate(
            flops=rows * width, bytes_accessed=rows * width * 6, transcendentals=0
        ),
    )(where, table, moved)


def collect(where, positions, pieces):
    rows, width = pieces[0].shape
    model_width = len(pieces) * width

    def kernel(where_ref, *refs):
        for k, position in enumerate(positions):
            start = pl.multiple_of(where_ref[position] * width, width)
            refs[-1][:, pl.ds(start, width)] = refs[k][...]

    return local_call(
        kernel,
        jax.ShapeDtypeStruct((rows, model_width), jnp.bfloat16),
        [where, *pieces],
        flops=rows * model_width,
        bytes_accessed=rows * model_width * 4,
    )


def final_sum(where, stream, tables, arrived):
    rows, model_width = stream.shape
    half = model_width // 2
    steps = 2
    came = [value for part in arrived for value in part]

    def kernel(where_ref, *refs):
        out_ref = refs[-1]
        for part in range(2):
            total = refs[part][...].astype(jnp.float32) + refs[2 + part][...].astype(jnp.float32)
            for k in range(len(arrived[part])):
                total = total + refs[4 + k + part * len(arrived[0])][...].astype(jnp.float32)
            start = pl.multiple_of(part * half + pl.program_id(0) * (half // steps), 128)
            out_ref[:, pl.ds(start, half // steps)] = total.astype(jnp.bfloat16)

    block = (rows, half // steps)
    here = pl.BlockSpec(block, lambda i, where: (0, i))
    return pl.pallas_call(
        kernel,
        grid_spec=pltpu.PrefetchScalarGridSpec(
            num_scalar_prefetch=1,
            grid=(steps,),
            in_specs=[here, pl.BlockSpec(block, lambda i, where: (0, steps + i))]
            + [pl.BlockSpec(block, lambda i, where: (where[0], i))] * 2
            + [here] * len(came),
            out_specs=pl.BlockSpec((rows, model_width), lambda i, where: (0, 0)),
        ),
        out_shape=jax.ShapeDtypeStruct((rows, model_width), jnp.bfloat16),
        compiler_params=pltpu.CompilerParams(vmem_limit_bytes=VMEM_BYTES),
        cost_estimate=pl.CostEstimate(
            flops=rows * model_width * 3, bytes_accessed=rows * model_width * 10, transcendentals=0
        ),
    )(where, stream, stream, *tables, *came)


def dense_body(residual, attn_out, norm_gain, expert_routes, route_gain, w_gate, w_up, w_down):
    devices = lax.axis_size("ep")
    experts = devices // FSPLIT
    chips = devices // 2
    far = chips // 2
    tok_here = expert_routes.shape[0]
    feat_here = residual.shape[1]
    model_width = w_gate.shape[0]
    width = 2 * feat_here
    ring = ring_order(chips)
    me = lax.axis_index("ep")
    core = me % 2
    seen = [
        [ring[(ring.index(i // 2) + d) % chips] for d in range(chips)] + [i // FSPLIT, i % 2]
        for i in range(devices)
    ]
    where = lax.dynamic_index_in_dim(jnp.asarray(seen, jnp.int32), me, 0, keepdims=False)

    stream_feat = (residual.astype(jnp.float32) + attn_out.astype(jnp.float32)).astype(jnp.bfloat16)
    by_core = stream_feat.reshape(chips, 2, tok_here, feat_here)
    swapped = swap_cores(lax.dynamic_index_in_dim(by_core, 1 - core, 1, keepdims=False))

    swapped, w_gate, w_up = lax.optimization_barrier((swapped, w_gate, w_up))
    tables = [pltpu.with_memory_space_constraint(table, pltpu.HBM) for table in (w_gate, w_up)]
    tables += [swap_cores(w_gate), swap_cores(w_up)]
    blocks = {0: first_blocks(where, by_core, swapped, expert_routes, route_gain, experts)}
    w_down = lax.optimization_barrier((swapped, w_down))[1]
    down = [pltpu.with_memory_space_constraint(w_down, pltpu.HBM), swap_cores(w_down)]

    for distance in range(1, far):
        for sign in (-1, 1):
            blocks[sign * distance] = ring_shift(blocks[sign * (distance - 1)], ring, -sign)
    groups = [[0]] + [[d, chips - d] for d in range(1, far)] + [[far]]
    gain_rows = norm_gain.reshape(chips, 1, width)
    carried, owns, positions, headers, ahead = None, [], [], None, None
    for group in groups:
        parts = [[blocks[d if d <= far else d - chips]] for d in group]
        if group == [far]:
            parts = [blocks[far]]
            headers = [blocks[d if d < far else d - chips] for d in range(chips) if d != far]
            headers.insert(far, blocks[far][0])
        if group == groups[-2]:
            ahead = (far, down)
        made, (carried, *rest) = accumulate(
            where, group, parts, gain_rows, tables, tok_here, carried, headers, ahead
        )
        owns.extend(made)
        positions.extend(group)
        if group == groups[max(far - 2, 0)]:
            lower, upper, carried = lax.optimization_barrier(
                (blocks[1 - far], blocks[far - 1], carried)
            )
            cut = lower.shape[0] - far * tok_here
            blocks[far] = [ring_shift(lower[:cut], ring, 1), ring_shift(upper[cut:], ring, -1)]
        if group == groups[-2]:
            tables, down, ahead = [rest[0]], rest[1], None

    leading = [(far, 0), (far, 1), (far - 1, 1), (chips - far + 1, 0)]
    hidden, lower, upper, after, before = leading_rows(where, leading, carried, down, chips)
    moving = {1: [ring_shift(lower, ring, 1), None], -1: [None, ring_shift(upper, ring, -1)]}
    second = {1: ring_shift(after, ring, 1), -1: ring_shift(before, ring, -1)}
    stream_rows = collect(where, positions, owns)
    stream_rows, hidden = lax.optimization_barrier((stream_rows, hidden))
    everything = [contribution(where, hidden, down, part) for part in range(2)]
    for distance in range(far - 1, 0, -1):
        for sign, order in ((1, (1, 0)), (-1, (0, 1))):
            position = (sign * distance) % chips
            sent = [None, None]
            for part in order:
                if moving[sign][part] is None:
                    sent[part] = second[sign]
                else:
                    value = add_rows(where, position, everything[part], moving[sign][part])
                    sent[part] = ring_shift(value, ring, sign)
            moving[sign] = sent
    arrived = [
        [moving[sign][part] for sign in (1, -1) if moving[sign][part] is not None]
        for part in range(2)
    ]
    return final_sum(where, stream_rows, everything, arrived)


def body(residual, attn_out, norm_gain, expert_routes, route_gain, w_gate, w_up, w_down):
    tok_here, route_slots = expert_routes.shape
    devices = lax.axis_size("ep")
    capacity = route_slots * tok_here // (devices // FSPLIT)
    dense = capacity >= tok_here and devices % 8 == 0
    dense = dense and devices * tok_here <= 4 * residual.shape[1]
    chosen = dense_body if dense else routed_body
    return chosen(residual, attn_out, norm_gain, expert_routes, route_gain, w_gate, w_up, w_down)


def solution(mesh):
    in_specs = (
        P("groups", "ep"),
        P("groups", "ep"),
        P(),
        P(("groups", "ep"), None),
        P(("groups", "ep"), None),
        P(None, "ep"),
        P(None, "ep"),
        P("ep", None),
    )
    out_specs = P(("groups", "ep"), None)
    return jax.shard_map(body, mesh=mesh, in_specs=in_specs, out_specs=out_specs, check_vma=False)
```

```python
import jax
import jax.numpy as jnp
from jax import lax
from jax.experimental import pallas as pl
from jax.experimental.pallas import tpu as pltpu
from jax.sharding import PartitionSpec as P

FSPLIT = 8


epsilon = 1e-06


def normalize(stream_rows, norm_gain):
    values = stream_rows.astype(jnp.float32)
    inv_rms = lax.rsqrt(jnp.mean(values * values, axis=-1, keepdims=True) + epsilon)
    return (values * inv_rms * norm_gain).astype(jnp.bfloat16)


def route_match(routes, experts, capacity):
    flat_ids = routes.reshape(-1)
    onehot = (flat_ids[:, None] == jnp.arange(experts, dtype=jnp.int32)[None, :]).astype(jnp.int32)
    earlier = jnp.cumsum(onehot, axis=0) - onehot
    slot_pos = jnp.sum(earlier * onehot, axis=1)
    slot_code = jnp.where(flat_ids < experts, flat_ids * capacity + slot_pos, -1)
    target = jnp.arange(experts * capacity, dtype=jnp.int32)
    return slot_code[None, :] == target[:, None]


def selection(routes, experts, capacity):
    matched = route_match(routes, experts, capacity).astype(jnp.int32)
    return matched.reshape(experts * capacity, routes.shape[0], routes.shape[1]).sum(axis=2)


def gain_table(routes, route_gain, experts, capacity):
    matched = route_match(routes, experts, capacity)
    weighted = jnp.where(matched, route_gain.reshape(-1)[None, :], 0.0)
    return weighted.reshape(experts * capacity, routes.shape[0], routes.shape[1]).sum(axis=2).T


def expert_rows(normed, w_gate, w_up, w_down):
    gate_act = jnp.dot(normed, w_gate, preferred_element_type=jnp.float32)
    up_act = jnp.dot(normed, w_up, preferred_element_type=jnp.float32)
    hidden = (jax.nn.silu(gate_act) * up_act).astype(jnp.bfloat16)
    return jnp.dot(hidden, w_down, preferred_element_type=jnp.float32).astype(jnp.bfloat16)


def routed_body(residual, attn_out, norm_gain, expert_routes, route_gain, w_gate, w_up, w_down):
    devices = lax.axis_size("ep")
    tok_here = expert_routes.shape[0]
    route_slots = expert_routes.shape[1]
    experts = devices // FSPLIT
    capacity = route_slots * tok_here // experts
    model_width = w_gate.shape[0]
    stream_feat = (residual.astype(jnp.float32) + attn_out.astype(jnp.float32)).astype(jnp.bfloat16)
    stream_rows = lax.all_to_all(stream_feat, "ep", split_axis=0, concat_axis=1, tiled=True)
    combine_weights = gain_table(expert_routes, route_gain, experts, capacity)
    normed_rows = normalize(stream_rows, norm_gain)
    select = selection(expert_routes, experts, capacity).astype(jnp.bfloat16)
    per_expert = jnp.dot(select, normed_rows, preferred_element_type=jnp.float32).astype(
        jnp.bfloat16
    )
    per_expert = per_expert.reshape(experts, 1, capacity, model_width)
    outgoing = jnp.broadcast_to(per_expert, (experts, FSPLIT, capacity, model_width))
    outgoing = outgoing.reshape(devices, capacity, model_width)
    received = lax.all_to_all(outgoing, "ep", split_axis=0, concat_axis=0, tiled=True)
    slot_count = received.shape[1]
    partial_value = expert_rows(received.reshape(-1, model_width), w_gate, w_up, w_down)
    partial_value = partial_value.reshape(devices, slot_count, model_width)
    returned = lax.all_to_all(partial_value, "ep", split_axis=0, concat_axis=0, tiled=True)
    summed = (
        returned.reshape(experts, FSPLIT, capacity, model_width).astype(jnp.float32).sum(axis=1)
    )
    summed = summed.reshape(experts * capacity, model_width)
    routed_sum = jnp.dot(combine_weights, summed, precision=lax.Precision.HIGHEST)
    return (stream_rows.astype(jnp.float32) + routed_sum).astype(jnp.bfloat16)


def ring_order(chips):
    return list(range(0, chips, 2)) + list(reversed(range(1, chips, 2)))


def swap_cores(value):
    return lax.ppermute(value, "ep", [(i, i ^ 1) for i in range(lax.axis_size("ep"))])


def ring_shift(value, ring, step):
    chips = len(ring)
    pairs = [
        (2 * ring[i] + core, 2 * ring[(i + step) % chips] + core)
        for i in range(chips)
        for core in range(2)
    ]
    return lax.ppermute(value, "ep", pairs)


COST_SCALE = 3
VMEM_BYTES = 20 * 1024 * 1024
WIDE_VMEM_BYTES = 121 * 512 * 1024
IN_VMEM = pl.BlockSpec(memory_space=pltpu.VMEM)
IN_SMEM = pl.BlockSpec(memory_space=pltpu.SMEM)
IN_HBM = pl.BlockSpec(memory_space=pltpu.HBM)


def local_call(
    kernel, out_shape, operands, flops, bytes_accessed, aliases=None, scratch=(), far=()
):
    return pl.pallas_call(
        kernel,
        out_shape=out_shape,
        in_specs=[
            IN_SMEM if k == 0 else IN_HBM if k in far else IN_VMEM for k in range(len(operands))
        ],
        out_specs=jax.tree.map(
            lambda made: IN_SMEM if made.dtype == jnp.int32 else IN_VMEM, out_shape
        ),
        scratch_shapes=list(scratch),
        input_output_aliases=aliases or {},
        compiler_params=pltpu.CompilerParams(vmem_limit_bytes=VMEM_BYTES),
        cost_estimate=pl.CostEstimate(
            flops=flops, bytes_accessed=bytes_accessed, transcendentals=0
        ),
    )(*operands)


def first_blocks(where, stream, swapped, routes, route_gain, experts):
    chips, _, tok_here, feat_here = stream.shape
    width = 2 * feat_here
    tokens = chips * tok_here
    head = -(-3 * (experts + 1) // 16) * 16

    def kernel(where_ref, stream_ref, swapped_ref, routes_ref, gain_ref, out_ref):
        core = where_ref[chips + 1]
        square = (tok_here, tok_here)
        diagonal = lax.broadcasted_iota(jnp.int32, square, 0) == lax.broadcasted_iota(
            jnp.int32, square, 1
        )

        def along(column):
            return jnp.sum(jnp.where(diagonal, column, 0.0), axis=0, keepdims=True)

        def split(left):
            for _ in range(3):
                piece = left.astype(jnp.bfloat16).astype(jnp.float32)
                left = left - piece
                yield piece

        row_at = lax.broadcasted_iota(jnp.int32, (head, tok_here), 0)
        for q in range(chips):
            mine = stream_ref[q, core]
            other = swapped_ref[q]
            left = jnp.where(core == 0, mine, other)
            right = jnp.where(core == 0, other, mine)
            at = head + q * tok_here
            out_ref[at : at + tok_here, :] = jnp.concatenate([left, right], axis=1)
            left, right = left.astype(jnp.float32), right.astype(jnp.float32)
            squares = jnp.sum(left * left + right * right, axis=1, keepdims=True)
            top = jnp.zeros((head, tok_here), jnp.float32)
            for row, piece in enumerate(split(along(squares))):
                top = jnp.where(row_at == row, piece, top)
            if q == 0:
                for expert in range(experts):
                    gains = jnp.where(routes_ref[...] == expert, gain_ref[...], 0.0)
                    gains = jnp.sum(gains, axis=1, keepdims=True)
                    for row, piece in enumerate(split(along(gains))):
                        top = jnp.where(row_at == 3 * (expert + 1) + row, piece, top)
            out_ref[:head, q * tok_here : (q + 1) * tok_here] = top.astype(jnp.bfloat16)
        if width > tokens:
            out_ref[:head, tokens:] = jnp.zeros((head, width - tokens), jnp.bfloat16)

    return local_call(
        kernel,
        pltpu.HBM((head + tokens, width), jnp.bfloat16),
        [where, stream, swapped, routes, route_gain],
        flops=4 * tokens * width,
        bytes_accessed=4 * tokens * width,
    )


def accumulate(where, positions, parts, norm_gain, tables, tok_here, carried, headers, ahead):
    count = len(positions)
    width = parts[0][0].shape[1]
    chips = norm_gain.shape[0]
    model_width = chips * width
    hidden_here = tables[0].shape[-1]
    both = 2 * hidden_here
    tokens = chips * tok_here
    sizes = [piece.shape[0] for piece in parts[0]]
    head = sum(sizes) - tokens
    offsets = [head] + [0] * (len(sizes) - 1)
    sizes = [size - at for size, at in zip(sizes, offsets)]
    starts = [sum(sizes[:k]) for k in range(len(sizes))]
    last = headers is not None
    first = carried is None
    slots = 0 if last else 4 * count

    def kernel(where_ref, *refs):
        refs = list(refs)
        xs = [[refs.pop(0) for _ in sizes] for _ in range(count)]
        scale_ref = refs.pop(0)
        stored = [refs.pop(0) for _ in tables]
        acc_in = None if first else refs.pop(0)
        tops = [refs.pop(0) for _ in headers] if last else []
        sources = [refs.pop(0) for _ in ahead[1]] if ahead else []
        owns = [refs.pop(0) for _ in range(count)]
        if last:
            hidden_ref = refs.pop(0)
        else:
            acc_out = refs.pop(0)
        if ahead:
            next_ref, down_ref = refs.pop(0), refs.pop(0)
        if last:
            column_ref = refs.pop(0)
        else:
            table_ref, sems = refs.pop(0), refs.pop(0)

        def fetch(which, position, target, sem):
            row = pl.multiple_of(where_ref[position] * width, width)
            copy = pltpu.make_async_copy(stored[which].at[pl.ds(row, width), :], target, sem)
            copy.start()
            return copy

        copies, later = {}, []
        if not last:
            for which in range(4):
                for b in range(count):
                    slot = which * count + b
                    copies[which, b] = fetch(
                        which, positions[b], table_ref.at[slot], sems.at[slot]
                    )
        if ahead:
            for which in range(4):
                later.append(fetch(which, ahead[0], next_ref.at[which], sems.at[slots + which]))
            for k, source in enumerate(sources):
                target = down_ref.at[k * hidden_here : (k + 1) * hidden_here, :]
                copy = pltpu.make_async_copy(source, target, sems.at[slots + 4 + k])
                copy.start()
                later.append(copy)
        begin = where_ref[0] * tok_here
        for b in range(count):
            for k, size in enumerate(sizes):

                @pl.when((begin >= starts[k]) & (begin < starts[k] + size))
                def _():
                    row = begin - starts[k] + offsets[k]
                    owns[b][...] = xs[b][k][pl.ds(pl.multiple_of(row, 16), tok_here), :]

        if last:
            expert = where_ref[chips]
            square = (tok_here, tok_here)
            row_at = lax.broadcasted_iota(jnp.int32, (head, tok_here), 0)
            diagonal = lax.broadcasted_iota(jnp.int32, square, 0) == lax.broadcasted_iota(
                jnp.int32, square, 1
            )

            def column(row, values):
                named = (row_at >= row) & (row_at < row + 3)
                along = jnp.sum(jnp.where(named, values, 0.0), axis=0, keepdims=True)
                return jnp.sum(jnp.where(diagonal, along, 0.0), axis=1, keepdims=True)

            for d in range(chips):
                values = tops[d][:head, :tok_here].astype(jnp.float32)
                at = pl.multiple_of(where_ref[d] * tok_here, tok_here)
                column_ref[pl.ds(at, tok_here), 0:1] = column(3 * (expert + 1), values)
            for q in range(chips):
                span = slice(q * tok_here, (q + 1) * tok_here)
                total = tops[0][:head, span].astype(jnp.float32)
                for d in range(1, chips):
                    total = total + tops[d][:head, span].astype(jnp.float32)
                mean = column(0, total) / model_width
                column_ref[span, 1:2] = lax.rsqrt(mean + epsilon)

        scaled = []
        for k, size in enumerate(sizes):
            for b in range(count):
                values = xs[b][k][offsets[k] : offsets[k] + size, :].astype(jnp.float32)
                scale = scale_ref[where_ref[positions[b]]]
                scaled.append((values * scale).astype(jnp.bfloat16))
        acts = {}
        for which in range(4):
            cols = slice(which * hidden_here, (which + 1) * hidden_here)
            for b in range(count):
                if not last:
                    copies[which, b].wait()
            for k, size in enumerate(sizes):
                span = slice(starts[k], starts[k] + size)
                total = None if first else acc_in[span, cols]
                for b in range(count):
                    if last:
                        table = stored[0][which]
                    else:
                        table = table_ref[which * count + b]
                    product = jnp.dot(
                        scaled[k * count + b], table, preferred_element_type=jnp.float32
                    )
                    total = product if total is None else total + product
                if not last:
                    acc_out[span, cols] = total
                elif which % 2 == 0:
                    acts[k] = total
                else:
                    gain, inv_rms = column_ref[span, 0:1], column_ref[span, 1:2]
                    gate_act, up_act = acts[k] * inv_rms, total * inv_rms
                    act = gate_act * jax.nn.sigmoid(gate_act) * up_act * gain
                    core = which // 2
                    out_cols = slice(core * hidden_here, (core + 1) * hidden_here)
                    hidden_ref[span, out_cols] = act.astype(jnp.bfloat16)
        for copy in later:
            copy.wait()

    operands = [where] + [piece for block in parts for piece in block]
    operands.append(norm_gain)
    distant = [] if last else list(range(len(operands), len(operands) + len(tables)))
    operands.extend(tables)
    aliases = {}
    if not first:
        if not last:
            aliases = {len(operands): count}
        operands.append(carried)
    out_shape = [jax.ShapeDtypeStruct((tok_here, width), jnp.bfloat16)] * count
    if last:
        operands.extend(headers)
        out_shape.append(jax.ShapeDtypeStruct((tokens, both), jnp.bfloat16))
    else:
        out_shape.append(jax.ShapeDtypeStruct((tokens, 2 * both), jnp.float32))
    if ahead:
        for source in ahead[1]:
            distant.append(len(operands))
            operands.append(source)
        out_shape.append(jax.ShapeDtypeStruct((4, width, hidden_here), jnp.bfloat16))
        out_shape.append(jax.ShapeDtypeStruct((both, model_width), jnp.bfloat16))
    if last:
        scratch = [pltpu.VMEM((tokens, 2), jnp.float32)]
    else:
        scratch = [
            pltpu.VMEM((slots, width, hidden_here), jnp.bfloat16),
            pltpu.SemaphoreType.DMA((slots + 6,)),
        ]
    made = local_call(
        kernel,
        out_shape,
        operands,
        flops=COST_SCALE * 4 * count * tokens * width * both,
        bytes_accessed=count * width * (tokens + 2 * both) * 2 + tokens * both * 16,
        aliases=aliases,
        scratch=scratch,
        far=distant,
    )
    return made[:count], made[count:]


def leading_rows(where, wanted, hidden, down, chips):
    tokens, units = hidden.shape
    model_width = down.shape[1]
    half = model_width // 2
    rows = tokens // chips

    def kernel(where_ref, hidden_ref, down_ref, kept_ref, *outs):
        kept_ref[...] = hidden_ref[...]
        for part in range(2):
            chosen = [k for k, (_, at) in enumerate(wanted) if at == part]
            taken = [
                hidden_ref[pl.ds(pl.multiple_of(where_ref[wanted[k][0]] * rows, rows), rows), :]
                for k in chosen
            ]
            out = jnp.dot(
                jnp.concatenate(taken, axis=0),
                down_ref[:, part * half : (part + 1) * half],
                preferred_element_type=jnp.float32,
            ).astype(jnp.bfloat16)
            for at, k in enumerate(chosen):
                outs[k][...] = out[at * rows : (at + 1) * rows, :]

    return local_call(
        kernel,
        [jax.ShapeDtypeStruct(hidden.shape, hidden.dtype)]
        + [pltpu.HBM((rows, half), jnp.bfloat16)] * len(wanted),
        [where, hidden, down],
        flops=2 * rows * units * half * len(wanted),
        bytes_accessed=2 * units * model_width,
    )


def contribution(hidden, down, part):
    tokens, units = hidden.shape
    half = down.shape[1] // 2
    steps = 7 if half % (7 * 128) == 0 else 1
    tile = half // steps

    def kernel(hidden_ref, down_ref, out_ref):
        out = jnp.dot(hidden_ref[...], down_ref[...], preferred_element_type=jnp.float32)
        out_ref[...] = out.astype(jnp.bfloat16)

    return pl.pallas_call(
        kernel,
        grid=(steps,),
        in_specs=[
            pl.BlockSpec((tokens, units), lambda i: (0, 0)),
            pl.BlockSpec((units, tile), lambda i: (0, part * steps + i)),
        ],
        out_specs=pl.BlockSpec((tokens, tile), lambda i: (0, i)),
        out_shape=pltpu.HBM((tokens, half), jnp.bfloat16),
        compiler_params=pltpu.CompilerParams(vmem_limit_bytes=VMEM_BYTES),
        cost_estimate=pl.CostEstimate(
            flops=2 * tokens * units * half,
            bytes_accessed=2 * half * (units + tokens),
            transcendentals=0,
        ),
    )(hidden, down)


def add_rows(where, position, table, moved):
    rows, width = moved.shape
    steps = 2

    def kernel(where_ref, table_ref, moved_ref, out_ref):
        total = table_ref[...].astype(jnp.float32) + moved_ref[...].astype(jnp.float32)
        out_ref[...] = total.astype(jnp.bfloat16)

    here = pl.BlockSpec((rows, width // steps), lambda i, where: (0, i))
    return pl.pallas_call(
        kernel,
        grid_spec=pltpu.PrefetchScalarGridSpec(
            num_scalar_prefetch=1,
            grid=(steps,),
            in_specs=[
                pl.BlockSpec((rows, width // steps), lambda i, where: (where[position], i)),
                here,
            ],
            out_specs=here,
        ),
        out_shape=pltpu.HBM((rows, width), jnp.bfloat16),
        compiler_params=pltpu.CompilerParams(vmem_limit_bytes=WIDE_VMEM_BYTES),
        cost_estimate=pl.CostEstimate(
            flops=rows * width, bytes_accessed=rows * width * 6, transcendentals=0
        ),
    )(where, table, moved)


def collect(where, positions, pieces):
    rows, width = pieces[0].shape
    model_width = len(pieces) * width

    def kernel(where_ref, *refs):
        for k, position in enumerate(positions):
            start = pl.multiple_of(where_ref[position] * width, width)
            refs[-1][:, pl.ds(start, width)] = refs[k][...]

    return local_call(
        kernel,
        pltpu.HBM((rows, model_width), jnp.bfloat16),
        [where, *pieces],
        flops=rows * model_width,
        bytes_accessed=rows * model_width * 4,
    )


def final_sum(where, stream, tables, arrived):
    rows, model_width = stream.shape
    half = model_width // 2
    steps = 2
    came = [value for part in arrived for value in part]

    def kernel(where_ref, *refs):
        out_ref = refs[-1]
        for part in range(2):
            total = refs[part][...].astype(jnp.float32) + refs[2 + part][...].astype(jnp.float32)
            for k in range(len(arrived[part])):
                total = total + refs[4 + k + part * len(arrived[0])][...].astype(jnp.float32)
            start = pl.multiple_of(part * half + pl.program_id(0) * (half // steps), 128)
            out_ref[:, pl.ds(start, half // steps)] = total.astype(jnp.bfloat16)

    block = (rows, half // steps)
    here = pl.BlockSpec(block, lambda i, where: (0, i))
    return pl.pallas_call(
        kernel,
        grid_spec=pltpu.PrefetchScalarGridSpec(
            num_scalar_prefetch=1,
            grid=(steps,),
            in_specs=[here, pl.BlockSpec(block, lambda i, where: (0, steps + i))]
            + [pl.BlockSpec(block, lambda i, where: (where[0], i))] * 2
            + [here] * len(came),
            out_specs=pl.BlockSpec((rows, model_width), lambda i, where: (0, 0)),
        ),
        out_shape=jax.ShapeDtypeStruct((rows, model_width), jnp.bfloat16),
        compiler_params=pltpu.CompilerParams(vmem_limit_bytes=VMEM_BYTES),
        cost_estimate=pl.CostEstimate(
            flops=rows * model_width * 3, bytes_accessed=rows * model_width * 10, transcendentals=0
        ),
    )(where, stream, stream, *tables, *came)


def dense_body(residual, attn_out, norm_gain, expert_routes, route_gain, w_gate, w_up, w_down):
    devices = lax.axis_size("ep")
    experts = devices // FSPLIT
    chips = devices // 2
    far = chips // 2
    tok_here = expert_routes.shape[0]
    feat_here = residual.shape[1]
    model_width = w_gate.shape[0]
    width = 2 * feat_here
    ring = ring_order(chips)
    me = lax.axis_index("ep")
    core = me % 2
    seen = [
        [ring[(ring.index(i // 2) + d) % chips] for d in range(chips)] + [i // FSPLIT, i % 2]
        for i in range(devices)
    ]
    where = lax.dynamic_index_in_dim(jnp.asarray(seen, jnp.int32), me, 0, keepdims=False)

    stream_feat = (residual.astype(jnp.float32) + attn_out.astype(jnp.float32)).astype(jnp.bfloat16)
    by_core = stream_feat.reshape(chips, 2, tok_here, feat_here)
    swapped = swap_cores(lax.dynamic_index_in_dim(by_core, 1 - core, 1, keepdims=False))

    swapped, w_gate, w_up = lax.optimization_barrier((swapped, w_gate, w_up))
    tables = [pltpu.with_memory_space_constraint(table, pltpu.HBM) for table in (w_gate, w_up)]
    tables += [swap_cores(w_gate), swap_cores(w_up)]
    blocks = {0: first_blocks(where, by_core, swapped, expert_routes, route_gain, experts)}
    w_down = lax.optimization_barrier((swapped, w_down))[1]
    down = [pltpu.with_memory_space_constraint(w_down, pltpu.HBM), swap_cores(w_down)]

    for distance in range(1, far):
        for sign in (-1, 1):
            blocks[sign * distance] = ring_shift(blocks[sign * (distance - 1)], ring, -sign)
    groups = [[0]] + [[d, chips - d] for d in range(1, far)] + [[far]]
    gain_rows = norm_gain.reshape(chips, 1, width)
    carried, owns, positions, headers, ahead = None, [], [], None, None
    for group in groups:
        parts = [[blocks[d if d <= far else d - chips]] for d in group]
        if group == [far]:
            parts = [blocks[far]]
            headers = [blocks[d if d < far else d - chips] for d in range(chips) if d != far]
            headers.insert(far, blocks[far][0])
        if group == groups[-2]:
            ahead = (far, down)
        made, (carried, *rest) = accumulate(
            where, group, parts, gain_rows, tables, tok_here, carried, headers, ahead
        )
        owns.extend(made)
        positions.extend(group)
        if group == groups[max(far - 2, 0)]:
            lower, upper, carried = lax.optimization_barrier(
                (blocks[1 - far], blocks[far - 1], carried)
            )
            cut = lower.shape[0] - far * tok_here
            blocks[far] = [ring_shift(lower[:cut], ring, 1), ring_shift(upper[cut:], ring, -1)]
        if group == groups[-2]:
            tables, down, ahead = [rest[0]], rest[1], None

    leading = [(far, 0), (far, 1), (far - 1, 1), (chips - far + 1, 0)]
    hidden, lower, upper, after, before = leading_rows(where, leading, carried, down, chips)
    moving = {1: [ring_shift(lower, ring, 1), None], -1: [None, ring_shift(upper, ring, -1)]}
    second = {1: ring_shift(after, ring, 1), -1: ring_shift(before, ring, -1)}
    stream_rows = collect(where, positions, owns)
    stream_rows, hidden = lax.optimization_barrier((stream_rows, hidden))
    everything = [contribution(hidden, down, part) for part in range(2)]
    for distance in range(far - 1, 0, -1):
        for sign, order in ((1, (1, 0)), (-1, (0, 1))):
            position = (sign * distance) % chips
            sent = [None, None]
            for part in order:
                if moving[sign][part] is None:
                    sent[part] = second[sign]
                else:
                    value = add_rows(where, position, everything[part], moving[sign][part])
                    sent[part] = ring_shift(value, ring, sign)
            moving[sign] = sent
    arrived = [
        [moving[sign][part] for sign in (1, -1) if moving[sign][part] is not None]
        for part in range(2)
    ]
    return final_sum(where, stream_rows, everything, arrived)


def body(residual, attn_out, norm_gain, expert_routes, route_gain, w_gate, w_up, w_down):
    tok_here, route_slots = expert_routes.shape
    devices = lax.axis_size("ep")
    capacity = route_slots * tok_here // (devices // FSPLIT)
    dense = capacity >= tok_here and devices % 8 == 0
    dense = dense and devices * tok_here <= 4 * residual.shape[1]
    chosen = dense_body if dense else routed_body
    return chosen(residual, attn_out, norm_gain, expert_routes, route_gain, w_gate, w_up, w_down)


def solution(mesh):
    in_specs = (
        P("groups", "ep"),
        P("groups", "ep"),
        P(),
        P(("groups", "ep"), None),
        P(("groups", "ep"), None),
        P(None, "ep"),
        P(None, "ep"),
        P("ep", None),
    )
    out_specs = P(("groups", "ep"), None)
    return jax.shard_map(body, mesh=mesh, in_specs=in_specs, out_specs=out_specs, check_vma=False)
```

```python
import jax
import jax.numpy as jnp
from jax import lax
from jax.experimental import pallas as pl
from jax.experimental.pallas import tpu as pltpu
from jax.sharding import PartitionSpec as P

FSPLIT = 8


epsilon = 1e-06


def normalize(stream_rows, norm_gain):
    values = stream_rows.astype(jnp.float32)
    inv_rms = lax.rsqrt(jnp.mean(values * values, axis=-1, keepdims=True) + epsilon)
    return (values * inv_rms * norm_gain).astype(jnp.bfloat16)


def route_match(routes, experts, capacity):
    flat_ids = routes.reshape(-1)
    onehot = (flat_ids[:, None] == jnp.arange(experts, dtype=jnp.int32)[None, :]).astype(jnp.int32)
    earlier = jnp.cumsum(onehot, axis=0) - onehot
    slot_pos = jnp.sum(earlier * onehot, axis=1)
    slot_code = jnp.where(flat_ids < experts, flat_ids * capacity + slot_pos, -1)
    target = jnp.arange(experts * capacity, dtype=jnp.int32)
    return slot_code[None, :] == target[:, None]


def selection(routes, experts, capacity):
    matched = route_match(routes, experts, capacity).astype(jnp.int32)
    return matched.reshape(experts * capacity, routes.shape[0], routes.shape[1]).sum(axis=2)


def gain_table(routes, route_gain, experts, capacity):
    matched = route_match(routes, experts, capacity)
    weighted = jnp.where(matched, route_gain.reshape(-1)[None, :], 0.0)
    return weighted.reshape(experts * capacity, routes.shape[0], routes.shape[1]).sum(axis=2).T


def expert_rows(normed, w_gate, w_up, w_down):
    gate_act = jnp.dot(normed, w_gate, preferred_element_type=jnp.float32)
    up_act = jnp.dot(normed, w_up, preferred_element_type=jnp.float32)
    hidden = (jax.nn.silu(gate_act) * up_act).astype(jnp.bfloat16)
    return jnp.dot(hidden, w_down, preferred_element_type=jnp.float32).astype(jnp.bfloat16)


def routed_body(residual, attn_out, norm_gain, expert_routes, route_gain, w_gate, w_up, w_down):
    devices = lax.axis_size("ep")
    tok_here = expert_routes.shape[0]
    route_slots = expert_routes.shape[1]
    experts = devices // FSPLIT
    capacity = route_slots * tok_here // experts
    model_width = w_gate.shape[0]
    stream_feat = (residual.astype(jnp.float32) + attn_out.astype(jnp.float32)).astype(jnp.bfloat16)
    stream_rows = lax.all_to_all(stream_feat, "ep", split_axis=0, concat_axis=1, tiled=True)
    combine_weights = gain_table(expert_routes, route_gain, experts, capacity)
    normed_rows = normalize(stream_rows, norm_gain)
    select = selection(expert_routes, experts, capacity).astype(jnp.bfloat16)
    per_expert = jnp.dot(select, normed_rows, preferred_element_type=jnp.float32).astype(
        jnp.bfloat16
    )
    per_expert = per_expert.reshape(experts, 1, capacity, model_width)
    outgoing = jnp.broadcast_to(per_expert, (experts, FSPLIT, capacity, model_width))
    outgoing = outgoing.reshape(devices, capacity, model_width)
    received = lax.all_to_all(outgoing, "ep", split_axis=0, concat_axis=0, tiled=True)
    slot_count = received.shape[1]
    partial_value = expert_rows(received.reshape(-1, model_width), w_gate, w_up, w_down)
    partial_value = partial_value.reshape(devices, slot_count, model_width)
    returned = lax.all_to_all(partial_value, "ep", split_axis=0, concat_axis=0, tiled=True)
    summed = (
        returned.reshape(experts, FSPLIT, capacity, model_width).astype(jnp.float32).sum(axis=1)
    )
    summed = summed.reshape(experts * capacity, model_width)
    routed_sum = jnp.dot(combine_weights, summed, precision=lax.Precision.HIGHEST)
    return (stream_rows.astype(jnp.float32) + routed_sum).astype(jnp.bfloat16)


def ring_order(chips):
    return list(range(0, chips, 2)) + list(reversed(range(1, chips, 2)))


def swap_cores(value):
    return lax.ppermute(value, "ep", [(i, i ^ 1) for i in range(lax.axis_size("ep"))])


def ring_shift(value, ring, step):
    chips = len(ring)
    pairs = [
        (2 * ring[i] + core, 2 * ring[(i + step) % chips] + core)
        for i in range(chips)
        for core in range(2)
    ]
    return lax.ppermute(value, "ep", pairs)


COST_SCALE = 3
VMEM_BYTES = 20 * 1024 * 1024
IN_VMEM = pl.BlockSpec(memory_space=pltpu.VMEM)
IN_SMEM = pl.BlockSpec(memory_space=pltpu.SMEM)
IN_HBM = pl.BlockSpec(memory_space=pltpu.HBM)


def local_call(
    kernel, out_shape, operands, flops, bytes_accessed, aliases=None, scratch=(), far=()
):
    return pl.pallas_call(
        kernel,
        out_shape=out_shape,
        in_specs=[
            IN_SMEM if k == 0 else IN_HBM if k in far else IN_VMEM for k in range(len(operands))
        ],
        out_specs=jax.tree.map(
            lambda made: IN_SMEM if made.dtype == jnp.int32 else IN_VMEM, out_shape
        ),
        scratch_shapes=list(scratch),
        input_output_aliases=aliases or {},
        compiler_params=pltpu.CompilerParams(vmem_limit_bytes=VMEM_BYTES),
        cost_estimate=pl.CostEstimate(
            flops=flops, bytes_accessed=bytes_accessed, transcendentals=0
        ),
    )(*operands)


def first_blocks(where, stream, swapped, routes, route_gain, experts):
    chips, _, tok_here, feat_here = stream.shape
    width = 2 * feat_here
    tokens = chips * tok_here
    head = -(-3 * (experts + 1) // 16) * 16

    def kernel(where_ref, stream_ref, swapped_ref, routes_ref, gain_ref, out_ref):
        core = where_ref[chips + 1]
        square = (tok_here, tok_here)
        diagonal = lax.broadcasted_iota(jnp.int32, square, 0) == lax.broadcasted_iota(
            jnp.int32, square, 1
        )

        def along(column):
            return jnp.sum(jnp.where(diagonal, column, 0.0), axis=0, keepdims=True)

        def split(left):
            for _ in range(3):
                piece = left.astype(jnp.bfloat16).astype(jnp.float32)
                left = left - piece
                yield piece

        row_at = lax.broadcasted_iota(jnp.int32, (head, tok_here), 0)
        for q in range(chips):
            mine = stream_ref[q, core]
            other = swapped_ref[q]
            left = jnp.where(core == 0, mine, other)
            right = jnp.where(core == 0, other, mine)
            at = head + q * tok_here
            out_ref[at : at + tok_here, :] = jnp.concatenate([left, right], axis=1)
            left, right = left.astype(jnp.float32), right.astype(jnp.float32)
            squares = jnp.sum(left * left + right * right, axis=1, keepdims=True)
            top = jnp.zeros((head, tok_here), jnp.float32)
            for row, piece in enumerate(split(along(squares))):
                top = jnp.where(row_at == row, piece, top)
            if q == 0:
                for expert in range(experts):
                    gains = jnp.where(routes_ref[...] == expert, gain_ref[...], 0.0)
                    gains = jnp.sum(gains, axis=1, keepdims=True)
                    for row, piece in enumerate(split(along(gains))):
                        top = jnp.where(row_at == 3 * (expert + 1) + row, piece, top)
            out_ref[:head, q * tok_here : (q + 1) * tok_here] = top.astype(jnp.bfloat16)
        if width > tokens:
            out_ref[:head, tokens:] = jnp.zeros((head, width - tokens), jnp.bfloat16)

    return local_call(
        kernel,
        pltpu.HBM((head + tokens, width), jnp.bfloat16),
        [where, stream, swapped, routes, route_gain],
        flops=4 * tokens * width,
        bytes_accessed=4 * tokens * width,
    )


def accumulate(where, positions, parts, norm_gain, tables, tok_here, carried, headers, ahead):
    count = len(positions)
    width = parts[0][0].shape[1]
    chips = norm_gain.shape[0]
    model_width = chips * width
    hidden_here = tables[0].shape[-1]
    both = 2 * hidden_here
    tokens = chips * tok_here
    sizes = [piece.shape[0] for piece in parts[0]]
    head = sum(sizes) - tokens
    offsets = [head] + [0] * (len(sizes) - 1)
    sizes = [size - at for size, at in zip(sizes, offsets)]
    starts = [sum(sizes[:k]) for k in range(len(sizes))]
    last = headers is not None
    first = carried is None
    slots = 0 if last else 4 * count

    def kernel(where_ref, *refs):
        refs = list(refs)
        xs = [[refs.pop(0) for _ in sizes] for _ in range(count)]
        scale_ref = refs.pop(0)
        stored = [refs.pop(0) for _ in tables]
        acc_in = None if first else refs.pop(0)
        tops = [refs.pop(0) for _ in headers] if last else []
        sources = [refs.pop(0) for _ in ahead[1]] if ahead else []
        owns = [refs.pop(0) for _ in range(count)]
        if last:
            hidden_ref = refs.pop(0)
        else:
            acc_out = refs.pop(0)
        if ahead:
            next_ref, down_ref = refs.pop(0), refs.pop(0)
        if last:
            column_ref = refs.pop(0)
        else:
            table_ref, sems = refs.pop(0), refs.pop(0)

        def fetch(which, position, target, sem):
            row = pl.multiple_of(where_ref[position] * width, width)
            copy = pltpu.make_async_copy(stored[which].at[pl.ds(row, width), :], target, sem)
            copy.start()
            return copy

        copies, later = {}, []
        if not last:
            for which in range(4):
                for b in range(count):
                    slot = which * count + b
                    copies[which, b] = fetch(
                        which, positions[b], table_ref.at[slot], sems.at[slot]
                    )
        if ahead:
            for which in range(4):
                later.append(fetch(which, ahead[0], next_ref.at[which], sems.at[slots + which]))
            for k, source in enumerate(sources):
                target = down_ref.at[k * hidden_here : (k + 1) * hidden_here, :]
                copy = pltpu.make_async_copy(source, target, sems.at[slots + 4 + k])
                copy.start()
                later.append(copy)
        begin = where_ref[0] * tok_here
        for b in range(count):
            for k, size in enumerate(sizes):

                @pl.when((begin >= starts[k]) & (begin < starts[k] + size))
                def _():
                    row = begin - starts[k] + offsets[k]
                    owns[b][...] = xs[b][k][pl.ds(pl.multiple_of(row, 16), tok_here), :]

        if last:
            expert = where_ref[chips]
            square = (tok_here, tok_here)
            row_at = lax.broadcasted_iota(jnp.int32, (head, tok_here), 0)
            diagonal = lax.broadcasted_iota(jnp.int32, square, 0) == lax.broadcasted_iota(
                jnp.int32, square, 1
            )

            def column(row, values):
                named = (row_at >= row) & (row_at < row + 3)
                along = jnp.sum(jnp.where(named, values, 0.0), axis=0, keepdims=True)
                return jnp.sum(jnp.where(diagonal, along, 0.0), axis=1, keepdims=True)

            for d in range(chips):
                values = tops[d][:head, :tok_here].astype(jnp.float32)
                at = pl.multiple_of(where_ref[d] * tok_here, tok_here)
                column_ref[pl.ds(at, tok_here), 0:1] = column(3 * (expert + 1), values)
            for q in range(chips):
                span = slice(q * tok_here, (q + 1) * tok_here)
                total = tops[0][:head, span].astype(jnp.float32)
                for d in range(1, chips):
                    total = total + tops[d][:head, span].astype(jnp.float32)
                mean = column(0, total) / model_width
                column_ref[span, 1:2] = lax.rsqrt(mean + epsilon)

        scaled = []
        for k, size in enumerate(sizes):
            for b in range(count):
                values = xs[b][k][offsets[k] : offsets[k] + size, :].astype(jnp.float32)
                scale = scale_ref[where_ref[positions[b]]]
                scaled.append((values * scale).astype(jnp.bfloat16))
        acts = {}
        for which in range(4):
            cols = slice(which * hidden_here, (which + 1) * hidden_here)
            for b in range(count):
                if not last:
                    copies[which, b].wait()
            for k, size in enumerate(sizes):
                span = slice(starts[k], starts[k] + size)
                total = None if first else acc_in[span, cols]
                for b in range(count):
                    if last:
                        table = stored[0][which]
                    else:
                        table = table_ref[which * count + b]
                    product = jnp.dot(
                        scaled[k * count + b], table, preferred_element_type=jnp.float32
                    )
                    total = product if total is None else total + product
                if not last:
                    acc_out[span, cols] = total
                elif which % 2 == 0:
                    acts[k] = total
                else:
                    gain, inv_rms = column_ref[span, 0:1], column_ref[span, 1:2]
                    gate_act, up_act = acts[k] * inv_rms, total * inv_rms
                    act = gate_act * jax.nn.sigmoid(gate_act) * up_act * gain
                    core = which // 2
                    out_cols = slice(core * hidden_here, (core + 1) * hidden_here)
                    hidden_ref[span, out_cols] = act.astype(jnp.bfloat16)
        for copy in later:
            copy.wait()

    operands = [where] + [piece for block in parts for piece in block]
    operands.append(norm_gain)
    distant = [] if last else list(range(len(operands), len(operands) + len(tables)))
    operands.extend(tables)
    aliases = {}
    if not first:
        if not last:
            aliases = {len(operands): count}
        operands.append(carried)
    out_shape = [jax.ShapeDtypeStruct((tok_here, width), jnp.bfloat16)] * count
    if last:
        operands.extend(headers)
        out_shape.append(jax.ShapeDtypeStruct((tokens, both), jnp.bfloat16))
    else:
        out_shape.append(jax.ShapeDtypeStruct((tokens, 2 * both), jnp.float32))
    if ahead:
        for source in ahead[1]:
            distant.append(len(operands))
            operands.append(source)
        out_shape.append(jax.ShapeDtypeStruct((4, width, hidden_here), jnp.bfloat16))
        out_shape.append(jax.ShapeDtypeStruct((both, model_width), jnp.bfloat16))
    if last:
        scratch = [pltpu.VMEM((tokens, 2), jnp.float32)]
    else:
        scratch = [
            pltpu.VMEM((slots, width, hidden_here), jnp.bfloat16),
            pltpu.SemaphoreType.DMA((slots + 6,)),
        ]
    made = local_call(
        kernel,
        out_shape,
        operands,
        flops=COST_SCALE * 4 * count * tokens * width * both,
        bytes_accessed=count * width * (tokens + 2 * both) * 2 + tokens * both * 16,
        aliases=aliases,
        scratch=scratch,
        far=distant,
    )
    return made[:count], made[count:]


def leading_rows(where, wanted, hidden, down, chips):
    tokens, units = hidden.shape
    model_width = down.shape[1]
    half = model_width // 2
    rows = tokens // chips

    def kernel(where_ref, hidden_ref, down_ref, kept_ref, *outs):
        kept_ref[...] = hidden_ref[...]
        for part in range(2):
            chosen = [k for k, (_, at) in enumerate(wanted) if at == part]
            taken = [
                hidden_ref[pl.ds(pl.multiple_of(where_ref[wanted[k][0]] * rows, rows), rows), :]
                for k in chosen
            ]
            out = jnp.dot(
                jnp.concatenate(taken, axis=0),
                down_ref[:, part * half : (part + 1) * half],
                preferred_element_type=jnp.float32,
            ).astype(jnp.bfloat16)
            for at, k in enumerate(chosen):
                outs[k][...] = out[at * rows : (at + 1) * rows, :]

    return local_call(
        kernel,
        [jax.ShapeDtypeStruct(hidden.shape, hidden.dtype)]
        + [pltpu.HBM((rows, half), jnp.bfloat16)] * len(wanted),
        [where, hidden, down],
        flops=2 * rows * units * half * len(wanted),
        bytes_accessed=2 * units * model_width,
    )


def contribution(where, hidden, down, part):
    tokens, units = hidden.shape
    half = down.shape[1] // 2
    tile = 512 if half % 512 == 0 else half

    def kernel(where_ref, hidden_ref, down_ref, out_ref):
        for start in range(0, half, tile):
            out = jnp.dot(
                hidden_ref[...],
                down_ref[:, part * half + start : part * half + start + tile],
                preferred_element_type=jnp.float32,
            )
            out_ref[:, start : start + tile] = out.astype(jnp.bfloat16)

    return local_call(
        kernel,
        pltpu.VMEM((tokens, half), jnp.bfloat16),
        [where, hidden, down],
        flops=2 * tokens * units * half,
        bytes_accessed=2 * half * (units + tokens),
    )


def add_rows(where, position, table, moved):
    rows, width = moved.shape
    steps = 2
    tile = width // steps

    def kernel(where_ref, table_ref, moved_ref, out_ref, came_ref, sems):
        cols = [slice(k * tile, (k + 1) * tile) for k in range(steps)]
        reads = [
            pltpu.make_async_copy(moved_ref.at[:, cols[k]], came_ref.at[:, cols[k]], sems.at[0, k])
            for k in range(steps)
        ]
        writes = [
            pltpu.make_async_copy(came_ref.at[:, cols[k]], out_ref.at[:, cols[k]], sems.at[1, k])
            for k in range(steps)
        ]
        for read in reads:
            read.start()
        at = pl.multiple_of(where_ref[position] * rows, rows)
        for k in range(steps):
            total = table_ref[pl.ds(at, rows), cols[k]].astype(jnp.float32)
            reads[k].wait()
            total = total + came_ref[:, cols[k]].astype(jnp.float32)
            came_ref[:, cols[k]] = total.astype(jnp.bfloat16)
            writes[k].start()
        for write in writes:
            write.wait()

    return pl.pallas_call(
        kernel,
        in_specs=[IN_SMEM, IN_VMEM, IN_HBM],
        out_specs=IN_HBM,
        out_shape=pltpu.HBM((rows, width), jnp.bfloat16),
        scratch_shapes=[
            pltpu.VMEM((rows, width), jnp.bfloat16),
            pltpu.SemaphoreType.DMA((2, steps)),
        ],
        compiler_params=pltpu.CompilerParams(vmem_limit_bytes=VMEM_BYTES),
        cost_estimate=pl.CostEstimate(
            flops=rows * width, bytes_accessed=rows * width * 6, transcendentals=0
        ),
    )(where, table, moved)


def collect(where, positions, pieces):
    rows, width = pieces[0].shape
    model_width = len(pieces) * width

    def kernel(where_ref, *refs):
        for k, position in enumerate(positions):
            start = pl.multiple_of(where_ref[position] * width, width)
            refs[-1][:, pl.ds(start, width)] = refs[k][...]

    return local_call(
        kernel,
        pltpu.VMEM((rows, model_width), jnp.bfloat16),
        [where, *pieces],
        flops=rows * model_width,
        bytes_accessed=rows * model_width * 4,
    )


def final_sum(where, stream, tables, arrived):
    rows, model_width = stream.shape
    half = model_width // 2
    steps = 2
    came = [value for part in arrived for value in part]

    def kernel(where_ref, *refs):
        out_ref = refs[-1]
        for part in range(2):
            total = refs[part][...].astype(jnp.float32) + refs[2 + part][...].astype(jnp.float32)
            for k in range(len(arrived[part])):
                total = total + refs[4 + k + part * len(arrived[0])][...].astype(jnp.float32)
            start = pl.multiple_of(part * half + pl.program_id(0) * (half // steps), 128)
            out_ref[:, pl.ds(start, half // steps)] = total.astype(jnp.bfloat16)

    block = (rows, half // steps)
    here = pl.BlockSpec(block, lambda i, where: (0, i))
    return pl.pallas_call(
        kernel,
        grid_spec=pltpu.PrefetchScalarGridSpec(
            num_scalar_prefetch=1,
            grid=(steps,),
            in_specs=[here, pl.BlockSpec(block, lambda i, where: (0, steps + i))]
            + [pl.BlockSpec(block, lambda i, where: (where[0], i))] * 2
            + [here] * len(came),
            out_specs=pl.BlockSpec((rows, model_width), lambda i, where: (0, 0)),
        ),
        out_shape=jax.ShapeDtypeStruct((rows, model_width), jnp.bfloat16),
        compiler_params=pltpu.CompilerParams(vmem_limit_bytes=VMEM_BYTES),
        cost_estimate=pl.CostEstimate(
            flops=rows * model_width * 3, bytes_accessed=rows * model_width * 10, transcendentals=0
        ),
    )(where, stream, stream, *tables, *came)


def dense_body(residual, attn_out, norm_gain, expert_routes, route_gain, w_gate, w_up, w_down):
    devices = lax.axis_size("ep")
    experts = devices // FSPLIT
    chips = devices // 2
    far = chips // 2
    tok_here = expert_routes.shape[0]
    feat_here = residual.shape[1]
    model_width = w_gate.shape[0]
    width = 2 * feat_here
    ring = ring_order(chips)
    me = lax.axis_index("ep")
    core = me % 2
    seen = [
        [ring[(ring.index(i // 2) + d) % chips] for d in range(chips)] + [i // FSPLIT, i % 2]
        for i in range(devices)
    ]
    where = lax.dynamic_index_in_dim(jnp.asarray(seen, jnp.int32), me, 0, keepdims=False)

    stream_feat = (residual.astype(jnp.float32) + attn_out.astype(jnp.float32)).astype(jnp.bfloat16)
    by_core = stream_feat.reshape(chips, 2, tok_here, feat_here)
    swapped = swap_cores(lax.dynamic_index_in_dim(by_core, 1 - core, 1, keepdims=False))

    swapped, w_gate, w_up = lax.optimization_barrier((swapped, w_gate, w_up))
    tables = [pltpu.with_memory_space_constraint(table, pltpu.HBM) for table in (w_gate, w_up)]
    tables += [swap_cores(w_gate), swap_cores(w_up)]
    blocks = {0: first_blocks(where, by_core, swapped, expert_routes, route_gain, experts)}
    w_down = lax.optimization_barrier((swapped, w_down))[1]
    down = [pltpu.with_memory_space_constraint(w_down, pltpu.HBM), swap_cores(w_down)]

    for distance in range(1, far):
        for sign in (-1, 1):
            blocks[sign * distance] = ring_shift(blocks[sign * (distance - 1)], ring, -sign)
    groups = [[0]] + [[d, chips - d] for d in range(1, far)] + [[far]]
    gain_rows = norm_gain.reshape(chips, 1, width)
    carried, owns, positions, headers, ahead = None, [], [], None, None
    for group in groups:
        parts = [[blocks[d if d <= far else d - chips]] for d in group]
        if group == [far]:
            parts = [blocks[far]]
            headers = [blocks[d if d < far else d - chips] for d in range(chips) if d != far]
            headers.insert(far, blocks[far][0])
        if group == groups[-2]:
            ahead = (far, down)
        made, (carried, *rest) = accumulate(
            where, group, parts, gain_rows, tables, tok_here, carried, headers, ahead
        )
        owns.extend(made)
        positions.extend(group)
        if group == groups[max(far - 2, 0)]:
            lower, upper, carried = lax.optimization_barrier(
                (blocks[1 - far], blocks[far - 1], carried)
            )
            cut = lower.shape[0] - far * tok_here
            blocks[far] = [ring_shift(lower[:cut], ring, 1), ring_shift(upper[cut:], ring, -1)]
        if group == groups[-2]:
            tables, down, ahead = [rest[0]], rest[1], None

    leading = [(far, 0), (far, 1), (far - 1, 1), (chips - far + 1, 0)]
    hidden, lower, upper, after, before = leading_rows(where, leading, carried, down, chips)
    moving = {1: [ring_shift(lower, ring, 1), None], -1: [None, ring_shift(upper, ring, -1)]}
    second = {1: ring_shift(after, ring, 1), -1: ring_shift(before, ring, -1)}
    stream_rows = collect(where, positions, owns)
    stream_rows, hidden = lax.optimization_barrier((stream_rows, hidden))
    everything = [contribution(where, hidden, down, part) for part in range(2)]
    for distance in range(far - 1, 0, -1):
        for sign, order in ((1, (1, 0)), (-1, (0, 1))):
            position = (sign * distance) % chips
            sent = [None, None]
            for part in order:
                if moving[sign][part] is None:
                    sent[part] = second[sign]
                else:
                    value = add_rows(where, position, everything[part], moving[sign][part])
                    sent[part] = ring_shift(value, ring, sign)
            moving[sign] = sent
    arrived = [
        [moving[sign][part] for sign in (1, -1) if moving[sign][part] is not None]
        for part in range(2)
    ]
    return final_sum(where, stream_rows, everything, arrived)


def body(residual, attn_out, norm_gain, expert_routes, route_gain, w_gate, w_up, w_down):
    tok_here, route_slots = expert_routes.shape
    devices = lax.axis_size("ep")
    capacity = route_slots * tok_here // (devices // FSPLIT)
    dense = capacity >= tok_here and devices % 8 == 0
    dense = dense and devices * tok_here <= 4 * residual.shape[1]
    chosen = dense_body if dense else routed_body
    return chosen(residual, attn_out, norm_gain, expert_routes, route_gain, w_gate, w_up, w_down)


def solution(mesh):
    in_specs = (
        P("groups", "ep"),
        P("groups", "ep"),
        P(),
        P(("groups", "ep"), None),
        P(("groups", "ep"), None),
        P(None, "ep"),
        P(None, "ep"),
        P("ep", None),
    )
    out_specs = P(("groups", "ep"), None)
    return jax.shard_map(body, mesh=mesh, in_specs=in_specs, out_specs=out_specs, check_vma=False)
```

```python
import jax
import jax.numpy as jnp
from jax import lax
from jax.experimental import pallas as pl
from jax.experimental.pallas import tpu as pltpu
from jax.sharding import PartitionSpec as P

FSPLIT = 8


epsilon = 1e-06


def normalize(stream_rows, norm_gain):
    values = stream_rows.astype(jnp.float32)
    inv_rms = lax.rsqrt(jnp.mean(values * values, axis=-1, keepdims=True) + epsilon)
    return (values * inv_rms * norm_gain).astype(jnp.bfloat16)


def route_match(routes, experts, capacity):
    flat_ids = routes.reshape(-1)
    onehot = (flat_ids[:, None] == jnp.arange(experts, dtype=jnp.int32)[None, :]).astype(jnp.int32)
    earlier = jnp.cumsum(onehot, axis=0) - onehot
    slot_pos = jnp.sum(earlier * onehot, axis=1)
    slot_code = jnp.where(flat_ids < experts, flat_ids * capacity + slot_pos, -1)
    target = jnp.arange(experts * capacity, dtype=jnp.int32)
    return slot_code[None, :] == target[:, None]


def selection(routes, experts, capacity):
    matched = route_match(routes, experts, capacity).astype(jnp.int32)
    return matched.reshape(experts * capacity, routes.shape[0], routes.shape[1]).sum(axis=2)


def gain_table(routes, route_gain, experts, capacity):
    matched = route_match(routes, experts, capacity)
    weighted = jnp.where(matched, route_gain.reshape(-1)[None, :], 0.0)
    return weighted.reshape(experts * capacity, routes.shape[0], routes.shape[1]).sum(axis=2).T


def expert_rows(normed, w_gate, w_up, w_down):
    gate_act = jnp.dot(normed, w_gate, preferred_element_type=jnp.float32)
    up_act = jnp.dot(normed, w_up, preferred_element_type=jnp.float32)
    hidden = (jax.nn.silu(gate_act) * up_act).astype(jnp.bfloat16)
    return jnp.dot(hidden, w_down, preferred_element_type=jnp.float32).astype(jnp.bfloat16)


def routed_body(residual, attn_out, norm_gain, expert_routes, route_gain, w_gate, w_up, w_down):
    devices = lax.axis_size("ep")
    tok_here = expert_routes.shape[0]
    route_slots = expert_routes.shape[1]
    experts = devices // FSPLIT
    capacity = route_slots * tok_here // experts
    model_width = w_gate.shape[0]
    stream_feat = (residual.astype(jnp.float32) + attn_out.astype(jnp.float32)).astype(jnp.bfloat16)
    stream_rows = lax.all_to_all(stream_feat, "ep", split_axis=0, concat_axis=1, tiled=True)
    combine_weights = gain_table(expert_routes, route_gain, experts, capacity)
    normed_rows = normalize(stream_rows, norm_gain)
    select = selection(expert_routes, experts, capacity).astype(jnp.bfloat16)
    per_expert = jnp.dot(select, normed_rows, preferred_element_type=jnp.float32).astype(
        jnp.bfloat16
    )
    per_expert = per_expert.reshape(experts, 1, capacity, model_width)
    outgoing = jnp.broadcast_to(per_expert, (experts, FSPLIT, capacity, model_width))
    outgoing = outgoing.reshape(devices, capacity, model_width)
    received = lax.all_to_all(outgoing, "ep", split_axis=0, concat_axis=0, tiled=True)
    slot_count = received.shape[1]
    partial_value = expert_rows(received.reshape(-1, model_width), w_gate, w_up, w_down)
    partial_value = partial_value.reshape(devices, slot_count, model_width)
    returned = lax.all_to_all(partial_value, "ep", split_axis=0, concat_axis=0, tiled=True)
    summed = (
        returned.reshape(experts, FSPLIT, capacity, model_width).astype(jnp.float32).sum(axis=1)
    )
    summed = summed.reshape(experts * capacity, model_width)
    routed_sum = jnp.dot(combine_weights, summed, precision=lax.Precision.HIGHEST)
    return (stream_rows.astype(jnp.float32) + routed_sum).astype(jnp.bfloat16)


def ring_order(chips):
    return list(range(0, chips, 2)) + list(reversed(range(1, chips, 2)))


def swap_cores(value):
    return lax.ppermute(value, "ep", [(i, i ^ 1) for i in range(lax.axis_size("ep"))])


def ring_shift(value, ring, step):
    chips = len(ring)
    pairs = [
        (2 * ring[i] + core, 2 * ring[(i + step) % chips] + core)
        for i in range(chips)
        for core in range(2)
    ]
    return lax.ppermute(value, "ep", pairs)


COST_SCALE = 3
VMEM_BYTES = 20 * 1024 * 1024
WIDE_VMEM_BYTES = 636 * 1024 * 1024 // 10
IN_VMEM = pl.BlockSpec(memory_space=pltpu.VMEM)
IN_SMEM = pl.BlockSpec(memory_space=pltpu.SMEM)
IN_HBM = pl.BlockSpec(memory_space=pltpu.HBM)


def local_call(
    kernel, out_shape, operands, flops, bytes_accessed, aliases=None, scratch=(), far=()
):
    return pl.pallas_call(
        kernel,
        out_shape=out_shape,
        in_specs=[
            IN_SMEM if k == 0 else IN_HBM if k in far else IN_VMEM for k in range(len(operands))
        ],
        out_specs=jax.tree.map(
            lambda made: IN_SMEM if made.dtype == jnp.int32 else IN_VMEM, out_shape
        ),
        scratch_shapes=list(scratch),
        input_output_aliases=aliases or {},
        compiler_params=pltpu.CompilerParams(vmem_limit_bytes=VMEM_BYTES),
        cost_estimate=pl.CostEstimate(
            flops=flops, bytes_accessed=bytes_accessed, transcendentals=0
        ),
    )(*operands)


def first_blocks(where, stream, swapped, routes, route_gain, experts):
    chips, _, tok_here, feat_here = stream.shape
    width = 2 * feat_here
    tokens = chips * tok_here
    head = -(-3 * (experts + 1) // 16) * 16

    def kernel(where_ref, stream_ref, swapped_ref, routes_ref, gain_ref, out_ref):
        core = where_ref[chips + 1]
        square = (tok_here, tok_here)
        diagonal = lax.broadcasted_iota(jnp.int32, square, 0) == lax.broadcasted_iota(
            jnp.int32, square, 1
        )

        def along(column):
            return jnp.sum(jnp.where(diagonal, column, 0.0), axis=0, keepdims=True)

        def split(left):
            for _ in range(3):
                piece = left.astype(jnp.bfloat16).astype(jnp.float32)
                left = left - piece
                yield piece

        row_at = lax.broadcasted_iota(jnp.int32, (head, tok_here), 0)
        for q in range(chips):
            mine = stream_ref[q, core]
            other = swapped_ref[q]
            left = jnp.where(core == 0, mine, other)
            right = jnp.where(core == 0, other, mine)
            at = head + q * tok_here
            out_ref[at : at + tok_here, :] = jnp.concatenate([left, right], axis=1)
            left, right = left.astype(jnp.float32), right.astype(jnp.float32)
            squares = jnp.sum(left * left + right * right, axis=1, keepdims=True)
            top = jnp.zeros((head, tok_here), jnp.float32)
            for row, piece in enumerate(split(along(squares))):
                top = jnp.where(row_at == row, piece, top)
            if q == 0:
                for expert in range(experts):
                    gains = jnp.where(routes_ref[...] == expert, gain_ref[...], 0.0)
                    gains = jnp.sum(gains, axis=1, keepdims=True)
                    for row, piece in enumerate(split(along(gains))):
                        top = jnp.where(row_at == 3 * (expert + 1) + row, piece, top)
            out_ref[:head, q * tok_here : (q + 1) * tok_here] = top.astype(jnp.bfloat16)
        if width > tokens:
            out_ref[:head, tokens:] = jnp.zeros((head, width - tokens), jnp.bfloat16)

    return local_call(
        kernel,
        pltpu.HBM((head + tokens, width), jnp.bfloat16),
        [where, stream, swapped, routes, route_gain],
        flops=4 * tokens * width,
        bytes_accessed=4 * tokens * width,
    )


def accumulate(where, positions, parts, norm_gain, tables, tok_here, carried, headers, ahead):
    count = len(positions)
    width = parts[0][0].shape[1]
    chips = norm_gain.shape[0]
    model_width = chips * width
    hidden_here = tables[0].shape[-1]
    both = 2 * hidden_here
    tokens = chips * tok_here
    sizes = [piece.shape[0] for piece in parts[0]]
    head = sum(sizes) - tokens
    offsets = [head] + [0] * (len(sizes) - 1)
    sizes = [size - at for size, at in zip(sizes, offsets)]
    starts = [sum(sizes[:k]) for k in range(len(sizes))]
    last = headers is not None
    first = carried is None
    slots = 0 if last else 4 * count

    def kernel(where_ref, *refs):
        refs = list(refs)
        xs = [[refs.pop(0) for _ in sizes] for _ in range(count)]
        scale_ref = refs.pop(0)
        stored = [refs.pop(0) for _ in tables]
        acc_in = None if first else refs.pop(0)
        tops = [refs.pop(0) for _ in headers] if last else []
        sources = [refs.pop(0) for _ in ahead[1]] if ahead else []
        owns = [refs.pop(0) for _ in range(count)]
        if last:
            hidden_ref = refs.pop(0)
        else:
            acc_out = refs.pop(0)
        if ahead:
            next_ref, down_ref = refs.pop(0), refs.pop(0)
        if last:
            column_ref = refs.pop(0)
        else:
            table_ref, sems = refs.pop(0), refs.pop(0)

        def fetch(which, position, target, sem):
            row = pl.multiple_of(where_ref[position] * width, width)
            copy = pltpu.make_async_copy(stored[which].at[pl.ds(row, width), :], target, sem)
            copy.start()
            return copy

        copies, later = {}, []
        if not last:
            for which in range(4):
                for b in range(count):
                    slot = which * count + b
                    copies[which, b] = fetch(
                        which, positions[b], table_ref.at[slot], sems.at[slot]
                    )
        if ahead:
            for which in range(4):
                later.append(fetch(which, ahead[0], next_ref.at[which], sems.at[slots + which]))
            for k, source in enumerate(sources):
                target = down_ref.at[k * hidden_here : (k + 1) * hidden_here, :]
                copy = pltpu.make_async_copy(source, target, sems.at[slots + 4 + k])
                copy.start()
                later.append(copy)
        begin = where_ref[0] * tok_here
        for b in range(count):
            for k, size in enumerate(sizes):

                @pl.when((begin >= starts[k]) & (begin < starts[k] + size))
                def _():
                    row = begin - starts[k] + offsets[k]
                    owns[b][...] = xs[b][k][pl.ds(pl.multiple_of(row, 16), tok_here), :]

        if last:
            expert = where_ref[chips]
            square = (tok_here, tok_here)
            row_at = lax.broadcasted_iota(jnp.int32, (head, tok_here), 0)
            diagonal = lax.broadcasted_iota(jnp.int32, square, 0) == lax.broadcasted_iota(
                jnp.int32, square, 1
            )

            def column(row, values):
                named = (row_at >= row) & (row_at < row + 3)
                along = jnp.sum(jnp.where(named, values, 0.0), axis=0, keepdims=True)
                return jnp.sum(jnp.where(diagonal, along, 0.0), axis=1, keepdims=True)

            for d in range(chips):
                values = tops[d][:head, :tok_here].astype(jnp.float32)
                at = pl.multiple_of(where_ref[d] * tok_here, tok_here)
                column_ref[pl.ds(at, tok_here), 0:1] = column(3 * (expert + 1), values)
            for q in range(chips):
                span = slice(q * tok_here, (q + 1) * tok_here)
                total = tops[0][:head, span].astype(jnp.float32)
                for d in range(1, chips):
                    total = total + tops[d][:head, span].astype(jnp.float32)
                mean = column(0, total) / model_width
                column_ref[span, 1:2] = lax.rsqrt(mean + epsilon)

        scaled = []
        for k, size in enumerate(sizes):
            for b in range(count):
                values = xs[b][k][offsets[k] : offsets[k] + size, :].astype(jnp.float32)
                scale = scale_ref[where_ref[positions[b]]]
                scaled.append((values * scale).astype(jnp.bfloat16))
        acts = {}
        for which in range(4):
            cols = slice(which * hidden_here, (which + 1) * hidden_here)
            for b in range(count):
                if not last:
                    copies[which, b].wait()
            for k, size in enumerate(sizes):
                span = slice(starts[k], starts[k] + size)
                total = None if first else acc_in[span, cols]
                for b in range(count):
                    if last:
                        table = stored[0][which]
                    else:
                        table = table_ref[which * count + b]
                    product = jnp.dot(
                        scaled[k * count + b], table, preferred_element_type=jnp.float32
                    )
                    total = product if total is None else total + product
                if not last:
                    acc_out[span, cols] = total
                elif which % 2 == 0:
                    acts[k] = total
                else:
                    gain, inv_rms = column_ref[span, 0:1], column_ref[span, 1:2]
                    gate_act, up_act = acts[k] * inv_rms, total * inv_rms
                    act = gate_act * jax.nn.sigmoid(gate_act) * up_act * gain
                    core = which // 2
                    out_cols = slice(core * hidden_here, (core + 1) * hidden_here)
                    hidden_ref[span, out_cols] = act.astype(jnp.bfloat16)
        for copy in later:
            copy.wait()

    operands = [where] + [piece for block in parts for piece in block]
    operands.append(norm_gain)
    distant = [] if last else list(range(len(operands), len(operands) + len(tables)))
    operands.extend(tables)
    aliases = {}
    if not first:
        if not last:
            aliases = {len(operands): count}
        operands.append(carried)
    out_shape = [jax.ShapeDtypeStruct((tok_here, width), jnp.bfloat16)] * count
    if last:
        operands.extend(headers)
        out_shape.append(jax.ShapeDtypeStruct((tokens, both), jnp.bfloat16))
    else:
        out_shape.append(jax.ShapeDtypeStruct((tokens, 2 * both), jnp.float32))
    if ahead:
        for source in ahead[1]:
            distant.append(len(operands))
            operands.append(source)
        out_shape.append(jax.ShapeDtypeStruct((4, width, hidden_here), jnp.bfloat16))
        out_shape.append(jax.ShapeDtypeStruct((both, model_width), jnp.bfloat16))
    if last:
        scratch = [pltpu.VMEM((tokens, 2), jnp.float32)]
    else:
        scratch = [
            pltpu.VMEM((slots, width, hidden_here), jnp.bfloat16),
            pltpu.SemaphoreType.DMA((slots + 6,)),
        ]
    made = local_call(
        kernel,
        out_shape,
        operands,
        flops=COST_SCALE * 4 * count * tokens * width * both,
        bytes_accessed=count * width * (tokens + 2 * both) * 2 + tokens * both * 16,
        aliases=aliases,
        scratch=scratch,
        far=distant,
    )
    return made[:count], made[count:]


def leading_rows(where, wanted, hidden, down, chips):
    tokens, units = hidden.shape
    model_width = down.shape[1]
    half = model_width // 2
    rows = tokens // chips

    def kernel(where_ref, hidden_ref, down_ref, kept_ref, *outs):
        kept_ref[...] = hidden_ref[...]
        for part in range(2):
            chosen = [k for k, (_, at) in enumerate(wanted) if at == part]
            taken = [
                hidden_ref[pl.ds(pl.multiple_of(where_ref[wanted[k][0]] * rows, rows), rows), :]
                for k in chosen
            ]
            out = jnp.dot(
                jnp.concatenate(taken, axis=0),
                down_ref[:, part * half : (part + 1) * half],
                preferred_element_type=jnp.float32,
            ).astype(jnp.bfloat16)
            for at, k in enumerate(chosen):
                outs[k][...] = out[at * rows : (at + 1) * rows, :]

    return local_call(
        kernel,
        [jax.ShapeDtypeStruct(hidden.shape, hidden.dtype)]
        + [pltpu.HBM((rows, half), jnp.bfloat16)] * len(wanted),
        [where, hidden, down],
        flops=2 * rows * units * half * len(wanted),
        bytes_accessed=2 * units * model_width,
    )


def contribution(where, hidden, down, part):
    tokens, units = hidden.shape
    half = down.shape[1] // 2
    tile = 512 if half % 512 == 0 else half

    def kernel(where_ref, hidden_ref, down_ref, out_ref):
        for start in range(0, half, tile):
            out = jnp.dot(
                hidden_ref[...],
                down_ref[:, part * half + start : part * half + start + tile],
                preferred_element_type=jnp.float32,
            )
            out_ref[:, start : start + tile] = out.astype(jnp.bfloat16)

    return local_call(
        kernel,
        pltpu.HBM((tokens, half), jnp.bfloat16),
        [where, hidden, down],
        flops=2 * tokens * units * half,
        bytes_accessed=2 * half * (units + tokens),
    )


def add_rows(where, position, table, moved):
    rows, width = moved.shape
    steps = 2
    tile = width // steps

    def kernel(where_ref, table_ref, moved_ref, out_ref, came_ref, here_ref, sems):
        at = pl.multiple_of(where_ref[position] * rows, rows)
        reads, writes = [], []
        for k in range(steps):
            cols = slice(k * tile, (k + 1) * tile)
            reads.append(
                [
                    pltpu.make_async_copy(
                        moved_ref.at[:, cols], came_ref.at[:, cols], sems.at[0, k]
                    ),
                    pltpu.make_async_copy(
                        table_ref.at[pl.ds(at, rows), cols], here_ref.at[:, cols], sems.at[1, k]
                    ),
                ]
            )
            writes.append(
                pltpu.make_async_copy(came_ref.at[:, cols], out_ref.at[:, cols], sems.at[2, k])
            )
        for pair in reads:
            for read in pair:
                read.start()
        for k in range(steps):
            cols = slice(k * tile, (k + 1) * tile)
            for read in reads[k]:
                read.wait()
            total = here_ref[:, cols].astype(jnp.float32) + came_ref[:, cols].astype(jnp.float32)
            came_ref[:, cols] = total.astype(jnp.bfloat16)
            writes[k].start()
        for write in writes:
            write.wait()

    return pl.pallas_call(
        kernel,
        in_specs=[IN_SMEM, IN_HBM, IN_HBM],
        out_specs=IN_HBM,
        out_shape=pltpu.HBM((rows, width), jnp.bfloat16),
        scratch_shapes=[
            pltpu.VMEM((rows, width), jnp.bfloat16),
            pltpu.VMEM((rows, width), jnp.bfloat16),
            pltpu.SemaphoreType.DMA((3, steps)),
        ],
        compiler_params=pltpu.CompilerParams(vmem_limit_bytes=WIDE_VMEM_BYTES),
        cost_estimate=pl.CostEstimate(
            flops=rows * width, bytes_accessed=rows * width * 6, transcendentals=0
        ),
    )(where, table, moved)


def collect(where, positions, pieces):
    rows, width = pieces[0].shape
    model_width = len(pieces) * width

    def kernel(where_ref, *refs):
        for k, position in enumerate(positions):
            start = pl.multiple_of(where_ref[position] * width, width)
            refs[-1][:, pl.ds(start, width)] = refs[k][...]

    return local_call(
        kernel,
        pltpu.HBM((rows, model_width), jnp.bfloat16),
        [where, *pieces],
        flops=rows * model_width,
        bytes_accessed=rows * model_width * 4,
    )


def final_sum(where, stream, tables, arrived):
    rows, model_width = stream.shape
    half = model_width // 2
    counts = [len(part) for part in arrived]
    came = [value for part in arrived for value in part]

    def kernel(where_ref, stream_ref, *refs):
        sources, (out_ref, held_ref, sum_ref, sems) = refs[: 2 + len(came)], refs[2 + len(came) :]
        at = pl.multiple_of(where_ref[0] * rows, rows)
        reads, writes, slot = [], [], 0
        for part in range(2):
            cols = slice(part * half, (part + 1) * half)
            first = 2 + sum(counts[:part])
            taken = [stream_ref.at[:, cols], sources[part].at[pl.ds(at, rows), :]]
            taken += [ref.at[...] for ref in sources[first : first + counts[part]]]
            reads.append([])
            for ref in taken:
                copy = pltpu.make_async_copy(ref, held_ref.at[slot], sems.at[slot])
                copy.start()
                reads[part].append((copy, slot))
                slot += 1
        for part in range(2):
            cols = slice(part * half, (part + 1) * half)
            total = jnp.zeros((rows, half), jnp.float32)
            for copy, k in reads[part]:
                copy.wait()
                total = total + held_ref[k].astype(jnp.float32)
            sum_ref[:, cols] = total.astype(jnp.bfloat16)
            write = pltpu.make_async_copy(
                sum_ref.at[:, cols], out_ref.at[:, cols], sems.at[slot + part]
            )
            write.start()
            writes.append(write)
        for write in writes:
            write.wait()

    slots = 4 + len(came)
    return pl.pallas_call(
        kernel,
        in_specs=[IN_SMEM] + [IN_HBM] * (3 + len(came)),
        out_specs=IN_HBM,
        out_shape=jax.ShapeDtypeStruct((rows, model_width), jnp.bfloat16),
        scratch_shapes=[
            pltpu.VMEM((slots, rows, half), jnp.bfloat16),
            pltpu.VMEM((rows, model_width), jnp.bfloat16),
            pltpu.SemaphoreType.DMA((slots + 2,)),
        ],
        compiler_params=pltpu.CompilerParams(vmem_limit_bytes=WIDE_VMEM_BYTES),
        cost_estimate=pl.CostEstimate(
            flops=rows * model_width * 3, bytes_accessed=rows * model_width * 10, transcendentals=0
        ),
    )(where, stream, *tables, *came)


def dense_body(residual, attn_out, norm_gain, expert_routes, route_gain, w_gate, w_up, w_down):
    devices = lax.axis_size("ep")
    experts = devices // FSPLIT
    chips = devices // 2
    far = chips // 2
    tok_here = expert_routes.shape[0]
    feat_here = residual.shape[1]
    model_width = w_gate.shape[0]
    width = 2 * feat_here
    ring = ring_order(chips)
    me = lax.axis_index("ep")
    core = me % 2
    seen = [
        [ring[(ring.index(i // 2) + d) % chips] for d in range(chips)] + [i // FSPLIT, i % 2]
        for i in range(devices)
    ]
    where = lax.dynamic_index_in_dim(jnp.asarray(seen, jnp.int32), me, 0, keepdims=False)

    stream_feat = (residual.astype(jnp.float32) + attn_out.astype(jnp.float32)).astype(jnp.bfloat16)
    by_core = stream_feat.reshape(chips, 2, tok_here, feat_here)
    swapped = swap_cores(lax.dynamic_index_in_dim(by_core, 1 - core, 1, keepdims=False))

    swapped, w_gate, w_up = lax.optimization_barrier((swapped, w_gate, w_up))
    tables = [pltpu.with_memory_space_constraint(table, pltpu.HBM) for table in (w_gate, w_up)]
    tables += [swap_cores(w_gate), swap_cores(w_up)]
    blocks = {0: first_blocks(where, by_core, swapped, expert_routes, route_gain, experts)}
    w_down = lax.optimization_barrier((swapped, w_down))[1]
    down = [pltpu.with_memory_space_constraint(w_down, pltpu.HBM), swap_cores(w_down)]

    for distance in range(1, far):
        for sign in (-1, 1):
            blocks[sign * distance] = ring_shift(blocks[sign * (distance - 1)], ring, -sign)
    groups = [[0]] + [[d, chips - d] for d in range(1, far)] + [[far]]
    gain_rows = norm_gain.reshape(chips, 1, width)
    carried, owns, positions, headers, ahead = None, [], [], None, None
    for group in groups:
        parts = [[blocks[d if d <= far else d - chips]] for d in group]
        if group == [far]:
            parts = [blocks[far]]
            headers = [blocks[d if d < far else d - chips] for d in range(chips) if d != far]
            headers.insert(far, blocks[far][0])
        if group == groups[-2]:
            ahead = (far, down)
        made, (carried, *rest) = accumulate(
            where, group, parts, gain_rows, tables, tok_here, carried, headers, ahead
        )
        owns.extend(made)
        positions.extend(group)
        if group == groups[max(far - 2, 0)]:
            lower, upper, carried = lax.optimization_barrier(
                (blocks[1 - far], blocks[far - 1], carried)
            )
            cut = lower.shape[0] - far * tok_here
            blocks[far] = [ring_shift(lower[:cut], ring, 1), ring_shift(upper[cut:], ring, -1)]
        if group == groups[-2]:
            tables, down, ahead = [rest[0]], rest[1], None

    leading = [(far, 0), (far, 1), (far - 1, 1), (chips - far + 1, 0)]
    hidden, lower, upper, after, before = leading_rows(where, leading, carried, down, chips)
    moving = {1: [ring_shift(lower, ring, 1), None], -1: [None, ring_shift(upper, ring, -1)]}
    second = {1: ring_shift(after, ring, 1), -1: ring_shift(before, ring, -1)}
    stream_rows = collect(where, positions, owns)
    stream_rows, hidden = lax.optimization_barrier((stream_rows, hidden))
    everything = [contribution(where, hidden, down, part) for part in range(2)]
    for distance in range(far - 1, 0, -1):
        for sign, order in ((1, (1, 0)), (-1, (0, 1))):
            position = (sign * distance) % chips
            sent = [None, None]
            for part in order:
                if moving[sign][part] is None:
                    sent[part] = second[sign]
                else:
                    value = add_rows(where, position, everything[part], moving[sign][part])
                    sent[part] = ring_shift(value, ring, sign)
            moving[sign] = sent
    arrived = [
        [moving[sign][part] for sign in (1, -1) if moving[sign][part] is not None]
        for part in range(2)
    ]
    return final_sum(where, stream_rows, everything, arrived)


def body(residual, attn_out, norm_gain, expert_routes, route_gain, w_gate, w_up, w_down):
    tok_here, route_slots = expert_routes.shape
    devices = lax.axis_size("ep")
    capacity = route_slots * tok_here // (devices // FSPLIT)
    dense = capacity >= tok_here and devices % 8 == 0
    dense = dense and devices * tok_here <= 4 * residual.shape[1]
    chosen = dense_body if dense else routed_body
    return chosen(residual, attn_out, norm_gain, expert_routes, route_gain, w_gate, w_up, w_down)


def solution(mesh):
    in_specs = (
        P("groups", "ep"),
        P("groups", "ep"),
        P(),
        P(("groups", "ep"), None),
        P(("groups", "ep"), None),
        P(None, "ep"),
        P(None, "ep"),
        P("ep", None),
    )
    out_specs = P(("groups", "ep"), None)
    return jax.shard_map(body, mesh=mesh, in_specs=in_specs, out_specs=out_specs, check_vma=False)
```

```python
import jax
import jax.numpy as jnp
from jax import lax
from jax.experimental import pallas as pl
from jax.experimental.pallas import tpu as pltpu
from jax.sharding import PartitionSpec as P

FSPLIT = 8


epsilon = 1e-06


def normalize(stream_rows, norm_gain):
    values = stream_rows.astype(jnp.float32)
    inv_rms = lax.rsqrt(jnp.mean(values * values, axis=-1, keepdims=True) + epsilon)
    return (values * inv_rms * norm_gain).astype(jnp.bfloat16)


def route_match(routes, experts, capacity):
    flat_ids = routes.reshape(-1)
    onehot = (flat_ids[:, None] == jnp.arange(experts, dtype=jnp.int32)[None, :]).astype(jnp.int32)
    earlier = jnp.cumsum(onehot, axis=0) - onehot
    slot_pos = jnp.sum(earlier * onehot, axis=1)
    slot_code = jnp.where(flat_ids < experts, flat_ids * capacity + slot_pos, -1)
    target = jnp.arange(experts * capacity, dtype=jnp.int32)
    return slot_code[None, :] == target[:, None]


def selection(routes, experts, capacity):
    matched = route_match(routes, experts, capacity).astype(jnp.int32)
    return matched.reshape(experts * capacity, routes.shape[0], routes.shape[1]).sum(axis=2)


def gain_table(routes, route_gain, experts, capacity):
    matched = route_match(routes, experts, capacity)
    weighted = jnp.where(matched, route_gain.reshape(-1)[None, :], 0.0)
    return weighted.reshape(experts * capacity, routes.shape[0], routes.shape[1]).sum(axis=2).T


def expert_rows(normed, w_gate, w_up, w_down):
    gate_act = jnp.dot(normed, w_gate, preferred_element_type=jnp.float32)
    up_act = jnp.dot(normed, w_up, preferred_element_type=jnp.float32)
    hidden = (jax.nn.silu(gate_act) * up_act).astype(jnp.bfloat16)
    return jnp.dot(hidden, w_down, preferred_element_type=jnp.float32).astype(jnp.bfloat16)


def routed_body(residual, attn_out, norm_gain, expert_routes, route_gain, w_gate, w_up, w_down):
    devices = lax.axis_size("ep")
    tok_here = expert_routes.shape[0]
    route_slots = expert_routes.shape[1]
    experts = devices // FSPLIT
    capacity = route_slots * tok_here // experts
    model_width = w_gate.shape[0]
    stream_feat = (residual.astype(jnp.float32) + attn_out.astype(jnp.float32)).astype(jnp.bfloat16)
    stream_rows = lax.all_to_all(stream_feat, "ep", split_axis=0, concat_axis=1, tiled=True)
    combine_weights = gain_table(expert_routes, route_gain, experts, capacity)
    normed_rows = normalize(stream_rows, norm_gain)
    select = selection(expert_routes, experts, capacity).astype(jnp.bfloat16)
    per_expert = jnp.dot(select, normed_rows, preferred_element_type=jnp.float32).astype(
        jnp.bfloat16
    )
    per_expert = per_expert.reshape(experts, 1, capacity, model_width)
    outgoing = jnp.broadcast_to(per_expert, (experts, FSPLIT, capacity, model_width))
    outgoing = outgoing.reshape(devices, capacity, model_width)
    received = lax.all_to_all(outgoing, "ep", split_axis=0, concat_axis=0, tiled=True)
    slot_count = received.shape[1]
    partial_value = expert_rows(received.reshape(-1, model_width), w_gate, w_up, w_down)
    partial_value = partial_value.reshape(devices, slot_count, model_width)
    returned = lax.all_to_all(partial_value, "ep", split_axis=0, concat_axis=0, tiled=True)
    summed = (
        returned.reshape(experts, FSPLIT, capacity, model_width).astype(jnp.float32).sum(axis=1)
    )
    summed = summed.reshape(experts * capacity, model_width)
    routed_sum = jnp.dot(combine_weights, summed, precision=lax.Precision.HIGHEST)
    return (stream_rows.astype(jnp.float32) + routed_sum).astype(jnp.bfloat16)


def ring_order(chips):
    return list(range(0, chips, 2)) + list(reversed(range(1, chips, 2)))


def swap_cores(value):
    return lax.ppermute(value, "ep", [(i, i ^ 1) for i in range(lax.axis_size("ep"))])


def ring_shift(value, ring, step):
    chips = len(ring)
    pairs = [
        (2 * ring[i] + core, 2 * ring[(i + step) % chips] + core)
        for i in range(chips)
        for core in range(2)
    ]
    return lax.ppermute(value, "ep", pairs)


COST_SCALE = 3
VMEM_BYTES = 20 * 1024 * 1024
IN_VMEM = pl.BlockSpec(memory_space=pltpu.VMEM)
IN_SMEM = pl.BlockSpec(memory_space=pltpu.SMEM)
IN_HBM = pl.BlockSpec(memory_space=pltpu.HBM)


def local_call(
    kernel, out_shape, operands, flops, bytes_accessed, aliases=None, scratch=(), far=()
):
    return pl.pallas_call(
        kernel,
        out_shape=out_shape,
        in_specs=[
            IN_SMEM if value.ndim == 1 else IN_HBM if k in far else IN_VMEM
            for k, value in enumerate(operands)
        ],
        out_specs=jax.tree.map(
            lambda made: IN_SMEM if made.dtype == jnp.int32 else IN_VMEM, out_shape
        ),
        scratch_shapes=list(scratch),
        input_output_aliases=aliases or {},
        compiler_params=pltpu.CompilerParams(vmem_limit_bytes=VMEM_BYTES),
        cost_estimate=pl.CostEstimate(
            flops=flops, bytes_accessed=bytes_accessed, transcendentals=0
        ),
    )(*operands)


def first_blocks(stream, swapped, routes, route_gain, experts):
    chips, _, tok_here, feat_here = stream.shape
    width = 2 * feat_here
    tokens = chips * tok_here
    head = -(-3 * (experts + 1) // 16) * 16

    def kernel(stream_ref, swapped_ref, routes_ref, gain_ref, out_ref):
        core = lax.rem(lax.axis_index("ep"), 2)
        square = (tok_here, tok_here)
        diagonal = lax.broadcasted_iota(jnp.int32, square, 0) == lax.broadcasted_iota(
            jnp.int32, square, 1
        )

        def along(column):
            return jnp.sum(jnp.where(diagonal, column, 0.0), axis=0, keepdims=True)

        def split(left):
            for _ in range(3):
                piece = left.astype(jnp.bfloat16).astype(jnp.float32)
                left = left - piece
                yield piece

        row_at = lax.broadcasted_iota(jnp.int32, (head, tok_here), 0)
        for q in range(chips):
            mine = stream_ref[q, core]
            other = swapped_ref[q]
            left = jnp.where(core == 0, mine, other)
            right = jnp.where(core == 0, other, mine)
            at = head + q * tok_here
            out_ref[at : at + tok_here, :] = jnp.concatenate([left, right], axis=1)
            left, right = left.astype(jnp.float32), right.astype(jnp.float32)
            squares = jnp.sum(left * left + right * right, axis=1, keepdims=True)
            top = jnp.zeros((head, tok_here), jnp.float32)
            for row, piece in enumerate(split(along(squares))):
                top = jnp.where(row_at == row, piece, top)
            if q == 0:
                for expert in range(experts):
                    gains = jnp.where(routes_ref[...] == expert, gain_ref[...], 0.0)
                    gains = jnp.sum(gains, axis=1, keepdims=True)
                    for row, piece in enumerate(split(along(gains))):
                        top = jnp.where(row_at == 3 * (expert + 1) + row, piece, top)
            out_ref[:head, q * tok_here : (q + 1) * tok_here] = top.astype(jnp.bfloat16)
        if width > tokens:
            out_ref[:head, tokens:] = jnp.zeros((head, width - tokens), jnp.bfloat16)

    return local_call(
        kernel,
        jax.ShapeDtypeStruct((head + tokens, width), jnp.bfloat16),
        [stream, swapped, routes, route_gain],
        flops=4 * tokens * width,
        bytes_accessed=4 * tokens * width,
    )


def accumulate(
    where, positions, parts, norm_gain, tables, tok_here, carried, headers, ahead, leading
):
    count = len(positions)
    width = parts[0][0].shape[1]
    chips = norm_gain.shape[0]
    model_width = chips * width
    hidden_here = tables[0].shape[-1]
    both = 2 * hidden_here
    half = model_width // 2
    tokens = chips * tok_here
    sizes = [piece.shape[0] for piece in parts[0]]
    head = sum(sizes) - tokens
    offsets = [head] + [0] * (len(sizes) - 1)
    sizes = [size - at for size, at in zip(sizes, offsets)]
    starts = [sum(sizes[:k]) for k in range(len(sizes))]
    last = headers is not None
    first = carried is None
    slots = 0 if last else 4 * count

    def kernel(where_ref, *refs):
        refs = list(refs)
        xs = [[refs.pop(0) for _ in sizes] for _ in range(count)]
        scale_ref = refs.pop(0)
        stored = [refs.pop(0) for _ in tables]
        acc_in = None if first else refs.pop(0)
        tops = [refs.pop(0) for _ in headers] if last else []
        sources = [refs.pop(0) for _ in ahead[1]] if ahead else []
        product_ref = refs.pop(0) if leading else None
        owns = [refs.pop(0) for _ in range(count)]
        if last:
            hidden_ref = refs.pop(0)
            leads = [refs.pop(0) for _ in leading[1]]
        else:
            acc_out = refs.pop(0)
        if ahead:
            next_ref, down_ref = refs.pop(0), refs.pop(0)
        if last:
            column_ref = refs.pop(0)
        else:
            table_ref, sems = refs.pop(0), refs.pop(0)

        def fetch(which, position, target, sem):
            row = pl.multiple_of(where_ref[position] * width, width)
            copy = pltpu.make_async_copy(stored[which].at[pl.ds(row, width), :], target, sem)
            copy.start()
            return copy

        copies, later = {}, []
        if not last:
            for which in range(4):
                for b in range(count):
                    slot = which * count + b
                    copies[which, b] = fetch(
                        which, positions[b], table_ref.at[slot], sems.at[slot]
                    )
        if ahead:
            for which in range(4):
                later.append(fetch(which, ahead[0], next_ref.at[which], sems.at[slots + which]))
            for k, source in enumerate(sources):
                target = down_ref.at[k * hidden_here : (k + 1) * hidden_here, :]
                copy = pltpu.make_async_copy(source, target, sems.at[slots + 4 + k])
                copy.start()
                later.append(copy)
        begin = where_ref[0] * tok_here
        for b in range(count):
            for k, size in enumerate(sizes):

                @pl.when((begin >= starts[k]) & (begin < starts[k] + size))
                def _():
                    row = begin - starts[k] + offsets[k]
                    owns[b][...] = xs[b][k][pl.ds(pl.multiple_of(row, 16), tok_here), :]

        if last:
            expert = where_ref[chips]
            square = (tok_here, tok_here)
            row_at = lax.broadcasted_iota(jnp.int32, (head, tok_here), 0)
            diagonal = lax.broadcasted_iota(jnp.int32, square, 0) == lax.broadcasted_iota(
                jnp.int32, square, 1
            )

            def column(row, values):
                named = (row_at >= row) & (row_at < row + 3)
                along = jnp.sum(jnp.where(named, values, 0.0), axis=0, keepdims=True)
                return jnp.sum(jnp.where(diagonal, along, 0.0), axis=1, keepdims=True)

            for d in range(chips):
                values = tops[d][:head, :tok_here].astype(jnp.float32)
                at = pl.multiple_of(where_ref[d] * tok_here, tok_here)
                column_ref[pl.ds(at, tok_here), 0:1] = column(3 * (expert + 1), values)
            for q in range(chips):
                span = slice(q * tok_here, (q + 1) * tok_here)
                total = tops[0][:head, span].astype(jnp.float32)
                for d in range(1, chips):
                    total = total + tops[d][:head, span].astype(jnp.float32)
                mean = column(0, total) / model_width
                column_ref[span, 1:2] = lax.rsqrt(mean + epsilon)

        scaled = []
        for k, size in enumerate(sizes):
            for b in range(count):
                values = xs[b][k][offsets[k] : offsets[k] + size, :].astype(jnp.float32)
                scale = scale_ref[where_ref[positions[b]]]
                scaled.append((values * scale).astype(jnp.bfloat16))
        acts = {}
        for which in range(4):
            cols = slice(which * hidden_here, (which + 1) * hidden_here)
            for b in range(count):
                if not last:
                    copies[which, b].wait()
            for k, size in enumerate(sizes):
                span = slice(starts[k], starts[k] + size)
                total = None if first else acc_in[span, cols]
                for b in range(count):
                    if last:
                        table = stored[0][which]
                    else:
                        table = table_ref[which * count + b]
                    product = jnp.dot(
                        scaled[k * count + b], table, preferred_element_type=jnp.float32
                    )
                    total = product if total is None else total + product
                if not last:
                    acc_out[span, cols] = total
                elif which % 2 == 0:
                    acts[k] = total
                else:
                    gain, inv_rms = column_ref[span, 0:1], column_ref[span, 1:2]
                    gate_act, up_act = acts[k] * inv_rms, total * inv_rms
                    act = gate_act * jax.nn.sigmoid(gate_act) * up_act * gain
                    core = which // 2
                    out_cols = slice(core * hidden_here, (core + 1) * hidden_here)
                    hidden_ref[span, out_cols] = act.astype(jnp.bfloat16)
        for copy in later:
            copy.wait()
        for part in range(2) if last else ():
            chosen = [k for k, (_, at) in enumerate(leading[1]) if at == part]
            rows = [where_ref[leading[1][k][0]] * tok_here for k in chosen]
            rows = [hidden_ref[pl.ds(pl.multiple_of(at, tok_here), tok_here), :] for at in rows]
            out = jnp.dot(
                jnp.concatenate(rows, axis=0),
                product_ref[:, part * half : (part + 1) * half],
                preferred_element_type=jnp.float32,
            ).astype(jnp.bfloat16)
            for at, k in enumerate(chosen):
                leads[k][...] = out[at * tok_here : (at + 1) * tok_here, :]

    operands = [where] + [piece for block in parts for piece in block]
    operands.append(norm_gain)
    distant = [] if last else list(range(len(operands), len(operands) + len(tables)))
    operands.extend(tables)
    aliases = {}
    if not first:
        if not last:
            aliases = {len(operands): count}
        operands.append(carried)
    out_shape = [jax.ShapeDtypeStruct((tok_here, width), jnp.bfloat16)] * count
    if last:
        operands.extend(headers)
        operands.append(leading[0])
        out_shape.append(jax.ShapeDtypeStruct((tokens, both), jnp.bfloat16))
        out_shape.extend(
            [jax.ShapeDtypeStruct((tok_here, half), jnp.bfloat16)] * len(leading[1])
        )
    else:
        out_shape.append(jax.ShapeDtypeStruct((tokens, 2 * both), jnp.float32))
    if ahead:
        for source in ahead[1]:
            distant.append(len(operands))
            operands.append(source)
        out_shape.append(jax.ShapeDtypeStruct((4, width, hidden_here), jnp.bfloat16))
        out_shape.append(jax.ShapeDtypeStruct((both, model_width), jnp.bfloat16))
    if last:
        scratch = [pltpu.VMEM((tokens, 2), jnp.float32)]
    else:
        scratch = [
            pltpu.VMEM((slots, width, hidden_here), jnp.bfloat16),
            pltpu.SemaphoreType.DMA((slots + 6,)),
        ]
    made = local_call(
        kernel,
        out_shape,
        operands,
        flops=COST_SCALE * 4 * count * tokens * width * both,
        bytes_accessed=count * width * (tokens + 2 * both) * 2 + tokens * both * 16,
        aliases=aliases,
        scratch=scratch,
        far=distant,
    )
    return made[:count], made[count:]


def contribution(where, hidden, down, part):
    tokens, units = hidden.shape
    half = down.shape[1] // 2
    tile = 512 if half % 512 == 0 else half

    def kernel(where_ref, hidden_ref, down_ref, out_ref):
        for start in range(0, half, tile):
            out = jnp.dot(
                hidden_ref[...],
                down_ref[:, part * half + start : part * half + start + tile],
                preferred_element_type=jnp.float32,
            )
            out_ref[:, start : start + tile] = out.astype(jnp.bfloat16)

    return local_call(
        kernel,
        jax.ShapeDtypeStruct((tokens, half), jnp.bfloat16),
        [where, hidden, down],
        flops=2 * tokens * units * half,
        bytes_accessed=2 * half * (units + tokens),
    )


def add_rows(where, position, table, moved):
    rows, width = moved.shape

    def kernel(where_ref, table_ref, moved_ref, out_ref):
        at = pl.multiple_of(where_ref[position] * rows, rows)
        total = table_ref[pl.ds(at, rows), :].astype(jnp.float32)
        out_ref[...] = (total + moved_ref[...].astype(jnp.float32)).astype(jnp.bfloat16)

    return local_call(
        kernel,
        jax.ShapeDtypeStruct((rows, width), jnp.bfloat16),
        [where, table, moved],
        flops=rows * width,
        bytes_accessed=rows * width * 6,
    )


def collect(where, positions, pieces):
    rows, width = pieces[0].shape
    model_width = len(pieces) * width

    def kernel(where_ref, *refs):
        for k, position in enumerate(positions):
            start = pl.multiple_of(where_ref[position] * width, width)
            refs[-1][:, pl.ds(start, width)] = refs[k][...]

    return local_call(
        kernel,
        jax.ShapeDtypeStruct((rows, model_width), jnp.bfloat16),
        [where, *pieces],
        flops=rows * model_width,
        bytes_accessed=rows * model_width * 4,
    )


def final_sum(where, stream, tables, arrived):
    rows, model_width = stream.shape
    half = model_width // 2
    came = [value for part in arrived for value in part]

    def kernel(where_ref, stream_ref, *refs):
        out_ref = refs[-1]
        at = pl.multiple_of(where_ref[0] * rows, rows)
        for part in range(2):
            cols = slice(part * half, (part + 1) * half)
            total = stream_ref[:, cols].astype(jnp.float32)
            total = total + refs[part][pl.ds(at, rows), :].astype(jnp.float32)
            for k in range(len(arrived[part])):
                total = total + refs[2 + k + part * len(arrived[0])][...].astype(jnp.float32)
            out_ref[:, cols] = total.astype(jnp.bfloat16)

    return local_call(
        kernel,
        jax.ShapeDtypeStruct((rows, model_width), jnp.bfloat16),
        [where, stream, *tables, *came],
        flops=rows * model_width * 3,
        bytes_accessed=rows * model_width * 10,
    )


def dense_body(residual, attn_out, norm_gain, expert_routes, route_gain, w_gate, w_up, w_down):
    devices = lax.axis_size("ep")
    experts = devices // FSPLIT
    chips = devices // 2
    far = chips // 2
    tok_here = expert_routes.shape[0]
    feat_here = residual.shape[1]
    model_width = w_gate.shape[0]
    width = 2 * feat_here
    ring = ring_order(chips)
    me = lax.axis_index("ep")
    core = me % 2
    seen = [
        [ring[(ring.index(i // 2) + d) % chips] for d in range(chips)] + [i // FSPLIT]
        for i in range(devices)
    ]
    where = lax.dynamic_index_in_dim(jnp.asarray(seen, jnp.int32), me, 0, keepdims=False)

    stream_feat = (residual.astype(jnp.float32) + attn_out.astype(jnp.float32)).astype(jnp.bfloat16)
    by_core = stream_feat.reshape(chips, 2, tok_here, feat_here)
    swapped = swap_cores(lax.dynamic_index_in_dim(by_core, 1 - core, 1, keepdims=False))

    swapped, w_gate, w_up = lax.optimization_barrier((swapped, w_gate, w_up))
    tables = [pltpu.with_memory_space_constraint(table, pltpu.HBM) for table in (w_gate, w_up)]
    tables += [swap_cores(w_gate), swap_cores(w_up)]
    blocks = {0: first_blocks(by_core, swapped, expert_routes, route_gain, experts)}
    w_down = lax.optimization_barrier((swapped, w_down))[1]
    down = [pltpu.with_memory_space_constraint(w_down, pltpu.HBM), swap_cores(w_down)]

    for distance in range(1, far):
        for sign in (-1, 1):
            blocks[sign * distance] = ring_shift(blocks[sign * (distance - 1)], ring, -sign)
    groups = [[0]] + [[d, chips - d] for d in range(1, far)] + [[far]]
    gain_rows = norm_gain.reshape(chips, 1, width)
    carried, owns, positions, headers, ahead, leading = None, [], [], None, None, None
    for group in groups:
        parts = [[blocks[d if d <= far else d - chips]] for d in group]
        if group == [far]:
            parts = [blocks[far]]
            headers = [blocks[d if d < far else d - chips] for d in range(chips) if d != far]
            headers.insert(far, blocks[far][0])
            leading = (down, [(far, 0), (far, 1), (far - 1, 1), (chips - far + 1, 0)])
        if group == groups[-2]:
            ahead = (far, down)
        made, (carried, *rest) = accumulate(
            where, group, parts, gain_rows, tables, tok_here, carried, headers, ahead, leading
        )
        owns.extend(made)
        positions.extend(group)
        if group == groups[max(far - 2, 0)]:
            lower, upper, carried = lax.optimization_barrier(
                (blocks[1 - far], blocks[far - 1], carried)
            )
            cut = lower.shape[0] - far * tok_here
            blocks[far] = [ring_shift(lower[:cut], ring, 1), ring_shift(upper[cut:], ring, -1)]
        if group == groups[-2]:
            tables, down, ahead = [rest[0]], rest[1], None

    hidden, (lower, upper, after, before) = carried, rest
    moving = {1: [ring_shift(lower, ring, 1), None], -1: [None, ring_shift(upper, ring, -1)]}
    second = {1: ring_shift(after, ring, 1), -1: ring_shift(before, ring, -1)}
    stream_rows = collect(where, positions, owns)
    stream_rows, hidden = lax.optimization_barrier((stream_rows, hidden))
    everything = [contribution(where, hidden, down, part) for part in range(2)]
    for distance in range(far - 1, 0, -1):
        for sign, order in ((1, (1, 0)), (-1, (0, 1))):
            position = (sign * distance) % chips
            sent = [None, None]
            for part in order:
                if moving[sign][part] is None:
                    sent[part] = second[sign]
                else:
                    value = add_rows(where, position, everything[part], moving[sign][part])
                    sent[part] = ring_shift(value, ring, sign)
            moving[sign] = sent
    arrived = [
        [moving[sign][part] for sign in (1, -1) if moving[sign][part] is not None]
        for part in range(2)
    ]
    return final_sum(where, stream_rows, everything, arrived)


def body(residual, attn_out, norm_gain, expert_routes, route_gain, w_gate, w_up, w_down):
    tok_here, route_slots = expert_routes.shape
    devices = lax.axis_size("ep")
    capacity = route_slots * tok_here // (devices // FSPLIT)
    dense = capacity >= tok_here and devices % 8 == 0
    dense = dense and devices * tok_here <= 4 * residual.shape[1]
    chosen = dense_body if dense else routed_body
    return chosen(residual, attn_out, norm_gain, expert_routes, route_gain, w_gate, w_up, w_down)


def solution(mesh):
    in_specs = (
        P("groups", "ep"),
        P("groups", "ep"),
        P(),
        P(("groups", "ep"), None),
        P(("groups", "ep"), None),
        P(None, "ep"),
        P(None, "ep"),
        P("ep", None),
    )
    out_specs = P(("groups", "ep"), None)
    return jax.shard_map(body, mesh=mesh, in_specs=in_specs, out_specs=out_specs, check_vma=False)
```

```python
import jax
import jax.numpy as jnp
from jax import lax
from jax.experimental import pallas as pl
from jax.experimental.pallas import tpu as pltpu
from jax.sharding import PartitionSpec as P

FSPLIT = 8


epsilon = 1e-06


def normalize(stream_rows, norm_gain):
    values = stream_rows.astype(jnp.float32)
    inv_rms = lax.rsqrt(jnp.mean(values * values, axis=-1, keepdims=True) + epsilon)
    return (values * inv_rms * norm_gain).astype(jnp.bfloat16)


def route_match(routes, experts, capacity):
    flat_ids = routes.reshape(-1)
    onehot = (flat_ids[:, None] == jnp.arange(experts, dtype=jnp.int32)[None, :]).astype(jnp.int32)
    earlier = jnp.cumsum(onehot, axis=0) - onehot
    slot_pos = jnp.sum(earlier * onehot, axis=1)
    slot_code = jnp.where(flat_ids < experts, flat_ids * capacity + slot_pos, -1)
    target = jnp.arange(experts * capacity, dtype=jnp.int32)
    return slot_code[None, :] == target[:, None]


def selection(routes, experts, capacity):
    matched = route_match(routes, experts, capacity).astype(jnp.int32)
    return matched.reshape(experts * capacity, routes.shape[0], routes.shape[1]).sum(axis=2)


def gain_table(routes, route_gain, experts, capacity):
    matched = route_match(routes, experts, capacity)
    weighted = jnp.where(matched, route_gain.reshape(-1)[None, :], 0.0)
    return weighted.reshape(experts * capacity, routes.shape[0], routes.shape[1]).sum(axis=2).T


def expert_rows(normed, w_gate, w_up, w_down):
    gate_act = jnp.dot(normed, w_gate, preferred_element_type=jnp.float32)
    up_act = jnp.dot(normed, w_up, preferred_element_type=jnp.float32)
    hidden = (jax.nn.silu(gate_act) * up_act).astype(jnp.bfloat16)
    return jnp.dot(hidden, w_down, preferred_element_type=jnp.float32).astype(jnp.bfloat16)


def routed_body(residual, attn_out, norm_gain, expert_routes, route_gain, w_gate, w_up, w_down):
    devices = lax.axis_size("ep")
    tok_here = expert_routes.shape[0]
    route_slots = expert_routes.shape[1]
    experts = devices // FSPLIT
    capacity = route_slots * tok_here // experts
    model_width = w_gate.shape[0]
    stream_feat = (residual.astype(jnp.float32) + attn_out.astype(jnp.float32)).astype(jnp.bfloat16)
    stream_rows = lax.all_to_all(stream_feat, "ep", split_axis=0, concat_axis=1, tiled=True)
    combine_weights = gain_table(expert_routes, route_gain, experts, capacity)
    normed_rows = normalize(stream_rows, norm_gain)
    select = selection(expert_routes, experts, capacity).astype(jnp.bfloat16)
    per_expert = jnp.dot(select, normed_rows, preferred_element_type=jnp.float32).astype(
        jnp.bfloat16
    )
    per_expert = per_expert.reshape(experts, 1, capacity, model_width)
    outgoing = jnp.broadcast_to(per_expert, (experts, FSPLIT, capacity, model_width))
    outgoing = outgoing.reshape(devices, capacity, model_width)
    received = lax.all_to_all(outgoing, "ep", split_axis=0, concat_axis=0, tiled=True)
    slot_count = received.shape[1]
    partial_value = expert_rows(received.reshape(-1, model_width), w_gate, w_up, w_down)
    partial_value = partial_value.reshape(devices, slot_count, model_width)
    returned = lax.all_to_all(partial_value, "ep", split_axis=0, concat_axis=0, tiled=True)
    summed = (
        returned.reshape(experts, FSPLIT, capacity, model_width).astype(jnp.float32).sum(axis=1)
    )
    summed = summed.reshape(experts * capacity, model_width)
    routed_sum = jnp.dot(combine_weights, summed, precision=lax.Precision.HIGHEST)
    return (stream_rows.astype(jnp.float32) + routed_sum).astype(jnp.bfloat16)


def ring_order(chips):
    return list(range(0, chips, 2)) + list(reversed(range(1, chips, 2)))


def swap_cores(value):
    return lax.ppermute(value, "ep", [(i, i ^ 1) for i in range(lax.axis_size("ep"))])


def ring_shift(value, ring, step):
    chips = len(ring)
    pairs = [
        (2 * ring[i] + core, 2 * ring[(i + step) % chips] + core)
        for i in range(chips)
        for core in range(2)
    ]
    return lax.ppermute(value, "ep", pairs)


COST_SCALE = 3
VMEM_BYTES = 20 * 1024 * 1024
IN_VMEM = pl.BlockSpec(memory_space=pltpu.VMEM)
IN_SMEM = pl.BlockSpec(memory_space=pltpu.SMEM)
IN_HBM = pl.BlockSpec(memory_space=pltpu.HBM)


def local_call(
    kernel, out_shape, operands, flops, bytes_accessed, aliases=None, scratch=(), far=()
):
    return pl.pallas_call(
        kernel,
        out_shape=out_shape,
        in_specs=[
            IN_SMEM if value.ndim == 1 else IN_HBM if k in far else IN_VMEM
            for k, value in enumerate(operands)
        ],
        out_specs=jax.tree.map(
            lambda made: IN_SMEM if made.dtype == jnp.int32 else IN_VMEM, out_shape
        ),
        scratch_shapes=list(scratch),
        input_output_aliases=aliases or {},
        compiler_params=pltpu.CompilerParams(vmem_limit_bytes=VMEM_BYTES),
        cost_estimate=pl.CostEstimate(
            flops=flops, bytes_accessed=bytes_accessed, transcendentals=0
        ),
    )(*operands)


def first_blocks(stream, swapped, routes, route_gain, experts):
    chips, _, tok_here, feat_here = stream.shape
    width = 2 * feat_here
    tokens = chips * tok_here
    head = -(-3 * (experts + 1) // 16) * 16

    def kernel(stream_ref, swapped_ref, routes_ref, gain_ref, out_ref):
        core = lax.rem(lax.axis_index("ep"), 2)
        square = (tok_here, tok_here)
        diagonal = lax.broadcasted_iota(jnp.int32, square, 0) == lax.broadcasted_iota(
            jnp.int32, square, 1
        )

        def along(column):
            return jnp.sum(jnp.where(diagonal, column, 0.0), axis=0, keepdims=True)

        def split(left):
            for _ in range(3):
                piece = left.astype(jnp.bfloat16).astype(jnp.float32)
                left = left - piece
                yield piece

        row_at = lax.broadcasted_iota(jnp.int32, (head, tok_here), 0)
        for q in range(chips):
            mine = stream_ref[q, core]
            other = swapped_ref[q]
            left = jnp.where(core == 0, mine, other)
            right = jnp.where(core == 0, other, mine)
            at = head + q * tok_here
            out_ref[at : at + tok_here, :] = jnp.concatenate([left, right], axis=1)
            left, right = left.astype(jnp.float32), right.astype(jnp.float32)
            squares = jnp.sum(left * left + right * right, axis=1, keepdims=True)
            top = jnp.zeros((head, tok_here), jnp.float32)
            for row, piece in enumerate(split(along(squares))):
                top = jnp.where(row_at == row, piece, top)
            if q == 0:
                for expert in range(experts):
                    gains = jnp.where(routes_ref[...] == expert, gain_ref[...], 0.0)
                    gains = jnp.sum(gains, axis=1, keepdims=True)
                    for row, piece in enumerate(split(along(gains))):
                        top = jnp.where(row_at == 3 * (expert + 1) + row, piece, top)
            out_ref[:head, q * tok_here : (q + 1) * tok_here] = top.astype(jnp.bfloat16)
        if width > tokens:
            out_ref[:head, tokens:] = jnp.zeros((head, width - tokens), jnp.bfloat16)

    return local_call(
        kernel,
        jax.ShapeDtypeStruct((head + tokens, width), jnp.bfloat16),
        [stream, swapped, routes, route_gain],
        flops=4 * tokens * width,
        bytes_accessed=4 * tokens * width,
    )


def accumulate(
    where, positions, parts, norm_gain, tables, tok_here, carried, headers, ahead, leading
):
    count = len(positions)
    width = parts[0][0].shape[1]
    chips = norm_gain.shape[0]
    model_width = chips * width
    hidden_here = tables[0].shape[-1]
    both = 2 * hidden_here
    half = model_width // 2
    tokens = chips * tok_here
    sizes = [piece.shape[0] for piece in parts[0]]
    head = sum(sizes) - tokens
    offsets = [head] + [0] * (len(sizes) - 1)
    sizes = [size - at for size, at in zip(sizes, offsets)]
    starts = [sum(sizes[:k]) for k in range(len(sizes))]
    last = headers is not None
    first = carried is None
    slots = 0 if last else 4 * count
    side = 128

    def kernel(where_ref, *refs):
        refs = list(refs)
        xs = [[refs.pop(0) for _ in sizes] for _ in range(count)]
        scale_ref = refs.pop(0)
        stored = [refs.pop(0) for _ in tables]
        acc_in = None if first else refs.pop(0)
        tops = [refs.pop(0) for _ in headers] if last else []
        sources = [refs.pop(0) for _ in ahead[1]] if ahead else []
        product_ref = refs.pop(0) if leading else None
        owns = [refs.pop(0) for _ in range(count)]
        if last:
            hidden_ref = refs.pop(0)
            leads = [refs.pop(0) for _ in leading[1]]
        else:
            acc_out = refs.pop(0)
        if ahead:
            next_ref, down_ref = refs.pop(0), refs.pop(0)
        if last:
            column_ref = refs.pop(0)
        else:
            table_ref, sems = refs.pop(0), refs.pop(0)

        def fetch(which, position, target, sem):
            row = pl.multiple_of(where_ref[position] * width, width)
            copy = pltpu.make_async_copy(stored[which].at[pl.ds(row, width), :], target, sem)
            copy.start()
            return copy

        copies, later = {}, []
        if not last:
            for which in range(4):
                for b in range(count):
                    slot = which * count + b
                    copies[which, b] = fetch(
                        which, positions[b], table_ref.at[slot], sems.at[slot]
                    )
        if ahead:
            for which in range(4):
                later.append(fetch(which, ahead[0], next_ref.at[which], sems.at[slots + which]))
            for k, source in enumerate(sources):
                target = down_ref.at[k * hidden_here : (k + 1) * hidden_here, :]
                copy = pltpu.make_async_copy(source, target, sems.at[slots + 4 + k])
                copy.start()
                later.append(copy)
        begin = where_ref[0] * tok_here
        for b in range(count):
            for k, size in enumerate(sizes):

                @pl.when((begin >= starts[k]) & (begin < starts[k] + size))
                def _():
                    row = begin - starts[k] + offsets[k]
                    owns[b][...] = xs[b][k][pl.ds(pl.multiple_of(row, 16), tok_here), :]

        if last:
            over_rows = (((0,), (0,)), ((), ()))
            gain_row = 3 * (where_ref[chips] + 1)
            row_at = lax.broadcasted_iota(jnp.int32, (head, side), 0)
            named = ((row_at >= gain_row) & (row_at < gain_row + 3)).astype(jnp.bfloat16)
            row_at = lax.rem(lax.broadcasted_iota(jnp.int32, (chips * head, side), 0), head)
            ones = (row_at < 3).astype(jnp.bfloat16)
            for d in range(chips):
                gains = lax.dot_general(
                    tops[d][:head, :tok_here],
                    named,
                    over_rows,
                    preferred_element_type=jnp.float32,
                )
                at = pl.multiple_of(where_ref[d] * tok_here, tok_here)
                column_ref[pl.ds(at, tok_here), 0:1] = gains[:, 0:1]
            squares = lax.dot_general(
                jnp.concatenate([top[:head, :tokens] for top in tops], axis=0),
                ones,
                over_rows,
                preferred_element_type=jnp.float32,
            )
            column_ref[:, 1:2] = lax.rsqrt(squares[:, 0:1] / model_width + epsilon)

        scaled = []
        for k, size in enumerate(sizes):
            for b in range(count):
                values = xs[b][k][offsets[k] : offsets[k] + size, :].astype(jnp.float32)
                scale = scale_ref[where_ref[positions[b]]]
                scaled.append((values * scale).astype(jnp.bfloat16))
        acts = {}
        for which in range(4):
            cols = slice(which * hidden_here, (which + 1) * hidden_here)
            for b in range(count):
                if not last:
                    copies[which, b].wait()
            for k, size in enumerate(sizes):
                span = slice(starts[k], starts[k] + size)
                total = None if first else acc_in[span, cols]
                for b in range(count):
                    if last:
                        table = stored[0][which]
                    else:
                        table = table_ref[which * count + b]
                    product = jnp.dot(
                        scaled[k * count + b], table, preferred_element_type=jnp.float32
                    )
                    total = product if total is None else total + product
                if not last:
                    acc_out[span, cols] = total
                elif which % 2 == 0:
                    acts[k] = total
                else:
                    gain, inv_rms = column_ref[span, 0:1], column_ref[span, 1:2]
                    gate_act, up_act = acts[k] * inv_rms, total * inv_rms
                    act = gate_act * jax.nn.sigmoid(gate_act) * up_act * gain
                    core = which // 2
                    out_cols = slice(core * hidden_here, (core + 1) * hidden_here)
                    hidden_ref[span, out_cols] = act.astype(jnp.bfloat16)
        for copy in later:
            copy.wait()
        for part in range(2) if last else ():
            chosen = [k for k, (_, at) in enumerate(leading[1]) if at == part]
            rows = [where_ref[leading[1][k][0]] * tok_here for k in chosen]
            rows = [hidden_ref[pl.ds(pl.multiple_of(at, tok_here), tok_here), :] for at in rows]
            out = jnp.dot(
                jnp.concatenate(rows, axis=0),
                product_ref[:, part * half : (part + 1) * half],
                preferred_element_type=jnp.float32,
            ).astype(jnp.bfloat16)
            for at, k in enumerate(chosen):
                leads[k][...] = out[at * tok_here : (at + 1) * tok_here, :]

    operands = [where] + [piece for block in parts for piece in block]
    operands.append(norm_gain)
    distant = [] if last else list(range(len(operands), len(operands) + len(tables)))
    operands.extend(tables)
    aliases = {}
    if not first:
        if not last:
            aliases = {len(operands): count}
        operands.append(carried)
    out_shape = [jax.ShapeDtypeStruct((tok_here, width), jnp.bfloat16)] * count
    if last:
        operands.extend(headers)
        operands.append(leading[0])
        out_shape.append(jax.ShapeDtypeStruct((tokens, both), jnp.bfloat16))
        out_shape.extend(
            [jax.ShapeDtypeStruct((tok_here, half), jnp.bfloat16)] * len(leading[1])
        )
    else:
        out_shape.append(jax.ShapeDtypeStruct((tokens, 2 * both), jnp.float32))
    if ahead:
        for source in ahead[1]:
            distant.append(len(operands))
            operands.append(source)
        out_shape.append(jax.ShapeDtypeStruct((4, width, hidden_here), jnp.bfloat16))
        out_shape.append(jax.ShapeDtypeStruct((both, model_width), jnp.bfloat16))
    if last:
        scratch = [pltpu.VMEM((tokens, 2), jnp.float32)]
    else:
        scratch = [
            pltpu.VMEM((slots, width, hidden_here), jnp.bfloat16),
            pltpu.SemaphoreType.DMA((slots + 6,)),
        ]
    made = local_call(
        kernel,
        out_shape,
        operands,
        flops=COST_SCALE * 4 * count * tokens * width * both,
        bytes_accessed=count * width * (tokens + 2 * both) * 2 + tokens * both * 16,
        aliases=aliases,
        scratch=scratch,
        far=distant,
    )
    return made[:count], made[count:]


def contribution(where, hidden, down, part):
    tokens, units = hidden.shape
    half = down.shape[1] // 2
    tile = 512 if half % 512 == 0 else half

    def kernel(where_ref, hidden_ref, down_ref, out_ref):
        for start in range(0, half, tile):
            out = jnp.dot(
                hidden_ref[...],
                down_ref[:, part * half + start : part * half + start + tile],
                preferred_element_type=jnp.float32,
            )
            out_ref[:, start : start + tile] = out.astype(jnp.bfloat16)

    return local_call(
        kernel,
        jax.ShapeDtypeStruct((tokens, half), jnp.bfloat16),
        [where, hidden, down],
        flops=2 * tokens * units * half,
        bytes_accessed=2 * half * (units + tokens),
    )


def add_rows(where, position, table, moved):
    rows, width = moved.shape

    def kernel(where_ref, table_ref, moved_ref, out_ref):
        at = pl.multiple_of(where_ref[position] * rows, rows)
        total = table_ref[pl.ds(at, rows), :].astype(jnp.float32)
        out_ref[...] = (total + moved_ref[...].astype(jnp.float32)).astype(jnp.bfloat16)

    return local_call(
        kernel,
        jax.ShapeDtypeStruct((rows, width), jnp.bfloat16),
        [where, table, moved],
        flops=rows * width,
        bytes_accessed=rows * width * 6,
    )


def collect(where, positions, pieces):
    rows, width = pieces[0].shape
    model_width = len(pieces) * width

    def kernel(where_ref, *refs):
        for k, position in enumerate(positions):
            start = pl.multiple_of(where_ref[position] * width, width)
            refs[-1][:, pl.ds(start, width)] = refs[k][...]

    return local_call(
        kernel,
        jax.ShapeDtypeStruct((rows, model_width), jnp.bfloat16),
        [where, *pieces],
        flops=rows * model_width,
        bytes_accessed=rows * model_width * 4,
    )


def final_sum(where, stream, tables, arrived):
    rows, model_width = stream.shape
    half = model_width // 2
    came = [value for part in arrived for value in part]

    steps = 2 if half % 256 == 0 else 1
    tile = half // steps

    def kernel(where_ref, stream_ref, *refs):
        out_ref, sum_ref, sems = refs[-3:]
        at = pl.multiple_of(where_ref[0] * rows, rows)
        writes = []
        for part in range(2):
            for step in range(steps):
                here = slice(step * tile, (step + 1) * tile)
                cols = slice(part * half + step * tile, part * half + (step + 1) * tile)
                total = stream_ref[:, cols].astype(jnp.float32)
                total = total + refs[part][pl.ds(at, rows), here].astype(jnp.float32)
                for k in range(len(arrived[part])):
                    value = refs[2 + k + part * len(arrived[0])][:, here]
                    total = total + value.astype(jnp.float32)
                sum_ref[:, cols] = total.astype(jnp.bfloat16)
                writes.append(
                    pltpu.make_async_copy(
                        sum_ref.at[:, cols], out_ref.at[:, cols], sems.at[len(writes)]
                    )
                )
                writes[-1].start()
        for write in writes:
            write.wait()

    operands = [where, stream, *tables, *came]
    return pl.pallas_call(
        kernel,
        in_specs=[IN_SMEM] + [IN_VMEM] * (len(operands) - 1),
        out_specs=IN_HBM,
        out_shape=jax.ShapeDtypeStruct((rows, model_width), jnp.bfloat16),
        scratch_shapes=[
            pltpu.VMEM((rows, model_width), jnp.bfloat16),
            pltpu.SemaphoreType.DMA((2 * steps,)),
        ],
        compiler_params=pltpu.CompilerParams(vmem_limit_bytes=VMEM_BYTES),
        cost_estimate=pl.CostEstimate(
            flops=rows * model_width * 3, bytes_accessed=rows * model_width * 10, transcendentals=0
        ),
    )(*operands)


def dense_body(residual, attn_out, norm_gain, expert_routes, route_gain, w_gate, w_up, w_down):
    devices = lax.axis_size("ep")
    experts = devices // FSPLIT
    chips = devices // 2
    far = chips // 2
    tok_here = expert_routes.shape[0]
    feat_here = residual.shape[1]
    model_width = w_gate.shape[0]
    width = 2 * feat_here
    ring = ring_order(chips)
    me = lax.axis_index("ep")
    core = me % 2
    seen = [
        [ring[(ring.index(i // 2) + d) % chips] for d in range(chips)] + [i // FSPLIT]
        for i in range(devices)
    ]
    where = lax.dynamic_index_in_dim(jnp.asarray(seen, jnp.int32), me, 0, keepdims=False)

    stream_feat = (residual.astype(jnp.float32) + attn_out.astype(jnp.float32)).astype(jnp.bfloat16)
    by_core = stream_feat.reshape(chips, 2, tok_here, feat_here)
    swapped = swap_cores(lax.dynamic_index_in_dim(by_core, 1 - core, 1, keepdims=False))

    swapped, w_gate, w_up = lax.optimization_barrier((swapped, w_gate, w_up))
    tables = [pltpu.with_memory_space_constraint(table, pltpu.HBM) for table in (w_gate, w_up)]
    tables += [swap_cores(w_gate), swap_cores(w_up)]
    blocks = {0: first_blocks(by_core, swapped, expert_routes, route_gain, experts)}
    w_down = lax.optimization_barrier((swapped, w_down))[1]
    down = [pltpu.with_memory_space_constraint(w_down, pltpu.HBM), swap_cores(w_down)]

    for distance in range(1, far):
        for sign in (-1, 1):
            blocks[sign * distance] = ring_shift(blocks[sign * (distance - 1)], ring, -sign)
    groups = [[0]] + [[d, chips - d] for d in range(1, far)] + [[far]]
    gain_rows = norm_gain.reshape(chips, 1, width)
    carried, owns, positions, headers, ahead, leading = None, [], [], None, None, None
    for group in groups:
        parts = [[blocks[d if d <= far else d - chips]] for d in group]
        if group == [far]:
            parts = [blocks[far]]
            headers = [blocks[d if d < far else d - chips] for d in range(chips) if d != far]
            headers.insert(far, blocks[far][0])
            leading = (down, [(far, 0), (far, 1), (far - 1, 1), (chips - far + 1, 0)])
        if group == groups[-2]:
            ahead = (far, down)
        made, (carried, *rest) = accumulate(
            where, group, parts, gain_rows, tables, tok_here, carried, headers, ahead, leading
        )
        owns.extend(made)
        positions.extend(group)
        if group == groups[max(far - 2, 0)]:
            lower, upper, carried = lax.optimization_barrier(
                (blocks[1 - far], blocks[far - 1], carried)
            )
            cut = lower.shape[0] - far * tok_here
            blocks[far] = [ring_shift(lower[:cut], ring, 1), ring_shift(upper[cut:], ring, -1)]
        if group == groups[-2]:
            tables, down, ahead = [rest[0]], rest[1], None

    hidden, (lower, upper, after, before) = carried, rest
    moving = {1: [ring_shift(lower, ring, 1), None], -1: [None, ring_shift(upper, ring, -1)]}
    second = {1: ring_shift(after, ring, 1), -1: ring_shift(before, ring, -1)}
    stream_rows = collect(where, positions, owns)
    stream_rows, hidden = lax.optimization_barrier((stream_rows, hidden))
    everything = [contribution(where, hidden, down, part) for part in range(2)]
    for distance in range(far - 1, 0, -1):
        for sign, order in ((1, (1, 0)), (-1, (0, 1))):
            position = (sign * distance) % chips
            sent = [None, None]
            for part in order:
                if moving[sign][part] is None:
                    sent[part] = second[sign]
                else:
                    value = add_rows(where, position, everything[part], moving[sign][part])
                    sent[part] = ring_shift(value, ring, sign)
            moving[sign] = sent
    arrived = [
        [moving[sign][part] for sign in (1, -1) if moving[sign][part] is not None]
        for part in range(2)
    ]
    return final_sum(where, stream_rows, everything, arrived)


def body(residual, attn_out, norm_gain, expert_routes, route_gain, w_gate, w_up, w_down):
    tok_here, route_slots = expert_routes.shape
    devices = lax.axis_size("ep")
    capacity = route_slots * tok_here // (devices // FSPLIT)
    dense = capacity >= tok_here and devices % 8 == 0
    dense = dense and devices * tok_here <= 4 * residual.shape[1]
    chosen = dense_body if dense else routed_body
    return chosen(residual, attn_out, norm_gain, expert_routes, route_gain, w_gate, w_up, w_down)


def solution(mesh):
    in_specs = (
        P("groups", "ep"),
        P("groups", "ep"),
        P(),
        P(("groups", "ep"), None),
        P(("groups", "ep"), None),
        P(None, "ep"),
        P(None, "ep"),
        P("ep", None),
    )
    out_specs = P(("groups", "ep"), None)
    return jax.shard_map(body, mesh=mesh, in_specs=in_specs, out_specs=out_specs, check_vma=False)
```

```python
import jax
import jax.numpy as jnp
from jax import lax
from jax.experimental import pallas as pl
from jax.experimental.pallas import tpu as pltpu
from jax.sharding import PartitionSpec as P

FSPLIT = 8


epsilon = 1e-06


def normalize(stream_rows, norm_gain):
    values = stream_rows.astype(jnp.float32)
    inv_rms = lax.rsqrt(jnp.mean(values * values, axis=-1, keepdims=True) + epsilon)
    return (values * inv_rms * norm_gain).astype(jnp.bfloat16)


def route_match(routes, experts, capacity):
    flat_ids = routes.reshape(-1)
    onehot = (flat_ids[:, None] == jnp.arange(experts, dtype=jnp.int32)[None, :]).astype(jnp.int32)
    earlier = jnp.cumsum(onehot, axis=0) - onehot
    slot_pos = jnp.sum(earlier * onehot, axis=1)
    slot_code = jnp.where(flat_ids < experts, flat_ids * capacity + slot_pos, -1)
    target = jnp.arange(experts * capacity, dtype=jnp.int32)
    return slot_code[None, :] == target[:, None]


def selection(routes, experts, capacity):
    matched = route_match(routes, experts, capacity).astype(jnp.int32)
    return matched.reshape(experts * capacity, routes.shape[0], routes.shape[1]).sum(axis=2)


def gain_table(routes, route_gain, experts, capacity):
    matched = route_match(routes, experts, capacity)
    weighted = jnp.where(matched, route_gain.reshape(-1)[None, :], 0.0)
    return weighted.reshape(experts * capacity, routes.shape[0], routes.shape[1]).sum(axis=2).T


def expert_rows(normed, w_gate, w_up, w_down):
    gate_act = jnp.dot(normed, w_gate, preferred_element_type=jnp.float32)
    up_act = jnp.dot(normed, w_up, preferred_element_type=jnp.float32)
    hidden = (jax.nn.silu(gate_act) * up_act).astype(jnp.bfloat16)
    return jnp.dot(hidden, w_down, preferred_element_type=jnp.float32).astype(jnp.bfloat16)


def routed_body(residual, attn_out, norm_gain, expert_routes, route_gain, w_gate, w_up, w_down):
    devices = lax.axis_size("ep")
    tok_here = expert_routes.shape[0]
    route_slots = expert_routes.shape[1]
    experts = devices // FSPLIT
    capacity = route_slots * tok_here // experts
    model_width = w_gate.shape[0]
    stream_feat = (residual.astype(jnp.float32) + attn_out.astype(jnp.float32)).astype(jnp.bfloat16)
    stream_rows = lax.all_to_all(stream_feat, "ep", split_axis=0, concat_axis=1, tiled=True)
    combine_weights = gain_table(expert_routes, route_gain, experts, capacity)
    normed_rows = normalize(stream_rows, norm_gain)
    select = selection(expert_routes, experts, capacity).astype(jnp.bfloat16)
    per_expert = jnp.dot(select, normed_rows, preferred_element_type=jnp.float32).astype(
        jnp.bfloat16
    )
    per_expert = per_expert.reshape(experts, 1, capacity, model_width)
    outgoing = jnp.broadcast_to(per_expert, (experts, FSPLIT, capacity, model_width))
    outgoing = outgoing.reshape(devices, capacity, model_width)
    received = lax.all_to_all(outgoing, "ep", split_axis=0, concat_axis=0, tiled=True)
    slot_count = received.shape[1]
    partial_value = expert_rows(received.reshape(-1, model_width), w_gate, w_up, w_down)
    partial_value = partial_value.reshape(devices, slot_count, model_width)
    returned = lax.all_to_all(partial_value, "ep", split_axis=0, concat_axis=0, tiled=True)
    summed = (
        returned.reshape(experts, FSPLIT, capacity, model_width).astype(jnp.float32).sum(axis=1)
    )
    summed = summed.reshape(experts * capacity, model_width)
    routed_sum = jnp.dot(combine_weights, summed, precision=lax.Precision.HIGHEST)
    return (stream_rows.astype(jnp.float32) + routed_sum).astype(jnp.bfloat16)


def ring_order(chips):
    return list(range(0, chips, 2)) + list(reversed(range(1, chips, 2)))


def swap_cores(value):
    return lax.ppermute(value, "ep", [(i, i ^ 1) for i in range(lax.axis_size("ep"))])


def ring_shift(value, ring, step):
    chips = len(ring)
    pairs = [
        (2 * ring[i] + core, 2 * ring[(i + step) % chips] + core)
        for i in range(chips)
        for core in range(2)
    ]
    return lax.ppermute(value, "ep", pairs)


COST_SCALE = 3
VMEM_BYTES = 20 * 1024 * 1024
IN_VMEM = pl.BlockSpec(memory_space=pltpu.VMEM)
IN_SMEM = pl.BlockSpec(memory_space=pltpu.SMEM)
IN_HBM = pl.BlockSpec(memory_space=pltpu.HBM)


def local_call(
    kernel, out_shape, operands, flops, bytes_accessed, aliases=None, scratch=(), far=()
):
    return pl.pallas_call(
        kernel,
        out_shape=out_shape,
        in_specs=[
            IN_SMEM if value.ndim == 1 else IN_HBM if k in far else IN_VMEM
            for k, value in enumerate(operands)
        ],
        out_specs=jax.tree.map(
            lambda made: IN_SMEM if made.dtype == jnp.int32 else IN_VMEM, out_shape
        ),
        scratch_shapes=list(scratch),
        input_output_aliases=aliases or {},
        compiler_params=pltpu.CompilerParams(vmem_limit_bytes=VMEM_BYTES),
        cost_estimate=pl.CostEstimate(
            flops=flops, bytes_accessed=bytes_accessed, transcendentals=0
        ),
    )(*operands)


def first_blocks(stream, swapped, routes, route_gain, experts):
    chips, _, tok_here, feat_here = stream.shape
    width = 2 * feat_here
    tokens = chips * tok_here
    head = -(-3 * (experts + 1) // 16) * 16

    def kernel(stream_ref, swapped_ref, routes_ref, gain_ref, out_ref):
        core = lax.rem(lax.axis_index("ep"), 2)
        square = (tok_here, tok_here)
        diagonal = lax.broadcasted_iota(jnp.int32, square, 0) == lax.broadcasted_iota(
            jnp.int32, square, 1
        )

        def along(column):
            return jnp.sum(jnp.where(diagonal, column, 0.0), axis=0, keepdims=True)

        def split(left):
            for _ in range(3):
                piece = left.astype(jnp.bfloat16).astype(jnp.float32)
                left = left - piece
                yield piece

        row_at = lax.broadcasted_iota(jnp.int32, (head, tok_here), 0)
        for q in range(chips):
            mine = stream_ref[q, core]
            other = swapped_ref[q]
            left = jnp.where(core == 0, mine, other)
            right = jnp.where(core == 0, other, mine)
            at = head + q * tok_here
            out_ref[at : at + tok_here, :] = jnp.concatenate([left, right], axis=1)
            left, right = left.astype(jnp.float32), right.astype(jnp.float32)
            squares = jnp.sum(left * left + right * right, axis=1, keepdims=True)
            top = jnp.zeros((head, tok_here), jnp.float32)
            for row, piece in enumerate(split(along(squares))):
                top = jnp.where(row_at == row, piece, top)
            if q == 0:
                for expert in range(experts):
                    gains = jnp.where(routes_ref[...] == expert, gain_ref[...], 0.0)
                    gains = jnp.sum(gains, axis=1, keepdims=True)
                    for row, piece in enumerate(split(along(gains))):
                        top = jnp.where(row_at == 3 * (expert + 1) + row, piece, top)
            out_ref[:head, q * tok_here : (q + 1) * tok_here] = top.astype(jnp.bfloat16)
        if width > tokens:
            out_ref[:head, tokens:] = jnp.zeros((head, width - tokens), jnp.bfloat16)

    return local_call(
        kernel,
        jax.ShapeDtypeStruct((head + tokens, width), jnp.bfloat16),
        [stream, swapped, routes, route_gain],
        flops=4 * tokens * width,
        bytes_accessed=4 * tokens * width,
    )


def accumulate(
    where, positions, parts, norm_gain, tables, tok_here, carried, headers, ahead, leading
):
    count = len(positions)
    width = parts[0][0].shape[1]
    chips = norm_gain.shape[0]
    model_width = chips * width
    hidden_here = tables[0].shape[-1]
    both = 2 * hidden_here
    half = model_width // 2
    tokens = chips * tok_here
    sizes = [piece.shape[0] for piece in parts[0]]
    head = sum(sizes) - tokens
    offsets = [head] + [0] * (len(sizes) - 1)
    sizes = [size - at for size, at in zip(sizes, offsets)]
    starts = [sum(sizes[:k]) for k in range(len(sizes))]
    last = headers is not None
    first = carried is None
    slots = 0 if last else 4 * count

    def kernel(where_ref, *refs):
        refs = list(refs)
        xs = [[refs.pop(0) for _ in sizes] for _ in range(count)]
        scale_ref = refs.pop(0)
        stored = [refs.pop(0) for _ in tables]
        acc_in = None if first else refs.pop(0)
        tops = [refs.pop(0) for _ in headers] if last else []
        sources = [refs.pop(0) for _ in ahead[1]] if ahead else []
        product_ref = refs.pop(0) if leading else None
        owns = [refs.pop(0) for _ in range(count)]
        if last:
            hidden_ref = refs.pop(0)
            leads = [refs.pop(0) for _ in leading[1]]
        else:
            acc_out = refs.pop(0)
        if ahead:
            next_ref, down_ref = refs.pop(0), refs.pop(0)
        if last:
            column_ref = refs.pop(0)
        else:
            table_ref, sems = refs.pop(0), refs.pop(0)

        def fetch(which, position, target, sem):
            row = pl.multiple_of(where_ref[position] * width, width)
            copy = pltpu.make_async_copy(stored[which].at[pl.ds(row, width), :], target, sem)
            copy.start()
            return copy

        copies, later = {}, []
        if not last:
            for which in range(4):
                for b in range(count):
                    slot = which * count + b
                    copies[which, b] = fetch(
                        which, positions[b], table_ref.at[slot], sems.at[slot]
                    )
        if ahead:
            for which in range(4):
                later.append(fetch(which, ahead[0], next_ref.at[which], sems.at[slots + which]))
            for k, source in enumerate(sources):
                target = down_ref.at[k * hidden_here : (k + 1) * hidden_here, :]
                copy = pltpu.make_async_copy(source, target, sems.at[slots + 4 + k])
                copy.start()
                later.append(copy)
        begin = where_ref[0] * tok_here
        for b in range(count):
            for k, size in enumerate(sizes):

                @pl.when((begin >= starts[k]) & (begin < starts[k] + size))
                def _():
                    row = begin - starts[k] + offsets[k]
                    owns[b][...] = xs[b][k][pl.ds(pl.multiple_of(row, 16), tok_here), :]

        if last:
            expert = where_ref[chips]
            square = (tok_here, tok_here)
            row_at = lax.broadcasted_iota(jnp.int32, (head, tok_here), 0)
            diagonal = lax.broadcasted_iota(jnp.int32, square, 0) == lax.broadcasted_iota(
                jnp.int32, square, 1
            )

            def column(row, values):
                named = (row_at >= row) & (row_at < row + 3)
                along = jnp.sum(jnp.where(named, values, 0.0), axis=0, keepdims=True)
                return jnp.sum(jnp.where(diagonal, along, 0.0), axis=1, keepdims=True)

            for d in range(chips):
                values = tops[d][:head, :tok_here].astype(jnp.float32)
                at = pl.multiple_of(where_ref[d] * tok_here, tok_here)
                column_ref[pl.ds(at, tok_here), 0:1] = column(3 * (expert + 1), values)
            for q in range(chips):
                span = slice(q * tok_here, (q + 1) * tok_here)
                total = tops[0][:head, span].astype(jnp.float32)
                for d in range(1, chips):
                    total = total + tops[d][:head, span].astype(jnp.float32)
                mean = column(0, total) / model_width
                column_ref[span, 1:2] = lax.rsqrt(mean + epsilon)

        scaled = []
        for k, size in enumerate(sizes):
            for b in range(count):
                values = xs[b][k][offsets[k] : offsets[k] + size, :].astype(jnp.float32)
                scale = scale_ref[where_ref[positions[b]]]
                scaled.append((values * scale).astype(jnp.bfloat16))
        acts = {}
        for which in range(4):
            cols = slice(which * hidden_here, (which + 1) * hidden_here)
            for b in range(count):
                if not last:
                    copies[which, b].wait()
            for k, size in enumerate(sizes):
                span = slice(starts[k], starts[k] + size)
                total = None if first else acc_in[span, cols]
                for b in range(count):
                    if last:
                        table = stored[0][which]
                    else:
                        table = table_ref[which * count + b]
                    product = jnp.dot(
                        scaled[k * count + b], table, preferred_element_type=jnp.float32
                    )
                    total = product if total is None else total + product
                if not last:
                    acc_out[span, cols] = total
                elif which % 2 == 0:
                    acts[k] = total
                else:
                    gain, inv_rms = column_ref[span, 0:1], column_ref[span, 1:2]
                    gate_act, up_act = acts[k] * inv_rms, total * inv_rms
                    act = gate_act * jax.nn.sigmoid(gate_act) * up_act * gain
                    core = which // 2
                    out_cols = slice(core * hidden_here, (core + 1) * hidden_here)
                    hidden_ref[span, out_cols] = act.astype(jnp.bfloat16)
        for copy in later:
            copy.wait()
        for part in range(2) if last else ():
            chosen = [k for k, (_, at) in enumerate(leading[1]) if at == part]
            rows = [where_ref[leading[1][k][0]] * tok_here for k in chosen]
            rows = [hidden_ref[pl.ds(pl.multiple_of(at, tok_here), tok_here), :] for at in rows]
            out = jnp.dot(
                jnp.concatenate(rows, axis=0),
                product_ref[:, part * half : (part + 1) * half],
                preferred_element_type=jnp.float32,
            ).astype(jnp.bfloat16)
            for at, k in enumerate(chosen):
                leads[k][...] = out[at * tok_here : (at + 1) * tok_here, :]

    operands = [where] + [piece for block in parts for piece in block]
    operands.append(norm_gain)
    distant = [] if last else list(range(len(operands), len(operands) + len(tables)))
    operands.extend(tables)
    aliases = {}
    if not first:
        if not last:
            aliases = {len(operands): count}
        operands.append(carried)
    out_shape = [jax.ShapeDtypeStruct((tok_here, width), jnp.bfloat16)] * count
    if last:
        operands.extend(headers)
        operands.append(leading[0])
        out_shape.append(jax.ShapeDtypeStruct((tokens, both), jnp.bfloat16))
        out_shape.extend(
            [jax.ShapeDtypeStruct((tok_here, half), jnp.bfloat16)] * len(leading[1])
        )
    else:
        out_shape.append(jax.ShapeDtypeStruct((tokens, 2 * both), jnp.float32))
    if ahead:
        for source in ahead[1]:
            distant.append(len(operands))
            operands.append(source)
        out_shape.append(jax.ShapeDtypeStruct((4, width, hidden_here), jnp.bfloat16))
        out_shape.append(jax.ShapeDtypeStruct((both, model_width), jnp.bfloat16))
    if last:
        scratch = [pltpu.VMEM((tokens, 2), jnp.float32)]
    else:
        scratch = [
            pltpu.VMEM((slots, width, hidden_here), jnp.bfloat16),
            pltpu.SemaphoreType.DMA((slots + 6,)),
        ]
    made = local_call(
        kernel,
        out_shape,
        operands,
        flops=COST_SCALE * 4 * count * tokens * width * both,
        bytes_accessed=count * width * (tokens + 2 * both) * 2 + tokens * both * 16,
        aliases=aliases,
        scratch=scratch,
        far=distant,
    )
    return made[:count], made[count:]


def contribution(where, hidden, down, part):
    tokens, units = hidden.shape
    half = down.shape[1] // 2
    tile = 512 if half % 512 == 0 else half

    def kernel(where_ref, hidden_ref, down_ref, out_ref):
        for start in range(0, half, tile):
            out = jnp.dot(
                hidden_ref[...],
                down_ref[:, part * half + start : part * half + start + tile],
                preferred_element_type=jnp.float32,
            )
            out_ref[:, start : start + tile] = out.astype(jnp.bfloat16)

    return local_call(
        kernel,
        jax.ShapeDtypeStruct((tokens, half), jnp.bfloat16),
        [where, hidden, down],
        flops=2 * tokens * units * half,
        bytes_accessed=2 * half * (units + tokens),
    )


def add_rows(where, position, table, moved):
    rows, width = moved.shape

    def kernel(where_ref, table_ref, moved_ref, out_ref):
        at = pl.multiple_of(where_ref[position] * rows, rows)
        total = table_ref[pl.ds(at, rows), :].astype(jnp.float32)
        out_ref[...] = (total + moved_ref[...].astype(jnp.float32)).astype(jnp.bfloat16)

    return local_call(
        kernel,
        jax.ShapeDtypeStruct((rows, width), jnp.bfloat16),
        [where, table, moved],
        flops=rows * width,
        bytes_accessed=rows * width * 6,
    )


def collect(where, positions, pieces):
    rows, width = pieces[0].shape
    model_width = len(pieces) * width

    def kernel(where_ref, *refs):
        for k, position in enumerate(positions):
            start = pl.multiple_of(where_ref[position] * width, width)
            refs[-1][:, pl.ds(start, width)] = refs[k][...]

    return local_call(
        kernel,
        jax.ShapeDtypeStruct((rows, model_width), jnp.bfloat16),
        [where, *pieces],
        flops=rows * model_width,
        bytes_accessed=rows * model_width * 4,
    )


def final_sum(where, stream, tables, arrived):
    rows, model_width = stream.shape
    half = model_width // 2
    came = [value for part in arrived for value in part]

    def kernel(where_ref, stream_ref, *refs):
        out_ref = refs[-1]
        at = pl.multiple_of(where_ref[0] * rows, rows)
        for part in range(2):
            cols = slice(part * half, (part + 1) * half)
            total = stream_ref[:, cols].astype(jnp.float32)
            total = total + refs[part][pl.ds(at, rows), :].astype(jnp.float32)
            for k in range(len(arrived[part])):
                total = total + refs[2 + k + part * len(arrived[0])][...].astype(jnp.float32)
            out_ref[:, cols] = total.astype(jnp.bfloat16)

    return local_call(
        kernel,
        jax.ShapeDtypeStruct((rows, model_width), jnp.bfloat16),
        [where, stream, *tables, *came],
        flops=rows * model_width * 3,
        bytes_accessed=rows * model_width * 10,
    )


def dense_body(residual, attn_out, norm_gain, expert_routes, route_gain, w_gate, w_up, w_down):
    devices = lax.axis_size("ep")
    experts = devices // FSPLIT
    chips = devices // 2
    far = chips // 2
    tok_here = expert_routes.shape[0]
    feat_here = residual.shape[1]
    model_width = w_gate.shape[0]
    width = 2 * feat_here
    ring = ring_order(chips)
    me = lax.axis_index("ep")
    core = me % 2
    seen = [
        [ring[(ring.index(i // 2) + d) % chips] for d in range(chips)] + [i // FSPLIT]
        for i in range(devices)
    ]
    where = lax.dynamic_index_in_dim(jnp.asarray(seen, jnp.int32), me, 0, keepdims=False)

    stream_feat = (residual.astype(jnp.float32) + attn_out.astype(jnp.float32)).astype(jnp.bfloat16)
    by_core = stream_feat.reshape(chips, 2, tok_here, feat_here)
    swapped = swap_cores(lax.dynamic_index_in_dim(by_core, 1 - core, 1, keepdims=False))

    blocks = {0: first_blocks(by_core, swapped, expert_routes, route_gain, experts)}

    blocks[0], w_gate, w_up, w_down = lax.optimization_barrier((blocks[0], w_gate, w_up, w_down))
    tables = [pltpu.with_memory_space_constraint(table, pltpu.HBM) for table in (w_gate, w_up)]
    tables += [swap_cores(w_gate), swap_cores(w_up)]
    down = [pltpu.with_memory_space_constraint(w_down, pltpu.HBM), swap_cores(w_down)]

    for distance in range(1, far):
        for sign in (-1, 1):
            blocks[sign * distance] = ring_shift(blocks[sign * (distance - 1)], ring, -sign)
    groups = [[0]] + [[d, chips - d] for d in range(1, far)] + [[far]]
    gain_rows = norm_gain.reshape(chips, 1, width)
    carried, owns, positions, headers, ahead, leading = None, [], [], None, None, None
    for group in groups:
        parts = [[blocks[d if d <= far else d - chips]] for d in group]
        if group == [far]:
            parts = [blocks[far]]
            headers = [blocks[d if d < far else d - chips] for d in range(chips) if d != far]
            headers.insert(far, blocks[far][0])
            leading = (down, [(far, 0), (far, 1), (far - 1, 1), (chips - far + 1, 0)])
        if group == groups[-2]:
            ahead = (far, down)
        made, (carried, *rest) = accumulate(
            where, group, parts, gain_rows, tables, tok_here, carried, headers, ahead, leading
        )
        owns.extend(made)
        positions.extend(group)
        if group == groups[max(far - 2, 0)]:
            lower, carried = lax.optimization_barrier((blocks[1 - far], carried))
            cut = lower.shape[0] - far * tok_here
            blocks[far] = [ring_shift(lower[:cut], ring, 1)]
            upper, carried = lax.optimization_barrier((blocks[far - 1], carried))
            blocks[far].append(ring_shift(upper[cut:], ring, -1))
        if group == groups[-2]:
            tables, down, ahead = [rest[0]], rest[1], None

    hidden, (lower, upper, after, before) = carried, rest
    moving = {1: [ring_shift(lower, ring, 1), None], -1: [None, ring_shift(upper, ring, -1)]}
    second = {1: ring_shift(after, ring, 1), -1: ring_shift(before, ring, -1)}
    stream_rows = collect(where, positions, owns)
    everything = [contribution(where, hidden, down, part) for part in range(2)]
    for distance in range(far - 1, 0, -1):
        for sign, order in ((1, (1, 0)), (-1, (0, 1))):
            position = (sign * distance) % chips
            sent = [None, None]
            for part in order:
                if moving[sign][part] is None:
                    sent[part] = second[sign]
                else:
                    value = add_rows(where, position, everything[part], moving[sign][part])
                    sent[part] = ring_shift(value, ring, sign)
            moving[sign] = sent
    arrived = [
        [moving[sign][part] for sign in (1, -1) if moving[sign][part] is not None]
        for part in range(2)
    ]
    return final_sum(where, stream_rows, everything, arrived)


def body(residual, attn_out, norm_gain, expert_routes, route_gain, w_gate, w_up, w_down):
    tok_here, route_slots = expert_routes.shape
    devices = lax.axis_size("ep")
    capacity = route_slots * tok_here // (devices // FSPLIT)
    dense = capacity >= tok_here and devices % 8 == 0
    dense = dense and devices * tok_here <= 4 * residual.shape[1]
    chosen = dense_body if dense else routed_body
    return chosen(residual, attn_out, norm_gain, expert_routes, route_gain, w_gate, w_up, w_down)


def solution(mesh):
    in_specs = (
        P("groups", "ep"),
        P("groups", "ep"),
        P(),
        P(("groups", "ep"), None),
        P(("groups", "ep"), None),
        P(None, "ep"),
        P(None, "ep"),
        P("ep", None),
    )
    out_specs = P(("groups", "ep"), None)
    return jax.shard_map(body, mesh=mesh, in_specs=in_specs, out_specs=out_specs, check_vma=False)
```

```python
import jax
import jax.numpy as jnp
from jax import lax
from jax.experimental import pallas as pl
from jax.experimental.pallas import tpu as pltpu
from jax.sharding import PartitionSpec as P

FSPLIT = 8


epsilon = 1e-06


def normalize(stream_rows, norm_gain):
    values = stream_rows.astype(jnp.float32)
    inv_rms = lax.rsqrt(jnp.mean(values * values, axis=-1, keepdims=True) + epsilon)
    return (values * inv_rms * norm_gain).astype(jnp.bfloat16)


def route_match(routes, experts, capacity):
    flat_ids = routes.reshape(-1)
    onehot = (flat_ids[:, None] == jnp.arange(experts, dtype=jnp.int32)[None, :]).astype(jnp.int32)
    earlier = jnp.cumsum(onehot, axis=0) - onehot
    slot_pos = jnp.sum(earlier * onehot, axis=1)
    slot_code = jnp.where(flat_ids < experts, flat_ids * capacity + slot_pos, -1)
    target = jnp.arange(experts * capacity, dtype=jnp.int32)
    return slot_code[None, :] == target[:, None]


def selection(routes, experts, capacity):
    matched = route_match(routes, experts, capacity).astype(jnp.int32)
    return matched.reshape(experts * capacity, routes.shape[0], routes.shape[1]).sum(axis=2)


def gain_table(routes, route_gain, experts, capacity):
    matched = route_match(routes, experts, capacity)
    weighted = jnp.where(matched, route_gain.reshape(-1)[None, :], 0.0)
    return weighted.reshape(experts * capacity, routes.shape[0], routes.shape[1]).sum(axis=2).T


def expert_rows(normed, w_gate, w_up, w_down):
    gate_act = jnp.dot(normed, w_gate, preferred_element_type=jnp.float32)
    up_act = jnp.dot(normed, w_up, preferred_element_type=jnp.float32)
    hidden = (jax.nn.silu(gate_act) * up_act).astype(jnp.bfloat16)
    return jnp.dot(hidden, w_down, preferred_element_type=jnp.float32).astype(jnp.bfloat16)


def routed_body(residual, attn_out, norm_gain, expert_routes, route_gain, w_gate, w_up, w_down):
    devices = lax.axis_size("ep")
    tok_here = expert_routes.shape[0]
    route_slots = expert_routes.shape[1]
    experts = devices // FSPLIT
    capacity = route_slots * tok_here // experts
    model_width = w_gate.shape[0]
    stream_feat = (residual.astype(jnp.float32) + attn_out.astype(jnp.float32)).astype(jnp.bfloat16)
    stream_rows = lax.all_to_all(stream_feat, "ep", split_axis=0, concat_axis=1, tiled=True)
    combine_weights = gain_table(expert_routes, route_gain, experts, capacity)
    normed_rows = normalize(stream_rows, norm_gain)
    select = selection(expert_routes, experts, capacity).astype(jnp.bfloat16)
    per_expert = jnp.dot(select, normed_rows, preferred_element_type=jnp.float32).astype(
        jnp.bfloat16
    )
    per_expert = per_expert.reshape(experts, 1, capacity, model_width)
    outgoing = jnp.broadcast_to(per_expert, (experts, FSPLIT, capacity, model_width))
    outgoing = outgoing.reshape(devices, capacity, model_width)
    received = lax.all_to_all(outgoing, "ep", split_axis=0, concat_axis=0, tiled=True)
    slot_count = received.shape[1]
    partial_value = expert_rows(received.reshape(-1, model_width), w_gate, w_up, w_down)
    partial_value = partial_value.reshape(devices, slot_count, model_width)
    returned = lax.all_to_all(partial_value, "ep", split_axis=0, concat_axis=0, tiled=True)
    summed = (
        returned.reshape(experts, FSPLIT, capacity, model_width).astype(jnp.float32).sum(axis=1)
    )
    summed = summed.reshape(experts * capacity, model_width)
    routed_sum = jnp.dot(combine_weights, summed, precision=lax.Precision.HIGHEST)
    return (stream_rows.astype(jnp.float32) + routed_sum).astype(jnp.bfloat16)


def ring_order(chips):
    return list(range(0, chips, 2)) + list(reversed(range(1, chips, 2)))


def swap_cores(value):
    return lax.ppermute(value, "ep", [(i, i ^ 1) for i in range(lax.axis_size("ep"))])


def ring_shift(value, ring, step):
    chips = len(ring)
    pairs = [
        (2 * ring[i] + core, 2 * ring[(i + step) % chips] + core)
        for i in range(chips)
        for core in range(2)
    ]
    return lax.ppermute(value, "ep", pairs)


COST_SCALE = 3
VMEM_BYTES = 20 * 1024 * 1024
IN_VMEM = pl.BlockSpec(memory_space=pltpu.VMEM)
IN_SMEM = pl.BlockSpec(memory_space=pltpu.SMEM)
IN_HBM = pl.BlockSpec(memory_space=pltpu.HBM)


def local_call(
    kernel, out_shape, operands, flops, bytes_accessed, aliases=None, scratch=(), far=()
):
    return pl.pallas_call(
        kernel,
        out_shape=out_shape,
        in_specs=[
            IN_SMEM if value.ndim == 1 else IN_HBM if k in far else IN_VMEM
            for k, value in enumerate(operands)
        ],
        out_specs=jax.tree.map(
            lambda made: IN_SMEM if made.dtype == jnp.int32 else IN_VMEM, out_shape
        ),
        scratch_shapes=list(scratch),
        input_output_aliases=aliases or {},
        compiler_params=pltpu.CompilerParams(vmem_limit_bytes=VMEM_BYTES),
        cost_estimate=pl.CostEstimate(
            flops=flops, bytes_accessed=bytes_accessed, transcendentals=0
        ),
    )(*operands)


def first_blocks(stream, swapped, routes, route_gain, experts, norm_gain, w_gate, w_up):
    chips, _, tok_here, feat_here = stream.shape
    width = 2 * feat_here
    tokens = chips * tok_here
    head = -(-3 * (experts + 1) // 16) * 16

    hidden_here = w_gate.shape[1]

    def kernel(stream_ref, swapped_ref, routes_ref, gain_ref, scale_ref, *refs):
        gate_ref, up_ref, out_ref, early_ref, table_ref, sems = refs
        chip = lax.div(lax.axis_index("ep"), 2)
        row = pl.multiple_of(chip * width, width)
        copies = [
            pltpu.make_async_copy(ref.at[pl.ds(row, width), :], table_ref.at[k], sems.at[k])
            for k, ref in enumerate((gate_ref, up_ref))
        ]
        core = lax.rem(lax.axis_index("ep"), 2)

        @pl.when(core == 1)
        def _():
            for copy in copies:
                copy.start()

        square = (tok_here, tok_here)
        diagonal = lax.broadcasted_iota(jnp.int32, square, 0) == lax.broadcasted_iota(
            jnp.int32, square, 1
        )

        def along(column):
            return jnp.sum(jnp.where(diagonal, column, 0.0), axis=0, keepdims=True)

        def split(left):
            for _ in range(3):
                piece = left.astype(jnp.bfloat16).astype(jnp.float32)
                left = left - piece
                yield piece

        row_at = lax.broadcasted_iota(jnp.int32, (head, tok_here), 0)
        for q in range(chips):
            mine = stream_ref[q, core]
            other = swapped_ref[q]
            left = jnp.where(core == 0, mine, other)
            right = jnp.where(core == 0, other, mine)
            at = head + q * tok_here
            out_ref[at : at + tok_here, :] = jnp.concatenate([left, right], axis=1)
            left, right = left.astype(jnp.float32), right.astype(jnp.float32)
            squares = jnp.sum(left * left + right * right, axis=1, keepdims=True)
            top = jnp.zeros((head, tok_here), jnp.float32)
            for row, piece in enumerate(split(along(squares))):
                top = jnp.where(row_at == row, piece, top)
            if q == 0:
                for expert in range(experts):
                    gains = jnp.where(routes_ref[...] == expert, gain_ref[...], 0.0)
                    gains = jnp.sum(gains, axis=1, keepdims=True)
                    for row, piece in enumerate(split(along(gains))):
                        top = jnp.where(row_at == 3 * (expert + 1) + row, piece, top)
            out_ref[:head, q * tok_here : (q + 1) * tok_here] = top.astype(jnp.bfloat16)
        if width > tokens:
            out_ref[:head, tokens:] = jnp.zeros((head, width - tokens), jnp.bfloat16)

        @pl.when(core == 1)
        def _():
            for copy in copies:
                copy.wait()
            for k in range(2):
                span = slice(k * tokens // 2, (k + 1) * tokens // 2)
                at = head + k * tokens // 2
                values = out_ref[at : at + tokens // 2, :].astype(jnp.float32)
                scaled = (values * scale_ref[chip]).astype(jnp.bfloat16)
                for which in range(2):
                    cols = slice(which * hidden_here, (which + 1) * hidden_here)
                    early_ref[span, cols] = jnp.dot(
                        scaled, table_ref[which], preferred_element_type=jnp.float32
                    )

    operands = [stream, swapped, routes, route_gain, norm_gain, w_gate, w_up]
    return local_call(
        kernel,
        [
            jax.ShapeDtypeStruct((head + tokens, width), jnp.bfloat16),
            jax.ShapeDtypeStruct((tokens, 2 * hidden_here), jnp.float32),
        ],
        operands,
        flops=4 * tokens * width,
        bytes_accessed=4 * tokens * width,
        scratch=[
            pltpu.VMEM((2, width, hidden_here), jnp.bfloat16),
            pltpu.SemaphoreType.DMA((2,)),
        ],
        far=[5, 6],
    )


def accumulate(
    where, positions, parts, norm_gain, tables, tok_here, carried, headers, ahead, leading, early
):
    count = len(positions)
    width = parts[0][0].shape[1]
    chips = norm_gain.shape[0]
    model_width = chips * width
    hidden_here = tables[0].shape[-1]
    both = 2 * hidden_here
    half = model_width // 2
    tokens = chips * tok_here
    sizes = [piece.shape[0] for piece in parts[0]]
    head = sum(sizes) - tokens
    offsets = [head] + [0] * (len(sizes) - 1)
    sizes = [size - at for size, at in zip(sizes, offsets)]
    starts = [sum(sizes[:k]) for k in range(len(sizes))]
    last = headers is not None
    first = carried is None
    slots = 0 if last else 4 * count

    def kernel(where_ref, *refs):
        refs = list(refs)
        xs = [[refs.pop(0) for _ in sizes] for _ in range(count)]
        scale_ref = refs.pop(0)
        stored = [refs.pop(0) for _ in tables]
        acc_in = None if first else refs.pop(0)
        early_ref = refs.pop(0) if first else None
        tops = [refs.pop(0) for _ in headers] if last else []
        sources = [refs.pop(0) for _ in ahead[1]] if ahead else []
        product_ref = refs.pop(0) if leading else None
        owns = [refs.pop(0) for _ in range(count)]
        if last:
            hidden_ref = refs.pop(0)
            leads = [refs.pop(0) for _ in leading[1]]
        else:
            acc_out = refs.pop(0)
        if ahead:
            next_ref, down_ref = refs.pop(0), refs.pop(0)
        if last:
            column_ref = refs.pop(0)
        else:
            table_ref, sems = refs.pop(0), refs.pop(0)

        def fetch(which, position, target, sem):
            row = pl.multiple_of(where_ref[position] * width, width)
            copy = pltpu.make_async_copy(stored[which].at[pl.ds(row, width), :], target, sem)
            copy.start()
            return copy

        copies, later = {}, []
        if not last:
            for which in range(4):
                for b in range(count):
                    slot = which * count + b
                    copies[which, b] = fetch(
                        which, positions[b], table_ref.at[slot], sems.at[slot]
                    )
        if ahead:
            for which in range(4):
                later.append(fetch(which, ahead[0], next_ref.at[which], sems.at[slots + which]))
            for k, source in enumerate(sources):
                target = down_ref.at[k * hidden_here : (k + 1) * hidden_here, :]
                copy = pltpu.make_async_copy(source, target, sems.at[slots + 4 + k])
                copy.start()
                later.append(copy)
        begin = where_ref[0] * tok_here
        for b in range(count):
            for k, size in enumerate(sizes):

                @pl.when((begin >= starts[k]) & (begin < starts[k] + size))
                def _():
                    row = begin - starts[k] + offsets[k]
                    owns[b][...] = xs[b][k][pl.ds(pl.multiple_of(row, 16), tok_here), :]

        if last:
            expert = where_ref[chips]
            square = (tok_here, tok_here)
            row_at = lax.broadcasted_iota(jnp.int32, (head, tok_here), 0)
            diagonal = lax.broadcasted_iota(jnp.int32, square, 0) == lax.broadcasted_iota(
                jnp.int32, square, 1
            )

            def column(row, values):
                named = (row_at >= row) & (row_at < row + 3)
                along = jnp.sum(jnp.where(named, values, 0.0), axis=0, keepdims=True)
                return jnp.sum(jnp.where(diagonal, along, 0.0), axis=1, keepdims=True)

            for d in range(chips):
                values = tops[d][:head, :tok_here].astype(jnp.float32)
                at = pl.multiple_of(where_ref[d] * tok_here, tok_here)
                column_ref[pl.ds(at, tok_here), 0:1] = column(3 * (expert + 1), values)
            for q in range(chips):
                span = slice(q * tok_here, (q + 1) * tok_here)
                total = tops[0][:head, span].astype(jnp.float32)
                for d in range(1, chips):
                    total = total + tops[d][:head, span].astype(jnp.float32)
                mean = column(0, total) / model_width
                column_ref[span, 1:2] = lax.rsqrt(mean + epsilon)

        scaled = []
        for k, size in enumerate(sizes):
            for b in range(count):
                values = xs[b][k][offsets[k] : offsets[k] + size, :].astype(jnp.float32)
                scale = scale_ref[where_ref[positions[b]]]
                scaled.append((values * scale).astype(jnp.bfloat16))
        acts = {}
        for which in range(4):
            cols = slice(which * hidden_here, (which + 1) * hidden_here)
            for b in range(count):
                if not last:
                    copies[which, b].wait()
            if first and which < 2:
                on_second = lax.rem(lax.axis_index("ep"), 2) == 1

                @pl.when(on_second)
                def _(cols=cols):
                    acc_out[:, cols] = early_ref[:, cols]

                @pl.when(jnp.logical_not(on_second))
                def _(cols=cols, which=which):
                    acc_out[:, cols] = jnp.dot(
                        scaled[0], table_ref[which], preferred_element_type=jnp.float32
                    )

                continue
            for k, size in enumerate(sizes):
                span = slice(starts[k], starts[k] + size)
                total = None if first else acc_in[span, cols]
                for b in range(count):
                    if last:
                        table = stored[0][which]
                    else:
                        table = table_ref[which * count + b]
                    product = jnp.dot(
                        scaled[k * count + b], table, preferred_element_type=jnp.float32
                    )
                    total = product if total is None else total + product
                if not last:
                    acc_out[span, cols] = total
                elif which % 2 == 0:
                    acts[k] = total
                else:
                    gain, inv_rms = column_ref[span, 0:1], column_ref[span, 1:2]
                    gate_act, up_act = acts[k] * inv_rms, total * inv_rms
                    act = gate_act * jax.nn.sigmoid(gate_act) * up_act * gain
                    core = which // 2
                    out_cols = slice(core * hidden_here, (core + 1) * hidden_here)
                    hidden_ref[span, out_cols] = act.astype(jnp.bfloat16)
        for copy in later:
            copy.wait()
        for part in range(2) if last else ():
            chosen = [k for k, (_, at) in enumerate(leading[1]) if at == part]
            rows = [where_ref[leading[1][k][0]] * tok_here for k in chosen]
            rows = [hidden_ref[pl.ds(pl.multiple_of(at, tok_here), tok_here), :] for at in rows]
            out = jnp.dot(
                jnp.concatenate(rows, axis=0),
                product_ref[:, part * half : (part + 1) * half],
                preferred_element_type=jnp.float32,
            ).astype(jnp.bfloat16)
            for at, k in enumerate(chosen):
                leads[k][...] = out[at * tok_here : (at + 1) * tok_here, :]

    operands = [where] + [piece for block in parts for piece in block]
    operands.append(norm_gain)
    distant = [] if last else list(range(len(operands), len(operands) + len(tables)))
    operands.extend(tables)
    aliases = {}
    if not first:
        if not last:
            aliases = {len(operands): count}
        operands.append(carried)
    else:
        operands.append(early)
    out_shape = [jax.ShapeDtypeStruct((tok_here, width), jnp.bfloat16)] * count
    if last:
        operands.extend(headers)
        operands.append(leading[0])
        out_shape.append(jax.ShapeDtypeStruct((tokens, both), jnp.bfloat16))
        out_shape.extend(
            [jax.ShapeDtypeStruct((tok_here, half), jnp.bfloat16)] * len(leading[1])
        )
    else:
        out_shape.append(jax.ShapeDtypeStruct((tokens, 2 * both), jnp.float32))
    if ahead:
        for source in ahead[1]:
            distant.append(len(operands))
            operands.append(source)
        out_shape.append(jax.ShapeDtypeStruct((4, width, hidden_here), jnp.bfloat16))
        out_shape.append(jax.ShapeDtypeStruct((both, model_width), jnp.bfloat16))
    if last:
        scratch = [pltpu.VMEM((tokens, 2), jnp.float32)]
    else:
        scratch = [
            pltpu.VMEM((slots, width, hidden_here), jnp.bfloat16),
            pltpu.SemaphoreType.DMA((slots + 6,)),
        ]
    made = local_call(
        kernel,
        out_shape,
        operands,
        flops=COST_SCALE * 4 * count * tokens * width * both,
        bytes_accessed=count * width * (tokens + 2 * both) * 2 + tokens * both * 16,
        aliases=aliases,
        scratch=scratch,
        far=distant,
    )
    return made[:count], made[count:]


def contribution(where, hidden, down, part):
    tokens, units = hidden.shape
    half = down.shape[1] // 2
    tile = 512 if half % 512 == 0 else half

    def kernel(where_ref, hidden_ref, down_ref, out_ref):
        for start in range(0, half, tile):
            out = jnp.dot(
                hidden_ref[...],
                down_ref[:, part * half + start : part * half + start + tile],
                preferred_element_type=jnp.float32,
            )
            out_ref[:, start : start + tile] = out.astype(jnp.bfloat16)

    return local_call(
        kernel,
        jax.ShapeDtypeStruct((tokens, half), jnp.bfloat16),
        [where, hidden, down],
        flops=2 * tokens * units * half,
        bytes_accessed=2 * half * (units + tokens),
    )


def add_rows(where, position, table, moved):
    rows, width = moved.shape

    def kernel(where_ref, table_ref, moved_ref, out_ref):
        at = pl.multiple_of(where_ref[position] * rows, rows)
        total = table_ref[pl.ds(at, rows), :].astype(jnp.float32)
        out_ref[...] = (total + moved_ref[...].astype(jnp.float32)).astype(jnp.bfloat16)

    return local_call(
        kernel,
        jax.ShapeDtypeStruct((rows, width), jnp.bfloat16),
        [where, table, moved],
        flops=rows * width,
        bytes_accessed=rows * width * 6,
    )


def collect(where, positions, pieces):
    rows, width = pieces[0].shape
    model_width = len(pieces) * width

    def kernel(where_ref, *refs):
        for k, position in enumerate(positions):
            start = pl.multiple_of(where_ref[position] * width, width)
            refs[-1][:, pl.ds(start, width)] = refs[k][...]

    return local_call(
        kernel,
        jax.ShapeDtypeStruct((rows, model_width), jnp.bfloat16),
        [where, *pieces],
        flops=rows * model_width,
        bytes_accessed=rows * model_width * 4,
    )


def final_sum(where, stream, tables, arrived):
    rows, model_width = stream.shape
    half = model_width // 2
    came = [value for part in arrived for value in part]

    def kernel(where_ref, stream_ref, *refs):
        out_ref = refs[-1]
        at = pl.multiple_of(where_ref[0] * rows, rows)
        for part in range(2):
            cols = slice(part * half, (part + 1) * half)
            total = stream_ref[:, cols].astype(jnp.float32)
            total = total + refs[part][pl.ds(at, rows), :].astype(jnp.float32)
            for k in range(len(arrived[part])):
                total = total + refs[2 + k + part * len(arrived[0])][...].astype(jnp.float32)
            out_ref[:, cols] = total.astype(jnp.bfloat16)

    return local_call(
        kernel,
        jax.ShapeDtypeStruct((rows, model_width), jnp.bfloat16),
        [where, stream, *tables, *came],
        flops=rows * model_width * 3,
        bytes_accessed=rows * model_width * 10,
    )


def dense_body(residual, attn_out, norm_gain, expert_routes, route_gain, w_gate, w_up, w_down):
    devices = lax.axis_size("ep")
    experts = devices // FSPLIT
    chips = devices // 2
    far = chips // 2
    tok_here = expert_routes.shape[0]
    feat_here = residual.shape[1]
    model_width = w_gate.shape[0]
    width = 2 * feat_here
    ring = ring_order(chips)
    me = lax.axis_index("ep")
    core = me % 2
    seen = [
        [ring[(ring.index(i // 2) + d) % chips] for d in range(chips)] + [i // FSPLIT]
        for i in range(devices)
    ]
    where = lax.dynamic_index_in_dim(jnp.asarray(seen, jnp.int32), me, 0, keepdims=False)

    stream_feat = (residual.astype(jnp.float32) + attn_out.astype(jnp.float32)).astype(jnp.bfloat16)
    by_core = stream_feat.reshape(chips, 2, tok_here, feat_here)
    swapped = swap_cores(lax.dynamic_index_in_dim(by_core, 1 - core, 1, keepdims=False))

    gain_rows = norm_gain.reshape(chips, 1, width)
    swapped, w_gate, w_up, w_down = lax.optimization_barrier((swapped, w_gate, w_up, w_down))
    tables = [pltpu.with_memory_space_constraint(table, pltpu.HBM) for table in (w_gate, w_up)]
    block, early = first_blocks(
        by_core, swapped, expert_routes, route_gain, experts, gain_rows, *tables
    )
    blocks = {0: block}
    tables += [swap_cores(w_gate), swap_cores(w_up)]
    down = [pltpu.with_memory_space_constraint(w_down, pltpu.HBM), swap_cores(w_down)]

    for distance in range(1, far):
        for sign in (-1, 1):
            blocks[sign * distance] = ring_shift(blocks[sign * (distance - 1)], ring, -sign)
    groups = [[0]] + [[d, chips - d] for d in range(1, far)] + [[far]]
    carried, owns, positions, headers, ahead, leading = None, [], [], None, None, None
    for group in groups:
        parts = [[blocks[d if d <= far else d - chips]] for d in group]
        if group == [far]:
            parts = [blocks[far]]
            headers = [blocks[d if d < far else d - chips] for d in range(chips) if d != far]
            headers.insert(far, blocks[far][0])
            leading = (down, [(far, 0), (far, 1), (far - 1, 1), (chips - far + 1, 0)])
        if group == groups[-2]:
            ahead = (far, down)
        made, (carried, *rest) = accumulate(
            where, group, parts, gain_rows, tables, tok_here, carried, headers, ahead, leading, early
        )
        owns.extend(made)
        positions.extend(group)
        if group == groups[max(far - 2, 0)]:
            lower, carried = lax.optimization_barrier((blocks[1 - far], carried))
            cut = lower.shape[0] - far * tok_here
            blocks[far] = [ring_shift(lower[:cut], ring, 1)]
            upper, carried = lax.optimization_barrier((blocks[far - 1], carried))
            blocks[far].append(ring_shift(upper[cut:], ring, -1))
        if group == groups[-2]:
            tables, down, ahead = [rest[0]], rest[1], None

    hidden, (lower, upper, after, before) = carried, rest
    moving = {1: [ring_shift(lower, ring, 1), None], -1: [None, ring_shift(upper, ring, -1)]}
    second = {1: ring_shift(after, ring, 1), -1: ring_shift(before, ring, -1)}
    stream_rows = collect(where, positions, owns)
    everything = [contribution(where, hidden, down, part) for part in range(2)]
    for distance in range(far - 1, 0, -1):
        for sign, order in ((1, (1, 0)), (-1, (0, 1))):
            position = (sign * distance) % chips
            sent = [None, None]
            for part in order:
                if moving[sign][part] is None:
                    sent[part] = second[sign]
                else:
                    value = add_rows(where, position, everything[part], moving[sign][part])
                    sent[part] = ring_shift(value, ring, sign)
            moving[sign] = sent
    arrived = [
        [moving[sign][part] for sign in (1, -1) if moving[sign][part] is not None]
        for part in range(2)
    ]
    return final_sum(where, stream_rows, everything, arrived)


def body(residual, attn_out, norm_gain, expert_routes, route_gain, w_gate, w_up, w_down):
    tok_here, route_slots = expert_routes.shape
    devices = lax.axis_size("ep")
    capacity = route_slots * tok_here // (devices // FSPLIT)
    dense = capacity >= tok_here and devices % 8 == 0
    dense = dense and devices * tok_here <= 4 * residual.shape[1]
    chosen = dense_body if dense else routed_body
    return chosen(residual, attn_out, norm_gain, expert_routes, route_gain, w_gate, w_up, w_down)


def solution(mesh):
    in_specs = (
        P("groups", "ep"),
        P("groups", "ep"),
        P(),
        P(("groups", "ep"), None),
        P(("groups", "ep"), None),
        P(None, "ep"),
        P(None, "ep"),
        P("ep", None),
    )
    out_specs = P(("groups", "ep"), None)
    return jax.shard_map(body, mesh=mesh, in_specs=in_specs, out_specs=out_specs, check_vma=False)
```

```python
import jax
import jax.numpy as jnp
from jax import lax
from jax.experimental import pallas as pl
from jax.experimental.pallas import tpu as pltpu
from jax.sharding import PartitionSpec as P

FSPLIT = 8


epsilon = 1e-06


def normalize(stream_rows, norm_gain):
    values = stream_rows.astype(jnp.float32)
    inv_rms = lax.rsqrt(jnp.mean(values * values, axis=-1, keepdims=True) + epsilon)
    return (values * inv_rms * norm_gain).astype(jnp.bfloat16)


def route_match(routes, experts, capacity):
    flat_ids = routes.reshape(-1)
    onehot = (flat_ids[:, None] == jnp.arange(experts, dtype=jnp.int32)[None, :]).astype(jnp.int32)
    earlier = jnp.cumsum(onehot, axis=0) - onehot
    slot_pos = jnp.sum(earlier * onehot, axis=1)
    slot_code = jnp.where(flat_ids < experts, flat_ids * capacity + slot_pos, -1)
    target = jnp.arange(experts * capacity, dtype=jnp.int32)
    return slot_code[None, :] == target[:, None]


def selection(routes, experts, capacity):
    matched = route_match(routes, experts, capacity).astype(jnp.int32)
    return matched.reshape(experts * capacity, routes.shape[0], routes.shape[1]).sum(axis=2)


def gain_table(routes, route_gain, experts, capacity):
    matched = route_match(routes, experts, capacity)
    weighted = jnp.where(matched, route_gain.reshape(-1)[None, :], 0.0)
    return weighted.reshape(experts * capacity, routes.shape[0], routes.shape[1]).sum(axis=2).T


def expert_rows(normed, w_gate, w_up, w_down):
    gate_act = jnp.dot(normed, w_gate, preferred_element_type=jnp.float32)
    up_act = jnp.dot(normed, w_up, preferred_element_type=jnp.float32)
    hidden = (jax.nn.silu(gate_act) * up_act).astype(jnp.bfloat16)
    return jnp.dot(hidden, w_down, preferred_element_type=jnp.float32).astype(jnp.bfloat16)


def routed_body(residual, attn_out, norm_gain, expert_routes, route_gain, w_gate, w_up, w_down):
    devices = lax.axis_size("ep")
    tok_here = expert_routes.shape[0]
    route_slots = expert_routes.shape[1]
    experts = devices // FSPLIT
    capacity = route_slots * tok_here // experts
    model_width = w_gate.shape[0]
    stream_feat = (residual.astype(jnp.float32) + attn_out.astype(jnp.float32)).astype(jnp.bfloat16)
    stream_rows = lax.all_to_all(stream_feat, "ep", split_axis=0, concat_axis=1, tiled=True)
    combine_weights = gain_table(expert_routes, route_gain, experts, capacity)
    normed_rows = normalize(stream_rows, norm_gain)
    select = selection(expert_routes, experts, capacity).astype(jnp.bfloat16)
    per_expert = jnp.dot(select, normed_rows, preferred_element_type=jnp.float32).astype(
        jnp.bfloat16
    )
    per_expert = per_expert.reshape(experts, 1, capacity, model_width)
    outgoing = jnp.broadcast_to(per_expert, (experts, FSPLIT, capacity, model_width))
    outgoing = outgoing.reshape(devices, capacity, model_width)
    received = lax.all_to_all(outgoing, "ep", split_axis=0, concat_axis=0, tiled=True)
    slot_count = received.shape[1]
    partial_value = expert_rows(received.reshape(-1, model_width), w_gate, w_up, w_down)
    partial_value = partial_value.reshape(devices, slot_count, model_width)
    returned = lax.all_to_all(partial_value, "ep", split_axis=0, concat_axis=0, tiled=True)
    summed = (
        returned.reshape(experts, FSPLIT, capacity, model_width).astype(jnp.float32).sum(axis=1)
    )
    summed = summed.reshape(experts * capacity, model_width)
    routed_sum = jnp.dot(combine_weights, summed, precision=lax.Precision.HIGHEST)
    return (stream_rows.astype(jnp.float32) + routed_sum).astype(jnp.bfloat16)


def ring_order(chips):
    return list(range(0, chips, 2)) + list(reversed(range(1, chips, 2)))


def swap_cores(value):
    return lax.ppermute(value, "ep", [(i, i ^ 1) for i in range(lax.axis_size("ep"))])


def ring_shift(value, ring, step):
    chips = len(ring)
    pairs = [
        (2 * ring[i] + core, 2 * ring[(i + step) % chips] + core)
        for i in range(chips)
        for core in range(2)
    ]
    return lax.ppermute(value, "ep", pairs)


COST_SCALE = 3
VMEM_BYTES = 20 * 1024 * 1024
IN_VMEM = pl.BlockSpec(memory_space=pltpu.VMEM)
IN_SMEM = pl.BlockSpec(memory_space=pltpu.SMEM)
IN_HBM = pl.BlockSpec(memory_space=pltpu.HBM)


def local_call(
    kernel, out_shape, operands, flops, bytes_accessed, aliases=None, scratch=(), far=()
):
    return pl.pallas_call(
        kernel,
        out_shape=out_shape,
        in_specs=[
            IN_SMEM if value.ndim == 1 else IN_HBM if k in far else IN_VMEM
            for k, value in enumerate(operands)
        ],
        out_specs=jax.tree.map(
            lambda made: IN_SMEM if made.dtype == jnp.int32 else IN_VMEM, out_shape
        ),
        scratch_shapes=list(scratch),
        input_output_aliases=aliases or {},
        compiler_params=pltpu.CompilerParams(vmem_limit_bytes=VMEM_BYTES),
        cost_estimate=pl.CostEstimate(
            flops=flops, bytes_accessed=bytes_accessed, transcendentals=0
        ),
    )(*operands)


def first_blocks(stream, swapped, routes, route_gain, experts):
    chips, _, tok_here, feat_here = stream.shape
    width = 2 * feat_here
    tokens = chips * tok_here
    head = -(-3 * (experts + 1) // 16) * 16

    def kernel(stream_ref, swapped_ref, routes_ref, gain_ref, out_ref):
        core = lax.rem(lax.axis_index("ep"), 2)
        square = (tok_here, tok_here)
        diagonal = lax.broadcasted_iota(jnp.int32, square, 0) == lax.broadcasted_iota(
            jnp.int32, square, 1
        )

        def along(column):
            return jnp.sum(jnp.where(diagonal, column, 0.0), axis=0, keepdims=True)

        def split(left):
            for _ in range(3):
                piece = left.astype(jnp.bfloat16).astype(jnp.float32)
                left = left - piece
                yield piece

        row_at = lax.broadcasted_iota(jnp.int32, (head, tok_here), 0)
        for q in range(chips):
            mine = stream_ref[q, core]
            other = swapped_ref[q]
            left = jnp.where(core == 0, mine, other)
            right = jnp.where(core == 0, other, mine)
            at = head + q * tok_here
            out_ref[at : at + tok_here, :] = jnp.concatenate([left, right], axis=1)
            left, right = left.astype(jnp.float32), right.astype(jnp.float32)
            squares = jnp.sum(left * left + right * right, axis=1, keepdims=True)
            top = jnp.zeros((head, tok_here), jnp.float32)
            for row, piece in enumerate(split(along(squares))):
                top = jnp.where(row_at == row, piece, top)
            if q == 0:
                for expert in range(experts):
                    gains = jnp.where(routes_ref[...] == expert, gain_ref[...], 0.0)
                    gains = jnp.sum(gains, axis=1, keepdims=True)
                    for row, piece in enumerate(split(along(gains))):
                        top = jnp.where(row_at == 3 * (expert + 1) + row, piece, top)
            out_ref[:head, q * tok_here : (q + 1) * tok_here] = top.astype(jnp.bfloat16)
        if width > tokens:
            out_ref[:head, tokens:] = jnp.zeros((head, width - tokens), jnp.bfloat16)

    return local_call(
        kernel,
        jax.ShapeDtypeStruct((head + tokens, width), jnp.bfloat16),
        [stream, swapped, routes, route_gain],
        flops=4 * tokens * width,
        bytes_accessed=4 * tokens * width,
    )


def accumulate(
    where, positions, parts, norm_gain, tables, tok_here, carried, headers, ahead, leading
):
    count = len(positions)
    width = parts[0][0].shape[1]
    chips = norm_gain.shape[0]
    model_width = chips * width
    hidden_here = tables[0].shape[-1]
    both = 2 * hidden_here
    half = model_width // 2
    tokens = chips * tok_here
    sizes = [piece.shape[0] for piece in parts[0]]
    head = sum(sizes) - tokens
    offsets = [head] + [0] * (len(sizes) - 1)
    sizes = [size - at for size, at in zip(sizes, offsets)]
    starts = [sum(sizes[:k]) for k in range(len(sizes))]
    last = headers is not None
    first = carried is None
    slots = 0 if last else 4 * count

    def kernel(where_ref, *refs):
        refs = list(refs)
        xs = [[refs.pop(0) for _ in sizes] for _ in range(count)]
        scale_ref = refs.pop(0)
        stored = [refs.pop(0) for _ in tables]
        acc_in = None if first else refs.pop(0)
        tops = [refs.pop(0) for _ in headers] if last else []
        sources = [refs.pop(0) for _ in ahead[1]] if ahead else []
        product_ref = refs.pop(0) if leading else None
        owns = [refs.pop(0) for _ in range(count)]
        if last:
            hidden_ref = refs.pop(0)
            leads = [refs.pop(0) for _ in leading[1]]
        else:
            acc_out = refs.pop(0)
        if ahead:
            next_ref, down_ref = refs.pop(0), refs.pop(0)
        if last:
            column_ref = refs.pop(0)
        else:
            table_ref, sems = refs.pop(0), refs.pop(0)

        def fetch(which, position, target, sem):
            row = pl.multiple_of(where_ref[position] * width, width)
            copy = pltpu.make_async_copy(stored[which].at[pl.ds(row, width), :], target, sem)
            copy.start()
            return copy

        copies, later = {}, []
        if not last:
            for which in range(4):
                for b in range(count):
                    slot = which * count + b
                    copies[which, b] = fetch(
                        which, positions[b], table_ref.at[slot], sems.at[slot]
                    )
        if ahead:
            for which in range(4):
                later.append(fetch(which, ahead[0], next_ref.at[which], sems.at[slots + which]))
            for k, source in enumerate(sources):
                target = down_ref.at[k * hidden_here : (k + 1) * hidden_here, :]
                copy = pltpu.make_async_copy(source, target, sems.at[slots + 4 + k])
                copy.start()
                later.append(copy)
        begin = where_ref[0] * tok_here
        for b in range(count):
            for k, size in enumerate(sizes):

                @pl.when((begin >= starts[k]) & (begin < starts[k] + size))
                def _():
                    row = begin - starts[k] + offsets[k]
                    owns[b][...] = xs[b][k][pl.ds(pl.multiple_of(row, 16), tok_here), :]

        if last:
            expert = where_ref[chips]
            square = (tok_here, tok_here)
            row_at = lax.broadcasted_iota(jnp.int32, (head, tok_here), 0)
            diagonal = lax.broadcasted_iota(jnp.int32, square, 0) == lax.broadcasted_iota(
                jnp.int32, square, 1
            )

            def column(row, values):
                named = (row_at >= row) & (row_at < row + 3)
                along = jnp.sum(jnp.where(named, values, 0.0), axis=0, keepdims=True)
                return jnp.sum(jnp.where(diagonal, along, 0.0), axis=1, keepdims=True)

            for d in range(chips):
                values = tops[d][:head, :tok_here].astype(jnp.float32)
                at = pl.multiple_of(where_ref[d] * tok_here, tok_here)
                column_ref[pl.ds(at, tok_here), 0:1] = column(3 * (expert + 1), values)
            for q in range(chips):
                span = slice(q * tok_here, (q + 1) * tok_here)
                total = tops[0][:head, span].astype(jnp.float32)
                for d in range(1, chips):
                    total = total + tops[d][:head, span].astype(jnp.float32)
                mean = column(0, total) / model_width
                column_ref[span, 1:2] = lax.rsqrt(mean + epsilon)

        scaled = []
        for k, size in enumerate(sizes):
            for b in range(count):
                values = xs[b][k][offsets[k] : offsets[k] + size, :].astype(jnp.float32)
                scale = scale_ref[where_ref[positions[b]]]
                scaled.append((values * scale).astype(jnp.bfloat16))
        acts = {}
        spans = [slice(at, at + size) for at, size in zip(starts, sizes)]
        if last:
            scaled, spans = [jnp.concatenate(scaled, axis=0)], [slice(0, tokens)]
        for which in range(4):
            cols = slice(which * hidden_here, (which + 1) * hidden_here)
            for b in range(count):
                if not last:
                    copies[which, b].wait()
            for k, span in enumerate(spans):
                total = None if first else acc_in[span, cols]
                for b in range(count):
                    if last:
                        table = stored[0][which]
                    else:
                        table = table_ref[which * count + b]
                    product = jnp.dot(
                        scaled[k * count + b], table, preferred_element_type=jnp.float32
                    )
                    total = product if total is None else total + product
                if not last:
                    acc_out[span, cols] = total
                elif which % 2 == 0:
                    acts[k] = total
                else:
                    gain, inv_rms = column_ref[span, 0:1], column_ref[span, 1:2]
                    gate_act, up_act = acts[k] * inv_rms, total * inv_rms
                    act = gate_act * jax.nn.sigmoid(gate_act) * up_act * gain
                    core = which // 2
                    out_cols = slice(core * hidden_here, (core + 1) * hidden_here)
                    hidden_ref[span, out_cols] = act.astype(jnp.bfloat16)
        for copy in later:
            copy.wait()
        for part in range(2) if last else ():
            chosen = [k for k, (_, at) in enumerate(leading[1]) if at == part]
            rows = [where_ref[leading[1][k][0]] * tok_here for k in chosen]
            rows = [hidden_ref[pl.ds(pl.multiple_of(at, tok_here), tok_here), :] for at in rows]
            out = jnp.dot(
                jnp.concatenate(rows, axis=0),
                product_ref[:, part * half : (part + 1) * half],
                preferred_element_type=jnp.float32,
            ).astype(jnp.bfloat16)
            for at, k in enumerate(chosen):
                leads[k][...] = out[at * tok_here : (at + 1) * tok_here, :]

    operands = [where] + [piece for block in parts for piece in block]
    operands.append(norm_gain)
    distant = [] if last else list(range(len(operands), len(operands) + len(tables)))
    operands.extend(tables)
    aliases = {}
    if not first:
        if not last:
            aliases = {len(operands): count}
        operands.append(carried)
    out_shape = [jax.ShapeDtypeStruct((tok_here, width), jnp.bfloat16)] * count
    if last:
        operands.extend(headers)
        operands.append(leading[0])
        out_shape.append(jax.ShapeDtypeStruct((tokens, both), jnp.bfloat16))
        out_shape.extend(
            [jax.ShapeDtypeStruct((tok_here, half), jnp.bfloat16)] * len(leading[1])
        )
    else:
        out_shape.append(jax.ShapeDtypeStruct((tokens, 2 * both), jnp.float32))
    if ahead:
        for source in ahead[1]:
            distant.append(len(operands))
            operands.append(source)
        out_shape.append(jax.ShapeDtypeStruct((4, width, hidden_here), jnp.bfloat16))
        out_shape.append(jax.ShapeDtypeStruct((both, model_width), jnp.bfloat16))
    if last:
        scratch = [pltpu.VMEM((tokens, 2), jnp.float32)]
    else:
        scratch = [
            pltpu.VMEM((slots, width, hidden_here), jnp.bfloat16),
            pltpu.SemaphoreType.DMA((slots + 6,)),
        ]
    made = local_call(
        kernel,
        out_shape,
        operands,
        flops=COST_SCALE * 4 * count * tokens * width * both,
        bytes_accessed=count * width * (tokens + 2 * both) * 2 + tokens * both * 16,
        aliases=aliases,
        scratch=scratch,
        far=distant,
    )
    return made[:count], made[count:]


def contribution(where, hidden, down, part):
    tokens, units = hidden.shape
    half = down.shape[1] // 2
    tile = 512 if half % 512 == 0 else half

    def kernel(where_ref, hidden_ref, down_ref, out_ref):
        for start in range(0, half, tile):
            out = jnp.dot(
                hidden_ref[...],
                down_ref[:, part * half + start : part * half + start + tile],
                preferred_element_type=jnp.float32,
            )
            out_ref[:, start : start + tile] = out.astype(jnp.bfloat16)

    return local_call(
        kernel,
        jax.ShapeDtypeStruct((tokens, half), jnp.bfloat16),
        [where, hidden, down],
        flops=2 * tokens * units * half,
        bytes_accessed=2 * half * (units + tokens),
    )


def add_rows(where, position, table, moved):
    rows, width = moved.shape

    def kernel(where_ref, table_ref, moved_ref, out_ref):
        at = pl.multiple_of(where_ref[position] * rows, rows)
        total = table_ref[pl.ds(at, rows), :].astype(jnp.float32)
        out_ref[...] = (total + moved_ref[...].astype(jnp.float32)).astype(jnp.bfloat16)

    return local_call(
        kernel,
        jax.ShapeDtypeStruct((rows, width), jnp.bfloat16),
        [where, table, moved],
        flops=rows * width,
        bytes_accessed=rows * width * 6,
    )


def collect(where, positions, pieces):
    rows, width = pieces[0].shape
    model_width = len(pieces) * width

    def kernel(where_ref, *refs):
        for k, position in enumerate(positions):
            start = pl.multiple_of(where_ref[position] * width, width)
            refs[-1][:, pl.ds(start, width)] = refs[k][...]

    return local_call(
        kernel,
        jax.ShapeDtypeStruct((rows, model_width), jnp.bfloat16),
        [where, *pieces],
        flops=rows * model_width,
        bytes_accessed=rows * model_width * 4,
    )


def final_sum(where, stream, tables, arrived):
    rows, model_width = stream.shape
    half = model_width // 2
    came = [value for part in arrived for value in part]

    def kernel(where_ref, stream_ref, *refs):
        out_ref = refs[-1]
        at = pl.multiple_of(where_ref[0] * rows, rows)
        for part in range(2):
            cols = slice(part * half, (part + 1) * half)
            total = stream_ref[:, cols].astype(jnp.float32)
            total = total + refs[part][pl.ds(at, rows), :].astype(jnp.float32)
            for k in range(len(arrived[part])):
                total = total + refs[2 + k + part * len(arrived[0])][...].astype(jnp.float32)
            out_ref[:, cols] = total.astype(jnp.bfloat16)

    return local_call(
        kernel,
        jax.ShapeDtypeStruct((rows, model_width), jnp.bfloat16),
        [where, stream, *tables, *came],
        flops=rows * model_width * 3,
        bytes_accessed=rows * model_width * 10,
    )


def dense_body(residual, attn_out, norm_gain, expert_routes, route_gain, w_gate, w_up, w_down):
    devices = lax.axis_size("ep")
    experts = devices // FSPLIT
    chips = devices // 2
    far = chips // 2
    tok_here = expert_routes.shape[0]
    feat_here = residual.shape[1]
    model_width = w_gate.shape[0]
    width = 2 * feat_here
    ring = ring_order(chips)
    me = lax.axis_index("ep")
    core = me % 2
    seen = [
        [ring[(ring.index(i // 2) + d) % chips] for d in range(chips)] + [i // FSPLIT]
        for i in range(devices)
    ]
    where = lax.dynamic_index_in_dim(jnp.asarray(seen, jnp.int32), me, 0, keepdims=False)

    stream_feat = (residual.astype(jnp.float32) + attn_out.astype(jnp.float32)).astype(jnp.bfloat16)
    by_core = stream_feat.reshape(chips, 2, tok_here, feat_here)
    swapped = swap_cores(lax.dynamic_index_in_dim(by_core, 1 - core, 1, keepdims=False))

    swapped, w_gate, w_up = lax.optimization_barrier((swapped, w_gate, w_up))
    tables = [pltpu.with_memory_space_constraint(table, pltpu.HBM) for table in (w_gate, w_up)]
    tables += [swap_cores(w_gate), swap_cores(w_up)]
    blocks = {0: first_blocks(by_core, swapped, expert_routes, route_gain, experts)}
    w_down = lax.optimization_barrier((swapped, w_down))[1]
    down = [pltpu.with_memory_space_constraint(w_down, pltpu.HBM), swap_cores(w_down)]

    for distance in range(1, far):
        for sign in (-1, 1):
            blocks[sign * distance] = ring_shift(blocks[sign * (distance - 1)], ring, -sign)
    groups = [[0]] + [[d, chips - d] for d in range(1, far)] + [[far]]
    gain_rows = norm_gain.reshape(chips, 1, width)
    carried, owns, positions, headers, ahead, leading = None, [], [], None, None, None
    for group in groups:
        parts = [[blocks[d if d <= far else d - chips]] for d in group]
        if group == [far]:
            parts = [blocks[far]]
            headers = [blocks[d if d < far else d - chips] for d in range(chips) if d != far]
            headers.insert(far, blocks[far][0])
            leading = (down, [(far, 0), (far, 1), (far - 1, 1), (chips - far + 1, 0)])
        if group == groups[-2]:
            ahead = (far, down)
        made, (carried, *rest) = accumulate(
            where, group, parts, gain_rows, tables, tok_here, carried, headers, ahead, leading
        )
        owns.extend(made)
        positions.extend(group)
        if group == groups[max(far - 2, 0)]:
            lower, upper, carried = lax.optimization_barrier(
                (blocks[1 - far], blocks[far - 1], carried)
            )
            cut = lower.shape[0] - far * tok_here
            blocks[far] = [ring_shift(lower[:cut], ring, 1), ring_shift(upper[cut:], ring, -1)]
        if group == groups[-2]:
            tables, down, ahead = [rest[0]], rest[1], None

    hidden, (lower, upper, after, before) = carried, rest
    moving = {1: [ring_shift(lower, ring, 1), None], -1: [None, ring_shift(upper, ring, -1)]}
    second = {1: ring_shift(after, ring, 1), -1: ring_shift(before, ring, -1)}
    stream_rows = collect(where, positions, owns)
    stream_rows, hidden = lax.optimization_barrier((stream_rows, hidden))
    everything = [contribution(where, hidden, down, part) for part in range(2)]
    for distance in range(far - 1, 0, -1):
        for sign, order in ((1, (1, 0)), (-1, (0, 1))):
            position = (sign * distance) % chips
            sent = [None, None]
            for part in order:
                if moving[sign][part] is None:
                    sent[part] = second[sign]
                else:
                    value = add_rows(where, position, everything[part], moving[sign][part])
                    sent[part] = ring_shift(value, ring, sign)
            moving[sign] = sent
    arrived = [
        [moving[sign][part] for sign in (1, -1) if moving[sign][part] is not None]
        for part in range(2)
    ]
    return final_sum(where, stream_rows, everything, arrived)


def body(residual, attn_out, norm_gain, expert_routes, route_gain, w_gate, w_up, w_down):
    tok_here, route_slots = expert_routes.shape
    devices = lax.axis_size("ep")
    capacity = route_slots * tok_here // (devices // FSPLIT)
    dense = capacity >= tok_here and devices % 8 == 0
    dense = dense and devices * tok_here <= 4 * residual.shape[1]
    chosen = dense_body if dense else routed_body
    return chosen(residual, attn_out, norm_gain, expert_routes, route_gain, w_gate, w_up, w_down)


def solution(mesh):
    in_specs = (
        P("groups", "ep"),
        P("groups", "ep"),
        P(),
        P(("groups", "ep"), None),
        P(("groups", "ep"), None),
        P(None, "ep"),
        P(None, "ep"),
        P("ep", None),
    )
    out_specs = P(("groups", "ep"), None)
    return jax.shard_map(body, mesh=mesh, in_specs=in_specs, out_specs=out_specs, check_vma=False)
```
